32 devices in a mesh: dp: 8 (over z, y), tensor: 4 (over x, core).
Axes of the slice: x: 2, y: 2, z: 4, core: 2. Of those that a mesh axis runs over, the one named last changes fastest.
Arguments:
- inputs: bfloat16 [8192, 2048], P(('dp', 'tensor')), may hold values from -6 to 6
- segments: int32 [8, 1024], P('dp', 'tensor'), may hold values from 0 to 2, as said below
- cotangent: bfloat16 [8192, 2048], P(('dp', 'tensor')), may hold values from -6 to 6
- qkv_weight: float32 [3, 2048, 2048], P(None, 'dp', 'tensor'), may hold values from -0.125 to 0.125
- qkv_first: float32 [3, 2048, 2048], P(None, 'dp', 'tensor')
- qkv_second: float32 [3, 2048, 2048], P(None, 'dp', 'tensor'), may hold values from 434.176 to 1720.32
- dense_weight: float32 [2048, 2048], P('tensor', 'dp'), may hold values from -0.75 to 0.75
- dense_first: float32 [2048, 2048], P('tensor', 'dp')
- dense_second: float32 [2048, 2048], P('tensor', 'dp'), may hold values from 13.1072 to 52.4288
- expand_weight: float32 [2048, 8192], P('dp', 'tensor'), may hold values from -0.125 to 0.125
- expand_first: float32 [2048, 8192], P('dp', 'tensor')
- expand_second: float32 [2048, 8192], P('dp', 'tensor'), may hold values from 155.648 to 622.592
- shrink_weight: float32 [8192, 2048], P('tensor', 'dp'), may hold values from -0.0625 to 0.0625
- shrink_first: float32 [8192, 2048], P('tensor', 'dp')
- shrink_second: float32 [8192, 2048], P('tensor', 'dp'), may hold values from 172.032 to 688.128
- small_params: float32 [11, 2048], P(None, 'dp')
- small_first: float32 [11, 2048], P(None, 'dp')
- small_second: float32 [11, 2048], P(None, 'dp'), may hold values from 868.352 to 3440.64
Outputs:
- output: bfloat16 [8192, 2048], P(('dp', 'tensor'))
- input_grad: float32 [8192, 2048], P(('dp', 'tensor'))
- qkv_new: float32 [3, 2048, 2048], P(None, 'dp', 'tensor')
- qkv_first_new: float32 [3, 2048, 2048], P(None, 'dp', 'tensor')
- qkv_second_new: float32 [3, 2048, 2048], P(None, 'dp', 'tensor')
- dense_new: float32 [2048, 2048], P('tensor', 'dp')
- dense_first_new: float32 [2048, 2048], P('tensor', 'dp')
- dense_second_new: float32 [2048, 2048], P('tensor', 'dp')
- expand_new: float32 [2048, 8192], P('dp', 'tensor')
- expand_first_new: float32 [2048, 8192], P('dp', 'tensor')
- expand_second_new: float32 [2048, 8192], P('dp', 'tensor')
- shrink_new: float32 [8192, 2048], P('tensor', 'dp')
- shrink_first_new: float32 [8192, 2048], P('tensor', 'dp')
- shrink_second_new: float32 [8192, 2048], P('tensor', 'dp')
- small_new: float32 [11, 2048], P(None, 'dp')
- small_first_new: float32 [11, 2048], P(None, 'dp')
- small_second_new: float32 [11, 2048], P(None, 'dp')
The draws below stay inside these ranges and needn't reach their ends.
Inputs may be any that keep to these rules, and one draw needn't show every extreme that they name: `segments`: each row holds three documents numbered 0, 1, 2 in order, each of 64 tokens or more; document 1 holds token 170 and token 768 of the row.
All inputs are finite; a program needn't handle non-finite values.
Results may differ from the reference program's by a relative error of at most 0.012.
The reference program's roundings to bfloat16 on the way count: a program that leaves them out, or rounds other values in their place, can miss the bound.
Values may be sent and summed in bfloat16 or wider, within the bound.
A program may use at most 192 MiB of HBM per device.

```python
import math
import jax
import jax.numpy as jnp
from jax import lax

D = 2048
HEADS = 32
HD = 64
ROT = 32
FF = 8192
TOK_DEV = 256
STEP = 10
SEQ = 1024
SEQS = 8
TOKENS = 8192
VROWS = 11


def signed_moment(key, shape, size):
    return size * jax.random.truncated_normal(key, -4.0, 4.0, shape, jnp.float32)


def draw_segments(key, part):
    key = jax.random.fold_in(key, 11)
    lead_key, span_key = jax.random.split(key)
    lead = jax.random.randint(lead_key, (SEQS,), SEQ // 16, SEQ // 6 + 1)
    span = jax.random.randint(span_key, (SEQS,), SEQ - TOK_DEV + 1 - lead, SEQ - lead - SEQ // 16 + 1)
    places = jnp.arange(SEQ, dtype=jnp.int32)[None, :]
    first_cut = (places >= lead[:, None]).astype(jnp.int32)
    second_cut = (places >= (lead + span)[:, None]).astype(jnp.int32)
    return first_cut + second_cut


def draw_small_params(key, part):
    key = jax.random.fold_in(key, 5)
    base = 0.3 * jax.random.truncated_normal(key, -3.0, 3.0, (VROWS, D), jnp.float32)
    row_index = jnp.arange(VROWS, dtype=jnp.int32)[:, None]
    return jnp.where(row_index == 0, 1.0 + base, base)


def draw_qkv_first(key, part):
    key = jax.random.fold_in(key, 21)
    return signed_moment(key, (3, D, D), 0.11 * math.sqrt(TOKENS))


def draw_dense_first(key, part):
    key = jax.random.fold_in(key, 22)
    return signed_moment(key, (D, D), 0.019 * math.sqrt(TOKENS))


def draw_expand_first(key, part):
    key = jax.random.fold_in(key, 23)
    return signed_moment(key, (D, FF), 0.066 * math.sqrt(TOKENS))


def draw_shrink_first(key, part):
    key = jax.random.fold_in(key, 24)
    return signed_moment(key, (FF, D), 0.07 * math.sqrt(TOKENS))


def draw_small_first(key, part):
    key = jax.random.fold_in(key, 25)
    return signed_moment(key, (VROWS, D), 0.156 * math.sqrt(TOKENS))


def level_of(rng, dims, cuts, smallest, largest):
    def one(position, shards_of):
        draws = jax.random.uniform(jax.random.fold_in(jax.random.fold_in(rng, 6), position), (shards_of,), jnp.float32, smallest / len(cuts), largest / len(cuts))
        return jnp.repeat(jnp.exp(draws), dims[position] // shards_of).reshape((-1,) + (1,) * (len(dims) - position - 1))

    factor_of = one(*cuts[0])
    for cut in cuts[1:]:
        factor_of = factor_of * one(*cut)
    return factor_of


def scatter_about(key, extent, spread, bound, shards=(), held_as=jnp.bfloat16):
    result = jax.random.normal(key, extent, jnp.float32) * spread
    if len(shards) > 0:
        result = level_of(key, extent, shards, -0.22, 0.18) * result
    return jnp.clip(result, min=-bound, max=bound).astype(held_as)


def setup_inputs(seed: int = 0) -> dict:
    arg_keys = jax.random.split(jax.random.key(seed), 19)
    inputs = scatter_about(arg_keys[0], (TOKENS, D), 1.0, 6.0, ((0, 32),))
    segments = draw_segments(jax.random.fold_in(arg_keys[18], 71), 0)
    cotangent = scatter_about(arg_keys[2], (TOKENS, D), 1.0, 6.0, ((0, 32),))
    qkv_weight = scatter_about(arg_keys[3], (3, D, D), D ** -0.5, 0.125, ((1, 8), (2, 4)), jnp.float32)
    qkv_first = draw_qkv_first(jax.random.fold_in(arg_keys[18], 71), 0)
    qkv_second = jnp.clip(jnp.exp(math.log(1720.32) - 1.3768156 * jax.random.uniform(arg_keys[5], (3, D, D), jnp.float32) ** level_of(arg_keys[5], (3, D, D), ((1, 8), (2, 4)), -0.2, 0.2)), 434.176, 1720.32)
    dense_weight = scatter_about(arg_keys[6], (D, D), (D // 32) ** -0.5, 0.75, ((0, 4), (1, 8)), jnp.float32)
    dense_first = draw_dense_first(jax.random.fold_in(arg_keys[18], 71), 0)
    dense_second = jnp.clip(jnp.exp(math.log(52.4288) - 1.3862944 * jax.random.uniform(arg_keys[8], (D, D), jnp.float32) ** level_of(arg_keys[8], (D, D), ((0, 4), (1, 8)), -0.2, 0.2)), 13.1072, 52.4288)
    expand_weight = scatter_about(arg_keys[9], (D, FF), D ** -0.5, 0.125, ((0, 8), (1, 4)), jnp.float32)
    expand_first = draw_expand_first(jax.random.fold_in(arg_keys[18], 71), 0)
    expand_second = jnp.clip(jnp.exp(math.log(622.592) - 1.3862944 * jax.random.uniform(arg_keys[11], (D, FF), jnp.float32) ** level_of(arg_keys[11], (D, FF), ((0, 8), (1, 4)), -0.2, 0.2)), 155.648, 622.592)
    shrink_weight = scatter_about(arg_keys[12], (FF, D), FF ** -0.5, 0.0625, ((0, 4), (1, 8)), jnp.float32)
    shrink_first = draw_shrink_first(jax.random.fold_in(arg_keys[18], 71), 0)
    shrink_second = jnp.clip(jnp.exp(math.log(688.128) - 1.3862944 * jax.random.uniform(arg_keys[14], (FF, D), jnp.float32) ** level_of(arg_keys[14], (FF, D), ((0, 4), (1, 8)), -0.2, 0.2)), 172.032, 688.128)
    small_params = draw_small_params(jax.random.fold_in(arg_keys[18], 71), 0)
    small_first = draw_small_first(jax.random.fold_in(arg_keys[18], 71), 0)
    small_second = jnp.clip(jnp.exp(math.log(3440.64) - 1.3768156 * jax.random.uniform(arg_keys[17], (VROWS, D), jnp.float32) ** level_of(arg_keys[17], (VROWS, D), ((1, 8),), -0.2, 0.2)), 868.352, 3440.64)
    return {"inputs": inputs, "segments": segments, "cotangent": cotangent, "qkv_weight": qkv_weight, "qkv_first": qkv_first, "qkv_second": qkv_second, "dense_weight": dense_weight, "dense_first": dense_first, "dense_second": dense_second, "expand_weight": expand_weight, "expand_first": expand_first, "expand_second": expand_second, "shrink_weight": shrink_weight, "shrink_first": shrink_first, "shrink_second": shrink_second, "small_params": small_params, "small_first": small_first, "small_second": small_second}


@jax.custom_vjp
def low(v):
    return lax.optimization_barrier(v.astype(jnp.bfloat16)).astype(jnp.float32)

@jax.custom_vjp
def low_back(v):
    return v

def low_keep(v):
    return (low(v), None)

def low_pass(kept, grad):
    return (grad,)

def back_keep(v):
    return (v, None)

def back_low(kept, grad):
    return (low(grad),)
low.defvjp(low_keep, low_pass)
low_back.defvjp(back_keep, back_low)
HIGHEST = lax.Precision.HIGHEST
norm_eps = 1e-05
beta_first = 0.9
beta_second = 0.95
adam_eps = 1e-08
weight_decay = 0.1
matrix_rate = 0.05
vector_rate = 1.0
masked_score = -1e+30

def doc_positions(doc_ids):
    places = jnp.arange(doc_ids.shape[0], dtype=jnp.int32)
    before = jnp.concatenate([doc_ids[:1] - 1, doc_ids[:-1]])
    starts = jnp.where(doc_ids != before, places, jnp.zeros_like(places))
    first = lax.cummax(starts, axis=0)
    return (places - first).astype(jnp.float32)

def doc_angles(doc_ids):
    half = ROT // 2
    freqs = 10000.0 ** (-jnp.arange(half, dtype=jnp.float32) / half)
    return doc_positions(doc_ids)[:, None] * freqs[None, :]

def rotate(values, angle):
    half = ROT // 2
    cosine = jnp.cos(angle)[:, None, :]
    sine = jnp.sin(angle)[:, None, :]
    first = values[..., :half]
    second = values[..., half:ROT]
    return jnp.concatenate([first * cosine - second * sine, second * cosine + first * sine, values[..., ROT:]], axis=-1)

def attend(queries, keys, values, doc_ids):
    length = queries.shape[0]
    block_rows = min(512, length)
    block_count = length // block_rows
    scale = HD ** (-0.5)
    key_places = jnp.arange(length, dtype=jnp.int32)

    def one_block(block_args):
        query_block, query_docs, start = block_args
        scores = jnp.einsum('qhd,khd->hqk', query_block, keys, precision=HIGHEST) * scale
        scores = low_back(scores)
        query_places = start + jnp.arange(block_rows, dtype=jnp.int32)
        allowed = (query_docs[:, None] == doc_ids[None, :]) & (key_places[None, :] <= query_places[:, None])
        scores = jnp.where(allowed[None], scores, masked_score)
        peak = lax.optimization_barrier(jnp.max(scores, axis=-1, keepdims=True))
        expo = jnp.exp(scores - peak)
        weights = low(expo / lax.optimization_barrier(jnp.sum(expo, axis=-1, keepdims=True)))
        return jnp.einsum('hqk,khd->qhd', weights, values, precision=HIGHEST)
    starts = (jnp.arange(block_count, dtype=jnp.int32) * block_rows).astype(jnp.int32)
    blocks = lax.map(jax.checkpoint(one_block), (queries.reshape(block_count, block_rows, HEADS, HD), doc_ids.reshape(block_count, block_rows), starts))
    return blocks.reshape(length, HEADS, HD)

def block_forward(rows, doc_ids, qkv_w, dense_w, expand_w, shrink_w, params):
    length = rows.shape[0]
    mean = lax.optimization_barrier(jnp.mean(rows, axis=-1, keepdims=True))
    centered = rows - mean
    variance = lax.optimization_barrier(jnp.mean(centered * centered, axis=-1, keepdims=True))
    normed = low(centered * lax.rsqrt(variance + norm_eps) * params[0] + params[1])
    projected = jnp.einsum('sd,jde->jse', normed, qkv_w, precision=HIGHEST) + params[2:5][:, None, :]
    projected = low_back(projected)
    angle = doc_angles(doc_ids)
    queries = low(rotate(projected[0].reshape(length, HEADS, HD), angle))
    keys = low(rotate(projected[1].reshape(length, HEADS, HD), angle))
    values = low(projected[2].reshape(length, HEADS, HD))
    attended = low(low_back(attend(queries, keys, values, doc_ids).reshape(length, D)))
    hidden_pre = low_back(jnp.dot(normed, expand_w, precision=HIGHEST) + params[7:].reshape(FF))
    hidden_act = low(jax.nn.gelu(hidden_pre, approximate=True))
    branch = jnp.dot(attended, dense_w, precision=HIGHEST) + jnp.dot(hidden_act, shrink_w, precision=HIGHEST)
    return rows + branch + params[5] + params[6]

def adam_update(weight, first, second, grad, rate, decay):
    first_new = beta_first * first + (1.0 - beta_first) * grad
    second_new = beta_second * second + (1.0 - beta_second) * grad * grad
    first_hat = first_new / (1.0 - beta_first ** STEP)
    second_hat = second_new / (1.0 - beta_second ** STEP)
    weight_new = weight - rate * (first_hat / (jnp.sqrt(second_hat) + adam_eps) + decay * weight)
    return (weight_new, first_new, second_new)

def reference(inputs, segments, cotangent, qkv_weight, qkv_first, qkv_second, dense_weight, dense_first, dense_second, expand_weight, expand_first, expand_second, shrink_weight, shrink_first, shrink_second, small_params, small_first, small_second):
    sequences = segments.shape[0]

    def forward(rows_all, qkv_w, dense_w, expand_w, shrink_w, params):
        qkv_w = low(qkv_w)
        dense_w = low(dense_w)
        expand_w = low(expand_w)
        shrink_w = low(shrink_w)
        params = low(params)

        def one_sequence(seq_args):
            return block_forward(seq_args[0], seq_args[1], qkv_w, dense_w, expand_w, shrink_w, params)
        outputs = lax.map(jax.checkpoint(one_sequence), (rows_all.reshape(sequences, SEQ, D), segments))
        return outputs.reshape(sequences * SEQ, D)
    output, pull = jax.vjp(forward, inputs.astype(jnp.float32), qkv_weight, dense_weight, expand_weight, shrink_weight, small_params)
    input_grad, qkv_grad, dense_grad, expand_grad, shrink_grad, small_grad = pull(cotangent.astype(jnp.float32))
    qkv_new = adam_update(qkv_weight, qkv_first, qkv_second, qkv_grad, matrix_rate, weight_decay)
    dense_new = adam_update(dense_weight, dense_first, dense_second, dense_grad, matrix_rate, weight_decay)
    expand_new = adam_update(expand_weight, expand_first, expand_second, expand_grad, matrix_rate, weight_decay)
    shrink_new = adam_update(shrink_weight, shrink_first, shrink_second, shrink_grad, matrix_rate, weight_decay)
    small_new = adam_update(small_params, small_first, small_second, small_grad, vector_rate, 0.0)
    return (output.astype(jnp.bfloat16), input_grad, qkv_new[0], qkv_new[1], qkv_new[2], dense_new[0], dense_new[1], dense_new[2], expand_new[0], expand_new[1], expand_new[2], shrink_new[0], shrink_new[1], shrink_new[2], small_new[0], small_new[1], small_new[2])
```

```python
import functools
import jax
import jax.numpy as jnp
from jax import lax
from jax.experimental import pallas as pl
from jax.experimental.pallas import tpu as pltpu
from jax.sharding import PartitionSpec as P

D = 2048
HD = 64
ROT = 32
FF = 8192
STEP = 10

norm_eps = 1e-05
beta_first = 0.9
beta_second = 0.95
adam_eps = 1e-08
weight_decay = 0.1
matrix_rate = 0.05
vector_rate = 1.0
masked_score = -1e30

SUB_BIT = 1
ROW_BIT = 0

bf16 = jnp.bfloat16
f32 = jnp.float32


def exchange(values, axis, bit):
    count = lax.axis_size(axis)
    return lax.ppermute(values, axis, [(i, i ^ (1 << bit)) for i in range(count)])


def place_order(count):
    bits = count.bit_length() - 1
    order = []
    for p in range(count):
        high = (p >> 1) & ((1 << (bits - 2)) - 1)
        order.append(((p & 1) << SUB_BIT) | (high << 2) | ((p >> (bits - 1)) << ROW_BIT))
    return order


def adam_update(weight, first, second, grad, rate, decay):
    first_new = beta_first * first + (1.0 - beta_first) * grad
    second_new = beta_second * second + (1.0 - beta_second) * grad * grad
    first_hat = first_new / (1.0 - beta_first**STEP)
    second_hat = second_new / (1.0 - beta_second**STEP)
    weight_new = weight - rate * (first_hat / (jnp.sqrt(second_hat) + adam_eps) + decay * weight)
    return (weight_new, first_new, second_new)


def gelu_value(pre_values):
    return jax.nn.gelu(pre_values, approximate=True)


def vmem_params(mib):
    return pltpu.CompilerParams(vmem_limit_bytes=mib * 2**20)


def place_of(block, count):
    bits = count.bit_length() - 1
    return ((block >> SUB_BIT) & 1) | ((block >> 2) << 1) | (((block >> ROW_BIT) & 1) << (bits - 1))


def move_blocks(count, source, load, store):
    width = D // count
    if width % 128 == 0:
        for j in range(count):
            start = pl.multiple_of(source(j) * width, width)
            store(pl.ds(j * width, width), load(pl.ds(start, width)))
        return
    for unit in range(count // 2):
        parts = []
        for half in range(2):
            block = source(2 * unit + half)
            value = load(pl.ds(pl.multiple_of((block >> 1) * 128, 128), 128))
            parts.append(pltpu.roll(value, ((block & 1) ^ half) * 64, 1))
        lane = lax.broadcasted_iota(jnp.int32, parts[0].shape, 1)
        store(pl.ds(unit * 128, 128), jnp.where(lane < 64, parts[0], parts[1]))


def norm_kernel(order, me_ref, x_ref, dy_ref, g_ref, b_ref, n_ref, ns_ref, dyr_ref, dys_ref, dysum_ref, tmp):
    me = me_ref[0]
    count = len(order)
    rows = x_ref[...].astype(f32)
    mean = jnp.mean(rows, axis=-1, keepdims=True)
    centered = rows - mean
    inv = lax.rsqrt(jnp.mean(centered * centered, axis=-1, keepdims=True) + norm_eps)
    tmp[...] = centered * inv * g_ref[...] + b_ref[...]
    dysum_ref[...] = jnp.sum(dy_ref[...].astype(f32), axis=0, keepdims=True)

    def store_to(ref):
        def store(lanes, value):
            ref[:, lanes] = value.astype(bf16)

        return store

    for flip, n_out, dy_out in ((0, n_ref, dyr_ref), (1, ns_ref, dys_ref)):
        source = lambda j: me ^ order[j ^ flip]
        move_blocks(count, source, lambda lanes: tmp[:, lanes], store_to(n_out))
        move_blocks(count, source, lambda lanes: dy_ref[:, lanes].astype(f32), store_to(dy_out))


def smem_spec():
    return pl.BlockSpec(memory_space=pltpu.SMEM)


def norm_call(order, me, x, dy, gain, shift):
    shape = jax.ShapeDtypeStruct(x.shape, bf16)
    vm = pl.BlockSpec(memory_space=pltpu.VMEM)
    return pl.pallas_call(
        functools.partial(norm_kernel, order),
        out_shape=[shape, shape, shape, shape, jax.ShapeDtypeStruct((1, D), f32)],
        in_specs=[smem_spec(), vm, vm, vm, vm],
        out_specs=[vm] * 5,
        scratch_shapes=[pltpu.VMEM(x.shape, f32)],
        compiler_params=vmem_params(32),
        name="norm",
    )(me, x, dy, gain, shift)


def assemble(order, me, keep_ref, recv_ref, tmp):
    count = len(order)

    def store(lanes, value):
        tmp[:, lanes] = value

    def add(lanes, value):
        tmp[:, lanes] += value

    move_blocks(count, lambda j: place_of(j ^ me, count), lambda lanes: keep_ref[:, lanes].astype(f32), store)
    move_blocks(count, lambda j: place_of(j ^ me, count) ^ 1, lambda lanes: recv_ref[:, lanes].astype(f32), add)


def out_kernel(order, me_ref, x_ref, keep_ref, recv_ref, b_ref, o_ref, tmp):
    assemble(order, me_ref[0], keep_ref, recv_ref, tmp)
    o_ref[...] = (x_ref[...].astype(f32) + tmp[...] + b_ref[0:1] + b_ref[1:2]).astype(bf16)


def out_call(order, me, x, keep, recv, biases):
    vm = pl.BlockSpec(memory_space=pltpu.VMEM)
    return pl.pallas_call(
        functools.partial(out_kernel, order),
        out_shape=jax.ShapeDtypeStruct(x.shape, bf16),
        in_specs=[smem_spec(), vm, vm, vm, vm],
        out_specs=vm,
        scratch_shapes=[pltpu.VMEM(x.shape, f32)],
        compiler_params=vmem_params(32),
        name="block_output",
    )(me, x, keep, recv, biases)


def norm_back_kernel(order, me_ref, x_ref, dy_ref, keep_ref, recv_ref, g_ref, o_ref, sums_ref, tmp):
    assemble(order, me_ref[0], keep_ref, recv_ref, tmp)
    rows = x_ref[...].astype(f32)
    centered = rows - jnp.mean(rows, axis=-1, keepdims=True)
    inv = lax.rsqrt(jnp.mean(centered * centered, axis=-1, keepdims=True) + norm_eps)
    unit = centered * inv
    back = tmp[...]
    sums_ref[0:1] = jnp.sum(back * unit, axis=0, keepdims=True)
    sums_ref[1:2] = jnp.sum(back, axis=0, keepdims=True)
    e = back * g_ref[...]
    o_ref[...] = dy_ref[...].astype(f32) + inv * (
        e - jnp.mean(e, axis=-1, keepdims=True) - unit * jnp.mean(e * unit, axis=-1, keepdims=True)
    )


def norm_back_call(order, me, x, dy, keep, recv, gain):
    vm = pl.BlockSpec(memory_space=pltpu.VMEM)
    return pl.pallas_call(
        functools.partial(norm_back_kernel, order),
        out_shape=[jax.ShapeDtypeStruct(x.shape, f32), jax.ShapeDtypeStruct((2, D), f32)],
        in_specs=[smem_spec()] + [vm] * 5,
        out_specs=[vm, vm],
        scratch_shapes=[pltpu.VMEM(x.shape, f32)],
        compiler_params=vmem_params(40),
        name="norm_back",
    )(me, x, dy, keep, recv, gain)


def swap_rotary(values):
    lane = lax.broadcasted_iota(jnp.int32, values.shape, 1)
    half = ROT // 2
    return jnp.where(
        lane % ROT < half, pltpu.roll(values, 128 - half, 1), pltpu.roll(values, half, 1)
    )


def rel_block(me_t, block, bits):
    rel = me_t ^ block
    return tuple((rel >> b) & 1 for b in range(bits))


def dot_nn(a, b):
    return lax.dot_general(a, b, (((1,), (0,)), ((), ())), preferred_element_type=f32)


def dot_nt(a, b):
    return lax.dot_general(a, b, (((1,), (1,)), ((), ())), preferred_element_type=f32)


def mask_bias(bias, dcol_ref, drow_ref, qb, rows):
    kend = (qb + 1) * rows
    shape = (kend, rows)
    key = lax.broadcasted_iota(jnp.int32, shape, 0)
    query = lax.broadcasted_iota(jnp.int32, shape, 1) + qb * rows
    same = dcol_ref[0, :kend, :] == drow_ref[0, 0:1, qb * rows : kend]
    bias[:kend, :] = jnp.where(same & (key <= query), 0.0, masked_score)


def attend_kernel(
    tbits, width, me_ref, proj_ref, cos_ref, sin_ref, dcol_ref, drow_ref, o_ref, qkv_ref, lse_ref, bias
):
    me_t = me_ref[1]
    rows = proj_ref.shape[-2]
    blocks = 1 << tbits
    scale = HD ** (-0.5)
    pairs = width // 128
    for b in range(blocks):
        rel = rel_block(me_t, b, tbits)
        place = slice(b * rows, (b + 1) * rows)
        cosine = cos_ref[0, place, :]
        sine = sin_ref[0, place, :]
        for j in range(2 * pairs):
            lanes = slice(j * 128, (j + 1) * 128)
            part = proj_ref[rel + (0, slice(None), lanes)]
            qkv_ref[0, place, lanes] = (part * cosine + swap_rotary(part) * sine).astype(bf16)
        qkv_ref[0, place, 2 * width :] = proj_ref[rel + (0, slice(None), slice(2 * width, None))].astype(bf16)
    lane = lax.broadcasted_iota(jnp.int32, (rows, 128), 1)
    zero = jnp.zeros((rows, 128), bf16)
    for qb in range(blocks):
        kend = (qb + 1) * rows
        place = slice(qb * rows, kend)
        rel = rel_block(me_t, qb, tbits)
        mask_bias(bias, dcol_ref, drow_ref, qb, rows)

        def pair_body(pair, carry):
            base = pl.multiple_of(pair * 128, 128)
            q = qkv_ref[0, place, pl.ds(base, 128)] * jnp.asarray(scale, bf16)
            k = qkv_ref[0, :kend, pl.ds(base + width, 128)]
            v = qkv_ref[0, :kend, pl.ds(base + 2 * width, 128)]
            vt = v.T
            outs = []
            for h in range(2):
                mine = (lane < HD) if h == 0 else (lane >= HD)
                s = dot_nt(k, jnp.where(mine, q, zero)) + bias[:kend, :]
                peak = jnp.max(s, axis=0, keepdims=True)
                expo = jnp.exp(s - peak)
                total = jnp.sum(expo, axis=0, keepdims=True)
                weights = (expo * (1.0 / total)).astype(bf16)
                outs.append(dot_nn(vt[h * HD : (h + 1) * HD, :], weights))
                lse_ref[0, pl.ds(pair * 2 + h, 1), place] = peak + jnp.log(total)
            both = jnp.concatenate(outs, axis=0)
            o_ref[rel + (0, slice(None), pl.ds(base, 128))] = both.T.astype(bf16)
            return carry

        lax.fori_loop(0, pairs, pair_body, 0)


def attend_call(me, proj, cosine, sine, doc_col, doc_row):
    tbits = proj.ndim - 3
    seqs = proj.shape[tbits]
    rows = proj.shape[-2]
    width = proj.shape[-1] // 3
    length = rows << tbits
    lead = (2,) * tbits
    seq3 = lambda s: (s, 0, 0)
    rel_map = lambda s: (0,) * tbits + (s, 0, 0)
    heads = width // HD
    return pl.pallas_call(
        functools.partial(attend_kernel, tbits, width),
        grid=(seqs,),
        out_shape=[
            jax.ShapeDtypeStruct(lead + (seqs, rows, width), bf16),
            jax.ShapeDtypeStruct((seqs, length, 3 * width), bf16),
            jax.ShapeDtypeStruct((seqs, heads, length), f32),
        ],
        in_specs=[
            smem_spec(),
            pl.BlockSpec(lead + (1, rows, 3 * width), rel_map),
            pl.BlockSpec((1, length, 128), seq3),
            pl.BlockSpec((1, length, 128), seq3),
            pl.BlockSpec((1, length, 1), seq3),
            pl.BlockSpec((1, 1, length), seq3),
        ],
        out_specs=[
            pl.BlockSpec(lead + (1, rows, width), rel_map),
            pl.BlockSpec((1, length, 3 * width), seq3),
            pl.BlockSpec((1, heads, length), seq3),
        ],
        scratch_shapes=[pltpu.VMEM((length, rows), f32)],
        compiler_params=vmem_params(50),
        name="attend",
    )(me, proj, cosine, sine, doc_col, doc_row)


def attend_back_kernel(
    tbits, width, me_ref, qkv_ref, do_ref, lse_ref, cos_ref, sin_ref, dcol_ref, drow_ref, o_ref, sum_ref, bias, dk, dv
):
    me_t = me_ref[1]
    rows = do_ref.shape[-2]
    blocks = 1 << tbits
    scale = HD ** (-0.5)
    pairs = width // 128
    lane = lax.broadcasted_iota(jnp.int32, (rows, 128), 1)
    zero = jnp.zeros((rows, 128), bf16)
    dk[...] = jnp.zeros_like(dk)
    dv[...] = jnp.zeros_like(dv)
    sum_ref[...] = jnp.zeros_like(sum_ref)
    for qb in range(blocks):
        kend = (qb + 1) * rows
        place = slice(qb * rows, kend)
        rel = rel_block(me_t, qb, tbits)
        mask_bias(bias, dcol_ref, drow_ref, qb, rows)

        def pair_body(pair, carry):
            base = pl.multiple_of(pair * 128, 128)
            lanes = pl.ds(base, 128)
            q = qkv_ref[0, place, lanes]
            k = qkv_ref[0, :kend, pl.ds(base + width, 128)]
            v = qkv_ref[0, :kend, pl.ds(base + 2 * width, 128)]
            kt = k.T
            do = do_ref[rel + (0, slice(None), lanes)]
            outs = []
            for h in range(2):
                mine = (lane < HD) if h == 0 else (lane >= HD)
                qm = jnp.where(mine, q, zero) * jnp.asarray(scale, bf16)
                dom = jnp.where(mine, do, zero)
                s = dot_nt(k, qm) + bias[:kend, :]
                probs = jnp.exp(s - lse_ref[0, pl.ds(pair * 2 + h, 1), place])
                dprobs = dot_nt(v, dom)
                inner = jnp.sum(probs * dprobs, axis=0, keepdims=True)
                ds = (probs * (dprobs - inner)).astype(bf16)
                dv[:kend, lanes] += dot_nn(probs.astype(bf16), dom)
                dk[:kend, lanes] += dot_nn(ds, qm)
                outs.append(dot_nn(kt[h * HD : (h + 1) * HD, :], ds))
            dq = jnp.concatenate(outs, axis=0).T * scale
            dq = dq * cos_ref[0, place, :] - swap_rotary(dq) * sin_ref[0, place, :]
            dq = dq.astype(bf16)
            o_ref[rel + (0, slice(None), lanes)] = dq
            sum_ref[0, :, lanes] += jnp.sum(dq.astype(f32), axis=0, keepdims=True)
            return carry

        lax.fori_loop(0, pairs, pair_body, 0)
    for b in range(blocks):
        rel = rel_block(me_t, b, tbits)
        place = slice(b * rows, (b + 1) * rows)
        cosine = cos_ref[0, place, :]
        sine = sin_ref[0, place, :]
        for j in range(pairs):
            lanes = slice(j * 128, (j + 1) * 128)
            part = dk[place, lanes]
            part = (part * cosine - swap_rotary(part) * sine).astype(bf16)
            kl = slice(width + j * 128, width + (j + 1) * 128)
            o_ref[rel + (0, slice(None), kl)] = part
            sum_ref[0, :, kl] += jnp.sum(part.astype(f32), axis=0, keepdims=True)
            part = dv[place, lanes].astype(bf16)
            vl = slice(2 * width + j * 128, 2 * width + (j + 1) * 128)
            o_ref[rel + (0, slice(None), vl)] = part
            sum_ref[0, :, vl] += jnp.sum(part.astype(f32), axis=0, keepdims=True)


def attend_back_call(me, qkv, do, lse, cosine, sine, doc_col, doc_row):
    tbits = do.ndim - 3
    seqs = do.shape[tbits]
    rows = do.shape[-2]
    width = do.shape[-1]
    length = rows << tbits
    lead = (2,) * tbits
    seq3 = lambda s: (s, 0, 0)
    rel_map = lambda s: (0,) * tbits + (s, 0, 0)
    heads = width // HD
    return pl.pallas_call(
        functools.partial(attend_back_kernel, tbits, width),
        grid=(seqs,),
        out_shape=[
            jax.ShapeDtypeStruct(lead + (seqs, rows, 3 * width), bf16),
            jax.ShapeDtypeStruct((seqs, 1, 3 * width), f32),
        ],
        in_specs=[
            smem_spec(),
            pl.BlockSpec((1, length, 3 * width), seq3),
            pl.BlockSpec(lead + (1, rows, width), rel_map),
            pl.BlockSpec((1, heads, length), seq3),
            pl.BlockSpec((1, length, 128), seq3),
            pl.BlockSpec((1, length, 128), seq3),
            pl.BlockSpec((1, length, 1), seq3),
            pl.BlockSpec((1, 1, length), seq3),
        ],
        out_specs=[
            pl.BlockSpec(lead + (1, rows, 3 * width), rel_map),
            pl.BlockSpec((1, 1, 3 * width), seq3),
        ],
        scratch_shapes=[
            pltpu.VMEM((length, rows), f32),
            pltpu.VMEM((length, width), f32),
            pltpu.VMEM((length, width), f32),
        ],
        compiler_params=vmem_params(50),
        name="attend_back",
    )(me, qkv, do, lse, cosine, sine, doc_col, doc_row)


def rotary_tables(doc_ids):
    length = doc_ids.shape[1]
    places = jnp.arange(length, dtype=jnp.int32)[None, :]
    before = jnp.concatenate([doc_ids[:, :1] - 1, doc_ids[:, :-1]], axis=1)
    starts = jnp.where(doc_ids != before, places, 0)
    first = lax.cummax(starts, axis=1)
    pos = (places - first).astype(f32)
    half = ROT // 2
    freqs = 10000.0 ** (-jnp.arange(half, dtype=f32) / half)
    angle = pos[:, :, None] * freqs
    cosine = jnp.cos(angle)
    sine = jnp.sin(angle)
    rest = doc_ids.shape + (HD - ROT,)
    cosine = jnp.concatenate([cosine, cosine, jnp.ones(rest, f32)], axis=-1)
    sine = jnp.concatenate([-sine, sine, jnp.zeros(rest, f32)], axis=-1)
    return jnp.concatenate([cosine, cosine], axis=-1), jnp.concatenate([sine, sine], axis=-1)


def per_device(
    inputs,
    segments,
    cotangent,
    qkv_weight,
    qkv_first,
    qkv_second,
    dense_weight,
    dense_first,
    dense_second,
    expand_weight,
    expand_first,
    expand_second,
    shrink_weight,
    shrink_first,
    shrink_second,
    small_params,
    small_first,
    small_second,
):
    dp = lax.axis_size("dp")
    tensor_count = lax.axis_size("tensor")
    dbits = dp.bit_length() - 1
    tbits = tensor_count.bit_length() - 1
    d_me = lax.axis_index("dp")
    t_me = lax.axis_index("tensor")
    sub = (d_me >> SUB_BIT) & 1
    order = place_order(dp)
    high_bits = list(range(2, dbits))
    gather_bits = high_bits + [ROW_BIT]
    rows = inputs.shape[0]
    me = jnp.stack([d_me, t_me]).astype(jnp.int32)

    stack = small_params.astype(bf16)[None]
    for bit in [SUB_BIT] + gather_bits:
        stack = jnp.concatenate([stack, exchange(stack, "dp", bit)], axis=0)
    block_of = jnp.asarray(order, jnp.int32) ^ d_me
    hit = jnp.arange(dp, dtype=jnp.int32)[:, None] == block_of[None, :]
    params = jnp.sum(
        jnp.where(hit[:, :, None, None], stack.astype(f32)[None], 0.0), axis=1
    )
    params = jnp.transpose(params, (1, 0, 2)).reshape(small_params.shape[0], D)

    ids = segments
    ids = jnp.concatenate([ids, exchange(ids, "dp", SUB_BIT)], axis=0)
    for bit in range(tbits):
        other = exchange(ids, "tensor", bit)
        flag = ((t_me >> bit) & 1) == 0
        ids = jnp.concatenate([jnp.where(flag, ids, other), jnp.where(flag, other, ids)], axis=1)
    cosine, sine = rotary_tables(ids)
    doc_col = ids[:, :, None]
    doc_row = ids[:, None, :]

    normed_own, normed_swap, back_own, back_swap, back_sum = norm_call(
        order, me, inputs, cotangent, params[0:1], params[1:2]
    )

    def gather_tokens(own, swapped):
        pieces = [own, exchange(swapped, "dp", SUB_BIT)]
        for bit in reversed(range(tbits)):
            pieces = pieces + [exchange(piece, "tensor", bit) for piece in pieces]
        return jnp.concatenate(pieces, axis=0)

    def gather_weight(low, split_axis, gather_axis):
        half = low.shape[split_axis] // 2
        keep = lax.dynamic_slice_in_dim(low, sub * half, half, split_axis)
        send = lax.dynamic_slice_in_dim(low, (1 - sub) * half, half, split_axis)
        pieces = [keep, exchange(send, "dp", SUB_BIT)]
        for bit in gather_bits:
            pieces = pieces + [exchange(piece, "dp", bit) for piece in pieces]
        return jnp.concatenate(pieces, axis=gather_axis)

    qkv_full = gather_weight(qkv_weight.astype(bf16), 2, 1)
    width = qkv_full.shape[2]
    qkv_wide = jnp.transpose(qkv_full, (1, 0, 2)).reshape(D, 3 * width)
    normed = gather_tokens(normed_own, normed_swap)
    expand_full = gather_weight(expand_weight.astype(bf16), 1, 0)
    hidden = expand_full.shape[1]
    back_rows = gather_tokens(back_own, back_swap)
    dense_full = gather_weight(dense_weight.astype(bf16), 0, 1)
    shrink_full = gather_weight(shrink_weight.astype(bf16), 0, 1)
    tokens = normed.shape[0]

    head_start = t_me * (2 * width) + sub * width
    hidden_start = t_me * (2 * hidden) + sub * hidden
    qkv_bias = lax.dynamic_slice_in_dim(params[2:5], head_start, width, 1).reshape(3 * width)
    expand_bias = lax.dynamic_slice_in_dim(params[7:].reshape(FF), hidden_start, hidden, 0)

    lead = (2,) * tbits
    proj = jnp.dot(normed, qkv_wide, preferred_element_type=f32) + qkv_bias
    attended, qkv_low, lse = attend_call(
        me, proj.reshape(lead + (2, rows, 3 * width)), cosine, sine, doc_col, doc_row
    )
    attended = attended.reshape(tokens, width)
    hidden_pre = jnp.dot(normed, expand_full, preferred_element_type=f32) + expand_bias
    hidden_act = gelu_value(hidden_pre).astype(bf16)

    def scatter_tokens(partial):
        half = tokens // 2
        recv = exchange(partial(half, tokens).astype(bf16), "tensor", 0)
        part = (partial(0, half) + recv.astype(f32)).astype(bf16)
        for bit in range(1, tbits):
            half = half // 2
            recv = exchange(part[half:], "tensor", bit)
            part = (part[:half].astype(f32) + recv.astype(f32)).astype(bf16)
        return part[:rows], exchange(part[rows:], "dp", SUB_BIT)

    def branch(start, stop):
        return jnp.dot(attended[start:stop], dense_full, preferred_element_type=f32) + jnp.dot(
            hidden_act[start:stop], shrink_full, preferred_element_type=f32
        )

    keep, recv = scatter_tokens(branch)
    output = out_call(order, me, inputs, keep, recv, params[5:7])

    def scatter_weight(partial, split_axis, gather_axis):
        recv = exchange(partial(1).astype(bf16), "dp", ROW_BIT)
        part = (partial(0) + recv.astype(f32)).astype(bf16)
        for bit in reversed(high_bits):
            half = part.shape[gather_axis] // 2
            recv = exchange(lax.slice_in_dim(part, half, 2 * half, axis=gather_axis), "dp", bit)
            part = (lax.slice_in_dim(part, 0, half, axis=gather_axis).astype(f32) + recv.astype(f32)).astype(bf16)
        half = part.shape[gather_axis] // 2
        recv = exchange(lax.slice_in_dim(part, half, 2 * half, axis=gather_axis), "dp", SUB_BIT)
        keep = lax.slice_in_dim(part, 0, half, axis=gather_axis)
        flag = sub == 0
        return jnp.concatenate(
            [jnp.where(flag, keep, recv), jnp.where(flag, recv, keep)], axis=split_axis
        ).astype(f32)

    halves = [slice(0, D // 2), slice(D // 2, D)]
    shrink_sum = scatter_weight(
        lambda i: jnp.einsum("sf,sd->fd", hidden_act, back_rows[:, halves[i]], preferred_element_type=f32), 0, 1
    )
    dense_sum = scatter_weight(
        lambda i: jnp.einsum("sk,sd->kd", attended, back_rows[:, halves[i]], preferred_element_type=f32), 0, 1
    )

    attended_back = jnp.einsum("sd,kd->sk", back_rows, dense_full, preferred_element_type=f32).astype(bf16)
    act_back = jnp.einsum("sd,fd->sf", back_rows, shrink_full, preferred_element_type=f32)
    pre_back = jax.vjp(gelu_value, hidden_pre)[1](act_back)[0].astype(bf16)
    expand_bias_grad = jnp.sum(pre_back, axis=0, dtype=f32)
    proj_back, qkv_bias_grad = attend_back_call(
        me, qkv_low, attended_back.reshape(lead + (2, rows, width)), lse, cosine, sine, doc_col, doc_row
    )
    proj_back = proj_back.reshape(tokens, 3 * width)
    qkv_bias_grad = jnp.sum(qkv_bias_grad, axis=(0, 1)).reshape(3, width)

    expand_sum = scatter_weight(
        lambda i: jnp.einsum("sd,sf->df", normed[:, halves[i]], pre_back, preferred_element_type=f32), 1, 0
    )

    def normed_back(start, stop):
        return jnp.einsum("se,de->sd", proj_back[start:stop], qkv_wide, preferred_element_type=f32) + jnp.einsum(
            "sf,df->sd", pre_back[start:stop], expand_full, preferred_element_type=f32
        )

    keep, recv = scatter_tokens(normed_back)
    input_grad, gain_shift = norm_back_call(order, me, inputs, cotangent, keep, recv, params[0:1])
    qkv_sum = scatter_weight(
        lambda i: jnp.einsum(
            "sd,se->de", normed[:, halves[i]], proj_back, preferred_element_type=f32
        ).reshape(D // 2, 3, width),
        2,
        0,
    )
    qkv_sum = jnp.transpose(qkv_sum, (1, 0, 2))

    qkv_rows = lax.dynamic_update_slice_in_dim(jnp.zeros((3, D), f32), qkv_bias_grad, head_start, 1)
    expand_rows = lax.dynamic_update_slice_in_dim(
        jnp.zeros((FF,), f32), expand_bias_grad, hidden_start, 0
    ).reshape(FF // D, D)
    params_grad = jnp.concatenate([gain_shift, qkv_rows, back_sum, back_sum, expand_rows], axis=0)
    part = params_grad
    for bit in reversed(range(dbits)):
        half = part.shape[1] // 2
        mine = (d_me >> bit) & 1
        send = lax.dynamic_slice_in_dim(part, (1 - mine) * half, half, 1)
        part = lax.dynamic_slice_in_dim(part, mine * half, half, 1) + exchange(send, "dp", bit)
    for bit in range(tbits):
        part = part + exchange(part, "tensor", bit)

    qkv_new = adam_update(qkv_weight, qkv_first, qkv_second, qkv_sum, matrix_rate, weight_decay)
    dense_new = adam_update(dense_weight, dense_first, dense_second, dense_sum, matrix_rate, weight_decay)
    expand_new = adam_update(expand_weight, expand_first, expand_second, expand_sum, matrix_rate, weight_decay)
    shrink_new = adam_update(shrink_weight, shrink_first, shrink_second, shrink_sum, matrix_rate, weight_decay)
    small_new = adam_update(small_params, small_first, small_second, part, vector_rate, 0.0)
    return (output, input_grad) + qkv_new + dense_new + expand_new + shrink_new + small_new


def solution(mesh):
    token_spec = P(("dp", "tensor"), None)
    qkv_spec = P(None, "dp", "tensor")
    row_spec = P("tensor", "dp")
    column_spec = P("dp", "tensor")
    small_spec = P(None, "dp")
    weight_specs = (qkv_spec,) * 3 + (row_spec,) * 3 + (column_spec,) * 3 + (row_spec,) * 3 + (small_spec,) * 3
    return jax.shard_map(
        per_device,
        mesh=mesh,
        in_specs=(token_spec, P("dp", "tensor"), token_spec) + weight_specs,
        out_specs=(token_spec, token_spec) + weight_specs,
        check_vma=False,
    )
```

```python
import functools
import jax
import jax.numpy as jnp
from jax import lax
from jax.experimental import pallas as pl
from jax.experimental.pallas import tpu as pltpu
from jax.sharding import PartitionSpec as P

D = 2048
HD = 64
ROT = 32
FF = 8192
STEP = 10

norm_eps = 1e-05
beta_first = 0.9
beta_second = 0.95
adam_eps = 1e-08
weight_decay = 0.1
matrix_rate = 0.05
vector_rate = 1.0
masked_score = -1e30

SUB_BIT = 1
ROW_BIT = 0

bf16 = jnp.bfloat16
f32 = jnp.float32


def exchange(values, axis, bit):
    count = lax.axis_size(axis)
    return lax.ppermute(values, axis, [(i, i ^ (1 << bit)) for i in range(count)])


def place_order(count):
    bits = count.bit_length() - 1
    order = []
    for p in range(count):
        high = (p >> 1) & ((1 << (bits - 2)) - 1)
        order.append(((p & 1) << SUB_BIT) | (high << 2) | ((p >> (bits - 1)) << ROW_BIT))
    return order


def adam_update(weight, first, second, grad, rate, decay):
    first_new = beta_first * first + (1.0 - beta_first) * grad
    second_new = beta_second * second + (1.0 - beta_second) * grad * grad
    first_hat = first_new / (1.0 - beta_first**STEP)
    second_hat = second_new / (1.0 - beta_second**STEP)
    weight_new = weight - rate * (first_hat / (jnp.sqrt(second_hat) + adam_eps) + decay * weight)
    return (weight_new, first_new, second_new)


def after(values, *others):
    return lax.optimization_barrier((values,) + others)[0]


def gelu_value(pre_values):
    return jax.nn.gelu(pre_values, approximate=True)


def vmem_params(mib):
    return pltpu.CompilerParams(vmem_limit_bytes=mib * 2**20)


def place_of(block, count):
    bits = count.bit_length() - 1
    return ((block >> SUB_BIT) & 1) | ((block >> 2) << 1) | (((block >> ROW_BIT) & 1) << (bits - 1))


def move_blocks(count, source, load, store):
    width = D // count
    if width % 128 == 0:
        for j in range(count):
            start = pl.multiple_of(source(j) * width, width)
            store(pl.ds(j * width, width), load(pl.ds(start, width)))
        return
    for unit in range(count // 2):
        parts = []
        for half in range(2):
            block = source(2 * unit + half)
            value = load(pl.ds(pl.multiple_of((block >> 1) * 128, 128), 128))
            parts.append(pltpu.roll(value, ((block & 1) ^ half) * 64, 1))
        lane = lax.broadcasted_iota(jnp.int32, parts[0].shape, 1)
        store(pl.ds(unit * 128, 128), jnp.where(lane < 64, parts[0], parts[1]))


def smem_spec():
    return pl.BlockSpec(memory_space=pltpu.SMEM)


def assemble(order, me, keep_ref, recv_ref, tmp):
    count = len(order)

    def store(lanes, value):
        tmp[:, lanes] = value

    def add(lanes, value):
        tmp[:, lanes] += value

    move_blocks(count, lambda j: place_of(j ^ me, count), lambda lanes: keep_ref[:, lanes].astype(f32), store)
    move_blocks(count, lambda j: place_of(j ^ me, count) ^ 1, lambda lanes: recv_ref[:, lanes].astype(f32), add)


def out_kernel(order, me_ref, x_ref, keep_ref, recv_ref, b_ref, o_ref, tmp):
    assemble(order, me_ref[0], keep_ref, recv_ref, tmp)
    o_ref[...] = (x_ref[...].astype(f32) + tmp[...] + b_ref[0:1] + b_ref[1:2]).astype(bf16)


def out_call(order, me, x, keep, recv, biases):
    vm = pl.BlockSpec(memory_space=pltpu.VMEM)
    return pl.pallas_call(
        functools.partial(out_kernel, order),
        out_shape=jax.ShapeDtypeStruct(x.shape, bf16),
        in_specs=[smem_spec(), vm, vm, vm, vm],
        out_specs=vm,
        scratch_shapes=[pltpu.VMEM(x.shape, f32)],
        compiler_params=vmem_params(32),
        name="block_output",
    )(me, x, keep, recv, biases)


def norm_back_kernel(order, me_ref, x_ref, dy_ref, keep_ref, recv_ref, g_ref, o_ref, sums_ref, tmp):
    assemble(order, me_ref[0], keep_ref, recv_ref, tmp)
    rows = x_ref[...].astype(f32)
    centered = rows - jnp.mean(rows, axis=-1, keepdims=True)
    inv = lax.rsqrt(jnp.mean(centered * centered, axis=-1, keepdims=True) + norm_eps)
    unit = centered * inv
    back = tmp[...]
    sums_ref[0:1] = jnp.sum(back * unit, axis=0, keepdims=True)
    sums_ref[1:2] = jnp.sum(back, axis=0, keepdims=True)
    e = back * g_ref[...]
    o_ref[...] = dy_ref[...].astype(f32) + inv * (
        e - jnp.mean(e, axis=-1, keepdims=True) - unit * jnp.mean(e * unit, axis=-1, keepdims=True)
    )


def norm_back_call(order, me, x, dy, keep, recv, gain):
    vm = pl.BlockSpec(memory_space=pltpu.VMEM)
    return pl.pallas_call(
        functools.partial(norm_back_kernel, order),
        out_shape=[jax.ShapeDtypeStruct(x.shape, f32), jax.ShapeDtypeStruct((2, D), f32)],
        in_specs=[smem_spec()] + [vm] * 5,
        out_specs=[vm, vm],
        scratch_shapes=[pltpu.VMEM(x.shape, f32)],
        compiler_params=vmem_params(40),
        name="norm_back",
    )(me, x, dy, keep, recv, gain)


def swap_rotary(values):
    lane = lax.broadcasted_iota(jnp.int32, values.shape, 1)
    half = ROT // 2
    return jnp.where(
        lane % ROT < half, pltpu.roll(values, 128 - half, 1), pltpu.roll(values, half, 1)
    )


def dot_nn(a, b):
    return lax.dot_general(a, b, (((1,), (0,)), ((), ())), preferred_element_type=f32)


def dot_nt(a, b):
    return lax.dot_general(a, b, (((1,), (1,)), ((), ())), preferred_element_type=f32)


def dot_tn(a, b):
    return lax.dot_general(a, b, (((0,), (0,)), ((), ())), preferred_element_type=f32)


def rel_index(rel, seq, tbits):
    index = seq
    for b in range(tbits):
        index = index | (((rel >> b) & 1) << (tbits - b))
    return index


def mask_bias(bias, start_row, qb, rows):
    kend = (qb + 1) * rows
    key = lax.broadcasted_iota(jnp.int32, (kend, rows), 0)
    query = lax.broadcasted_iota(jnp.int32, (kend, rows), 1) + qb * rows
    bias[:kend, :] = jnp.where((key >= start_row) & (key <= query), 0.0, masked_score)


def attend_rows(qkv, lse, bias, o, seq, qb, width, out_rows):
    rows = bias.shape[1]
    kend = (qb + 1) * rows
    place = slice(qb * rows, kend)
    lane = lax.broadcasted_iota(jnp.int32, (rows, 128), 1)
    zero = jnp.zeros((rows, 128), bf16)

    def pair_body(pair, carry):
        base = pl.multiple_of(pair * 128, 128)
        q = qkv[seq, place, pl.ds(base, 128)] * jnp.asarray(HD ** (-0.5), bf16)
        k = qkv[seq, :kend, pl.ds(base + width, 128)]
        v = qkv[seq, :kend, pl.ds(base + 2 * width, 128)]
        vt = v.T
        outs = []
        for h in range(2):
            mine = (lane < HD) if h == 0 else (lane >= HD)
            s = dot_nt(k, jnp.where(mine, q, zero)) + bias[:kend, :]
            peak = jnp.max(s, axis=0, keepdims=True)
            expo = jnp.exp(s - peak)
            total = jnp.sum(expo, axis=0, keepdims=True)
            weights = (expo * (1.0 / total)).astype(bf16)
            outs.append(dot_nn(vt[h * HD : (h + 1) * HD, :], weights))
            lse[seq, pl.ds(pair * 2 + h, 1), place] = peak + jnp.log(total)
        o[out_rows, pl.ds(base, 128)] = jnp.concatenate(outs, axis=0).T.astype(bf16)
        return carry

    lax.fori_loop(0, width // 128, pair_body, 0)


def attend_back_rows(qkv, lse, bias, do, cosb, sinb, dk, dv, dp, sums, seq, qb, width, out_rows):
    rows = bias.shape[1]
    kend = (qb + 1) * rows
    place = slice(qb * rows, kend)
    scale = HD ** (-0.5)
    lane = lax.broadcasted_iota(jnp.int32, (rows, 128), 1)
    zero = jnp.zeros((rows, 128), bf16)

    def pair_body(pair, carry):
        base = pl.multiple_of(pair * 128, 128)
        lanes = pl.ds(base, 128)
        q = qkv[seq, place, lanes]
        k = qkv[seq, :kend, pl.ds(base + width, 128)]
        v = qkv[seq, :kend, pl.ds(base + 2 * width, 128)]
        kt = k.T
        dout = do[out_rows, lanes]
        outs = []
        for h in range(2):
            mine = (lane < HD) if h == 0 else (lane >= HD)
            qm = jnp.where(mine, q, zero) * jnp.asarray(scale, bf16)
            dom = jnp.where(mine, dout, zero)
            s = dot_nt(k, qm) + bias[:kend, :]
            probs = jnp.exp(s - lse[seq, pl.ds(pair * 2 + h, 1), place])
            dprobs = dot_nt(v, dom)
            inner = jnp.sum(probs * dprobs, axis=0, keepdims=True)
            ds = (probs * (dprobs - inner)).astype(bf16)
            dv[:kend, lanes] += dot_nn(probs.astype(bf16), dom)
            dk[:kend, lanes] += dot_nn(ds, qm)
            outs.append(dot_nn(kt[h * HD : (h + 1) * HD, :], ds))
        dq = jnp.concatenate(outs, axis=0).T * scale
        dq = dq * cosb[seq, place, :] - swap_rotary(dq) * sinb[seq, place, :]
        dq = dq.astype(bf16)
        dp[out_rows, lanes] = dq
        sums[0:1, lanes] += jnp.sum(dq.astype(f32), axis=0, keepdims=True)
        return carry

    lax.fori_loop(0, width // 128, pair_body, 0)


def attend_back_keys(cosb, sinb, dk, dv, dp, sums, seq, b, width, out_rows):
    rows = out_rows.size
    place = slice(b * rows, (b + 1) * rows)
    cosine = cosb[seq, place, :]
    sine = sinb[seq, place, :]
    for j in range(width // 128):
        lanes = slice(j * 128, (j + 1) * 128)
        part = dk[place, lanes]
        part = (part * cosine - swap_rotary(part) * sine).astype(bf16)
        kl = slice(width + j * 128, width + (j + 1) * 128)
        dp[out_rows, kl] = part
        sums[0:1, kl] += jnp.sum(part.astype(f32), axis=0, keepdims=True)
        part = dv[place, lanes].astype(bf16)
        vl = slice(2 * width + j * 128, 2 * width + (j + 1) * 128)
        dp[out_rows, vl] = part
        sums[0:1, vl] += jnp.sum(part.astype(f32), axis=0, keepdims=True)


class Links:
    def __init__(self, send_sems, recv_sems, local_sems):
        self.send_sems, self.recv_sems, self.local_sems = send_sems, recv_sems, local_sems
        self.sent, self.count, self.locals = [], 0, 0

    def send(self, src, dst, axis, bit):
        partner = lax.axis_index(axis) ^ (1 << bit)
        i = self.count
        self.count += 1
        copy = pltpu.make_async_remote_copy(
            src_ref=src,
            dst_ref=dst,
            send_sem=self.send_sems.at[i],
            recv_sem=self.recv_sems.at[i],
            device_id={axis: partner},
            device_id_type=pl.DeviceIdType.MESH,
        )
        copy.start()
        self.sent.append(copy)
        return copy

    def local(self, src, dst):
        copy = pltpu.make_async_copy(src, dst, self.local_sems.at[self.locals])
        self.locals += 1
        copy.start()
        return copy

    def finish(self):
        for copy in self.sent:
            copy.wait_send()


def greet(dbits, tbits):
    barrier = pltpu.get_barrier_semaphore()
    partners = [("dp", b) for b in range(dbits)] + [("tensor", b) for b in range(tbits)]
    for axis, bit in partners:
        pl.semaphore_signal(
            barrier,
            inc=1,
            device_id={axis: lax.axis_index(axis) ^ (1 << bit)},
            device_id_type=pl.DeviceIdType.MESH,
        )
    pl.semaphore_wait(barrier, len(partners))


class Gathered:
    def __init__(self, links, slot, count, bits):
        self.links, self.slot, self.bits = links, slot, bits
        self.arrived = {0: None}
        self.steps = []
        size = 1
        for step, bit in enumerate(bits):
            self.steps.append((bit, size))
            size *= 2

    def push(self, p, first=0):
        for step in range(max(first, 1), len(self.steps)):
            bit, size = self.steps[step]
            if p < size:
                self.arrived[p + size] = self.links.send(self.slot(p), self.slot(p + size), "dp", bit)

    def start(self, outgoing):
        self.arrived[1] = self.links.send(outgoing, self.slot(1), "dp", self.bits[0])

    def take(self, p):
        self.arrived[p].wait_recv()
        self.push(p)


class GatheredPairs(Gathered):
    def __init__(self, links, slot, count, bits, own, received):
        super().__init__(links, slot, count, bits)
        self.own, self.received = own, received

    def push(self, p, first=0):
        if p % 2 == 0 and (p > 0 or first > 0):
            unit = p // 2
            for step in range(1, len(self.steps)):
                bit, size = self.steps[step]
                if p < size:
                    other = unit + size // 2
                    self.arrived[2 * other] = self.links.send(self.slot(unit), self.slot(other), "dp", bit)

    def start(self, outgoing):
        self.arrived[1] = self.links.send(outgoing, self.received, "dp", self.bits[0])

    def take(self, p):
        if p == 1:
            self.arrived[1].wait_recv()
            both = [self.own[...].astype(f32), self.received[...].astype(f32)]
            self.slot(0)[...] = jnp.concatenate(both, axis=1).astype(bf16)
            self.push(0, 1)
        elif p % 2 == 0:
            self.arrived[p].wait_recv()
            self.push(p)


def cast_store(dst, src):
    dst[...] = src[...].astype(bf16)


def gather_kernel(
    cfg,
    x_ref, dy_ref, ids_ref, small_ref, freq_ref, qkv_ref, w1_ref, wo_ref, w2_ref,
    n_out, dy_out, wq_out, w1_out, wo_out, w2_out, h_out, gp_out, o_out, dp_out, params_out, dysum_out, sums_out,
    n, dyb, wq, w1, wo, w2, sq, s1, so, s2, sta, stb, stc, std, tmp, nsw, pbuf, idb, cosb, sinb, startb,
    qkvb, lse, bias, o, do, dk, dv, dp, hst, gst, send_sems, recv_sems, local_sems, *pieces
):
    dbits, tbits = cfg
    order = place_order(1 << dbits)
    count = len(order)
    me = lax.axis_index("dp")
    me_t = lax.axis_index("tensor")
    sub = (me >> SUB_BIT) & 1
    rows = x_ref.shape[0]
    width = wo.shape[0]
    hidden = w2.shape[0]
    blk = D // count
    seqs = 2
    blocks = 1 << tbits
    length = rows * blocks
    links = Links(send_sems, recv_sems, local_sems)
    bits = [SUB_BIT] + list(range(2, dbits)) + [ROW_BIT]

    own_q = pl.ds(pl.multiple_of(sub * width, width), width)
    other_q = pl.ds(pl.multiple_of((1 - sub) * width, width), width)
    own_h = pl.ds(pl.multiple_of(sub * hidden, hidden), hidden)
    other_h = pl.ds(pl.multiple_of((1 - sub) * hidden, hidden), hidden)
    loads_q = []
    for j in range(3):
        lanes = pl.ds(j * width, width)
        loads_q.append(links.local(qkv_ref.at[j, :, other_q], std.at[:, lanes]))
        loads_q.append(links.local(qkv_ref.at[j, :, own_q], stc.at[:, lanes]))
    loads_2 = [links.local(w2_ref.at[other_h, :], stb), links.local(w2_ref.at[own_h, :], sta)]

    def row_slot(ref):
        return lambda p: ref.at[pl.ds(p * blk, blk), :]

    def column_gather(ref, own, received):
        unit = max(blk, 128)
        slot = lambda p: ref.at[:, pl.ds(p * unit, unit)]
        if unit == blk:
            return Gathered(links, slot, count, bits), slot(0)
        return GatheredPairs(links, slot, count, bits, own, received), own

    gq = Gathered(links, row_slot(wq), count, bits)
    g1 = Gathered(links, row_slot(w1), count, bits)
    go, wo_own = column_gather(wo, *pieces[0:2])
    g2, w2_own = column_gather(w2, *pieces[2:4])

    pbuf[0] = small_ref[...]
    idb[0] = ids_ref[...]
    greet(dbits, tbits)
    size = 1

    def ring(buf, size, axis, bit):
        return links.send(buf.at[pl.ds(0, size)], buf.at[pl.ds(size, size)], axis, bit)

    hop_p = ring(pbuf, 1, "dp", bits[0])
    hop_i = ring(idb, 1, "dp", SUB_BIT)

    for copy in loads_q:
        copy.wait()
    cast_store(sq, std.at[:, pl.ds(0, 3 * width)])
    gq.start(sq)
    wq[0:blk, :] = stc[:, : 3 * width].astype(bf16)
    gq.push(0)
    loads_1 = [links.local(w1_ref.at[:, other_h], std), links.local(w1_ref.at[:, own_h], stc)]

    x = x_ref[...].astype(f32)
    mean = jnp.mean(x, axis=-1, keepdims=True)
    x = x - mean
    inv = lax.rsqrt(jnp.mean(x * x, axis=-1, keepdims=True) + norm_eps)
    tmp[...] = x * inv

    ihops = [("tensor", bit) for bit in reversed(range(tbits))]
    isize = 2
    for step, bit in enumerate(bits[1:]):
        hop_p.wait_recv()
        size *= 2
        hop_p = ring(pbuf, size, "dp", bit)
        if step < len(ihops):
            hop_i.wait_recv()
            hop_i = ring(idb, isize, *ihops[step])
            isize *= 2
    hop_p.wait_recv()

    for a in range(0, count, max(1, 128 // blk)):
        part = [pbuf[place_of((a + k) ^ me, count)].astype(f32) for k in range(max(1, 128 // blk))]
        lanes = pl.ds(a * blk, max(blk, 128))
        params_out[:, lanes] = part[0] if len(part) == 1 else jnp.concatenate(part, axis=1)

    tmp[...] = tmp[...] * params_out[0:1, :] + params_out[1:2, :]

    def store_to(ref, count_rows):
        def store(lanes, value):
            ref[0:count_rows, lanes] = value.astype(bf16)

        return store

    load_tmp = lambda lanes: tmp[:, lanes]
    move_blocks(count, lambda j: me ^ order[j ^ 1], load_tmp, store_to(nsw, rows))
    tok = lambda ref, i: ref.at[pl.ds(i * rows, rows), :]
    n_in = {1: links.send(nsw, tok(n, 1), "dp", SUB_BIT)}
    move_blocks(count, lambda j: me ^ order[j], load_tmp, store_to(n, rows))

    def push_tokens(ref, arrived, i):
        for step, bit in enumerate(reversed(range(tbits))):
            size = 2 << step
            if i < size:
                arrived[i + size] = links.send(tok(ref, i), tok(ref, i + size), "tensor", bit)

    push_tokens(n, n_in, 0)

    def take_tokens(ref, arrived, i):
        arrived[i].wait_recv()
        push_tokens(ref, arrived, i)

    gq.take(1)
    for copy in loads_1:
        copy.wait()
    cast_store(s1, std)
    g1.start(s1)
    w1[0:blk, :] = stc[...].astype(bf16)
    g1.push(0)

    for copy in loads_2:
        copy.wait()
    cast_store(s2, stb)
    w2_own[...] = sta[...].astype(bf16)
    own_k = pl.ds(pl.multiple_of(sub * width, width), width)
    other_k = pl.ds(pl.multiple_of((1 - sub) * width, width), width)
    loads_o = [
        links.local(wo_ref.at[other_k, :], stb.at[pl.ds(0, width), :]),
        links.local(wo_ref.at[own_k, :], sta.at[pl.ds(0, width), :]),
    ]
    take_tokens(n, n_in, 1)
    g1.take(1)

    load_dy = lambda lanes: dy_ref[:, lanes].astype(f32)
    move_blocks(count, lambda j: me ^ order[j], load_dy, store_to(dyb, rows))
    n_in[1].wait_send()
    links.sent = [copy for copy in links.sent if copy is not n_in[1]]
    move_blocks(count, lambda j: me ^ order[j ^ 1], load_dy, store_to(nsw, rows))
    for copy in loads_o:
        copy.wait()
    so[...] = stb[0:width, :].astype(bf16)
    wo_own[...] = sta[0:width, :].astype(bf16)
    dy_in = {1: links.send(nsw, tok(dyb, 1), "dp", SUB_BIT)}
    go.start(so)
    g2.start(s2)
    push_tokens(dyb, dy_in, 0)
    go.push(0)

    for step in range(len(bits) - 1, len(ihops)):
        hop_i.wait_recv()
        hop_i = ring(idb, isize, *ihops[step])
        isize *= 2
    hop_i.wait_recv()
    half = ROT // 2
    for seq in range(seqs):
        row = jnp.concatenate(
            [idb[rel_index(me_t ^ b, seq, tbits)][0:1, :] for b in range(blocks)], axis=1
        ).astype(f32)
        first = jnp.sum(jnp.where(row < 1.0, 1.0, 0.0), axis=1, keepdims=True)
        second = jnp.sum(jnp.where(row < 2.0, 1.0, 0.0), axis=1, keepdims=True)
        begin = jnp.where(row < 1.0, 0.0, jnp.where(row < 2.0, first, second))
        place = lax.broadcasted_iota(jnp.int32, (1, length), 1).astype(f32)
        startb[seq, 0:1, :] = begin.astype(jnp.int32)
        angle = freq_ref[:, 0:1] * (place - begin)
        cosine, sine = jnp.cos(angle), jnp.sin(angle)
        rest = (HD - ROT, length)
        cosine = jnp.concatenate([cosine, cosine, jnp.ones(rest, f32)], axis=0)
        sine = jnp.concatenate([-sine, sine, jnp.zeros(rest, f32)], axis=0)
        cosb[seq] = jnp.concatenate([cosine, cosine], axis=0).T
        sinb[seq] = jnp.concatenate([sine, sine], axis=0).T

    dysum_out[...] = jnp.sum(dy_ref[...].astype(f32), axis=0, keepdims=True)

    head_start = me_t * (2 * width) + sub * width
    hidden_start = me_t * (2 * hidden) + sub * hidden
    lanes = pl.ds(pl.multiple_of(head_start, width), width)
    qkv_bias = [params_out[2 + j : 3 + j, lanes] for j in range(3)]
    row = 7 + hidden_start // D
    hidden_bias = params_out[pl.ds(row, 1), pl.ds(pl.multiple_of(hidden_start % D, hidden), hidden)]

    for p in range(2, count):
        gq.take(p)
    pairs = width // 128
    for c in range(blocks):
        for i in (2 * c, 2 * c + 1):
            if i > 1:
                take_tokens(n, n_in, i)
        rel = sum(((c >> (tbits - 1 - b)) & 1) << b for b in range(tbits))
        block = me_t ^ rel
        place = pl.ds(pl.multiple_of(block * rows, rows), rows)
        part = dot_nn(n[2 * c * rows : (2 * c + 2) * rows, :], wq[...])
        for seq in range(seqs):
            seq_rows = slice(seq * rows, (seq + 1) * rows)
            cosine, sine = cosb[seq, place, :], sinb[seq, place, :]
            for j in range(3 * pairs):
                kind, pair = j // pairs, j % pairs
                value = part[seq_rows, j * 128 : (j + 1) * 128] + qkv_bias[kind][:, pair * 128 : (pair + 1) * 128]
                if kind < 2:
                    value = value * cosine + swap_rotary(value) * sine
                qkvb[seq, place, j * 128 : (j + 1) * 128] = value.astype(bf16)
    stores = [links.local(n, n_out), links.local(wq, wq_out)]

    mid = count // 2

    def seq_rows_of(seq, b):
        return pl.ds(pl.multiple_of(rel_index(me_t ^ b, seq, tbits) * rows, rows), rows)

    def attend(seq):
        for qb in range(blocks):
            mask_bias(bias, startb[seq, 0:1, qb * rows : (qb + 1) * rows], qb, rows)
            attend_rows(qkvb, lse, bias, o, seq, qb, width, seq_rows_of(seq, qb))

    def attend_back(seq):
        dk[...] = jnp.zeros_like(dk)
        dv[...] = jnp.zeros_like(dv)
        for qb in range(blocks):
            mask_bias(bias, startb[seq, 0:1, qb * rows : (qb + 1) * rows], qb, rows)
            attend_back_rows(
                qkvb, lse, bias, do, cosb, sinb, dk, dv, dp, sums_out, seq, qb, width, seq_rows_of(seq, qb)
            )
        for b in range(blocks):
            attend_back_keys(cosb, sinb, dk, dv, dp, sums_out, seq, b, width, seq_rows_of(seq, b))

    sums_out[...] = jnp.zeros_like(sums_out)
    go.take(1)
    g2.push(0)
    g2.take(1)
    g1.take(2)
    attend(0)
    take_tokens(dyb, dy_in, 1)
    for p in range(3, mid):
        g1.take(p)
    attend(1)
    stores.append(links.local(o, o_out))
    for p in range(mid, count):
        g1.take(p)
    stores.append(links.local(w1, w1_out))

    kept = {}
    tile = hst.shape[2]
    for c in range(blocks):
        place = pl.ds(2 * c * rows, 2 * rows)
        for t in range(hidden // tile):
            lanes = pl.ds(t * tile, tile)
            slot = (c * (hidden // tile) + t) % 2
            for copy in kept.pop(slot, ()):
                copy.wait()
            v = dot_nn(n[place, :], w1[:, lanes]) + hidden_bias[:, t * tile : (t + 1) * tile]
            root = 0.7978845608028654
            square = v * v
            th = jnp.tanh(root * (v + 0.044715 * v * square))
            hst[slot] = (0.5 * v * (1.0 + th)).astype(bf16)
            gst[slot] = (
                0.5 * (1.0 + th) + 0.5 * v * (1.0 - th * th) * (root * (1.0 + (3 * 0.044715) * square))
            ).astype(bf16)
            kept[slot] = (
                links.local(hst.at[slot], h_out.at[place, lanes]),
                links.local(gst.at[slot], gp_out.at[place, lanes]),
            )
    for copies in kept.values():
        stores.extend(copies)

    for p in range(2, count):
        go.take(p)
    stores.append(links.local(wo, wo_out))
    for c in range(blocks):
        for i in (2 * c, 2 * c + 1):
            if i > 1:
                take_tokens(dyb, dy_in, i)
        place = slice(2 * c * rows, (2 * c + 2) * rows)
        do[place, :] = dot_nt(dyb[place, :], wo[...]).astype(bf16)
    stores.append(links.local(dyb, dy_out))
    g2.take(2)
    attend_back(0)
    for p in range(3, mid):
        g2.take(p)
    attend_back(1)
    stores.append(links.local(dp, dp_out))
    for p in range(mid, count):
        g2.take(p)
    stores.append(links.local(w2, w2_out))
    for copy in stores:
        copy.wait()
    links.finish()


def gather_call(dbits, tbits, x, dy, ids, small, qkv_weight, expand_weight, dense_weight, shrink_weight):
    count = 1 << dbits
    blk = D // count
    rows = x.shape[0]
    width = qkv_weight.shape[2] // 2
    hidden = expand_weight.shape[1] // 2
    tokens = rows * (2 << tbits)
    length = rows << tbits
    heads = width // HD
    half = ROT // 2
    freqs = (10000.0 ** (-jnp.arange(half, dtype=f32) / half))[:, None] * jnp.ones((1, 128), f32)
    any_spec = pl.BlockSpec(memory_space=pl.ANY)
    vm = pl.BlockSpec(memory_space=pltpu.VMEM)
    shape = lambda s, t=bf16: jax.ShapeDtypeStruct(s, t)
    vmem = lambda s, t=bf16: pltpu.VMEM(s, t)
    weights = 4 * (2 * count - 1) + 2 * 32 + 16
    scratch = [
        vmem((tokens, D)),
        vmem((tokens, D)),
        vmem((D, 3 * width)),
        vmem((D, hidden)),
        vmem((width, D)),
        vmem((hidden, D)),
        vmem((blk, 3 * width)),
        vmem((blk, hidden)),
        vmem((width, blk)),
        vmem((hidden, blk)),
        vmem((hidden, blk), f32),
        vmem((hidden, blk), f32),
        vmem((blk, hidden), f32),
        vmem((blk, hidden), f32),
        vmem((rows, D), f32),
        vmem((rows, D)),
        vmem((count, small.shape[0], blk)),
        vmem((2 << tbits, 8, rows), jnp.int32),
        vmem((2, length, 128), f32),
        vmem((2, length, 128), f32),
        vmem((2, 8, length), jnp.int32),
        vmem((2, length, 3 * width)),
        vmem((2, heads, length), f32),
        vmem((length, rows), f32),
        vmem((tokens, width)),
        vmem((tokens, width)),
        vmem((length, width), f32),
        vmem((length, width), f32),
        vmem((tokens, 3 * width)),
        vmem((2, 2 * rows, min(hidden, 512))),
        vmem((2, 2 * rows, min(hidden, 512))),
        pltpu.SemaphoreType.DMA((weights,)),
        pltpu.SemaphoreType.DMA((weights,)),
        pltpu.SemaphoreType.DMA((40,)),
    ]
    pieces = (vmem((width, blk)), vmem((hidden, blk)))
    scratch += [pieces[0]] * 2 + [pieces[1]] * 2 if blk % 128 else [vmem((16, 128))] * 4
    return pl.pallas_call(
        functools.partial(gather_kernel, (dbits, tbits)),
        out_shape=[
            shape((tokens, D)),
            shape((tokens, D)),
            shape((D, 3 * width)),
            shape((D, hidden)),
            shape((width, D)),
            shape((hidden, D)),
            shape((tokens, hidden)),
            shape((tokens, hidden)),
            shape((tokens, width)),
            shape((tokens, 3 * width)),
            shape((small.shape[0], D), f32),
            shape((1, D), f32),
            shape((8, 3 * width), f32),
        ],
        in_specs=[vm] * 5 + [any_spec] * 4,
        out_specs=[any_spec] * 10 + [vm] * 3,
        scratch_shapes=scratch,
        compiler_params=pltpu.CompilerParams(
            vmem_limit_bytes=62 * 2**20, collective_id=0, has_side_effects=True
        ),
        cost_estimate=pl.CostEstimate(flops=2 * 10**10, bytes_accessed=10**8, transcendentals=10**7),
        name="gather",
    )(x, dy, ids, small, freqs, qkv_weight, expand_weight, dense_weight, shrink_weight)


def adam_kernel(split_rows, parts, me_ref, w_ref, m_ref, v_ref, ka_ref, kb_ref, r_ref, wo_ref, mo_ref, vo_ref):
    sub = (me_ref[0] >> SUB_BIT) & 1
    own = ka_ref[...].astype(f32) + kb_ref[...].astype(f32)
    other = r_ref[...].astype(f32)
    if split_rows:
        grad = jnp.where(pl.program_id(0) // parts == sub, own, other)
    else:
        grad = jnp.concatenate([jnp.where(sub == 0, own, other), jnp.where(sub == 0, other, own)], axis=1)
    grad = grad.reshape(w_ref.shape)
    wo_ref[...], mo_ref[...], vo_ref[...] = adam_update(
        w_ref[...], m_ref[...], v_ref[...], grad, matrix_rate, weight_decay
    )


def adam_call(me, weight, first, second, keep_a, keep_b, recv, split_rows):
    shape = weight.shape
    parts = 1
    if len(shape) == 3:
        grid = shape[0]
        full = pl.BlockSpec((1,) + shape[1:], lambda i: (i, 0, 0))
        part = pl.BlockSpec((shape[1], shape[2] // 2), lambda i: (0, i))
    elif split_rows:
        block = min(512, shape[0] // 2)
        grid = shape[0] // block
        parts = grid // 2
        full = pl.BlockSpec((block, shape[1]), lambda i: (i, 0))
        part = pl.BlockSpec((block, shape[1]), lambda i: (i % parts, 0))
    else:
        block = 64
        grid = shape[0] // block
        full = pl.BlockSpec((block, shape[1]), lambda i: (i, 0))
        part = pl.BlockSpec((block, shape[1] // 2), lambda i: (i, 0))
    return tuple(
        pl.pallas_call(
            functools.partial(adam_kernel, split_rows, parts),
            grid=(grid,),
            out_shape=[jax.ShapeDtypeStruct(shape, f32)] * 3,
            in_specs=[smem_spec()] + [full] * 3 + [part] * 3,
            out_specs=[full] * 3,
            compiler_params=vmem_params(32),
            name="adam",
        )(me, weight, first, second, keep_a, keep_b, recv)
    )


def per_device(
    inputs,
    segments,
    cotangent,
    qkv_weight,
    qkv_first,
    qkv_second,
    dense_weight,
    dense_first,
    dense_second,
    expand_weight,
    expand_first,
    expand_second,
    shrink_weight,
    shrink_first,
    shrink_second,
    small_params,
    small_first,
    small_second,
):
    dp = lax.axis_size("dp")
    tensor_count = lax.axis_size("tensor")
    dbits = dp.bit_length() - 1
    tbits = tensor_count.bit_length() - 1
    d_me = lax.axis_index("dp")
    t_me = lax.axis_index("tensor")
    sub = (d_me >> SUB_BIT) & 1
    order = place_order(dp)
    high_bits = list(range(2, dbits))
    gather_bits = high_bits + [ROW_BIT]
    rows = inputs.shape[0]
    me = jnp.stack([d_me, t_me]).astype(jnp.int32)

    small_low = jnp.pad(small_params.astype(bf16), ((0, 16 - small_params.shape[0]), (0, 0)))
    ids = jnp.broadcast_to(segments, (8, rows))
    (
        normed, back_rows, qkv_wide, expand_full, dense_full, shrink_full, hidden_act, gelu_slope, attended, proj_back,
        params, back_sum, sums,
    ) = gather_call(
        dbits, tbits, inputs, cotangent, ids, small_low, qkv_weight, expand_weight, dense_weight, shrink_weight
    )
    width, hidden = dense_full.shape[0], shrink_full.shape[0]
    tokens = normed.shape[0]
    head_start = t_me * (2 * width) + sub * width
    hidden_start = t_me * (2 * hidden) + sub * hidden
    qkv_bias_grad = sums[0].reshape(3, width)

    def scatter_tokens(partial, gate):
        half = tokens // 2
        first = partial(half, tokens, gate).astype(bf16)
        recv = exchange(first, "tensor", 0)
        part = (partial(0, half, first) + recv.astype(f32)).astype(bf16)
        done = part
        for bit in range(1, tbits):
            half = half // 2
            recv = exchange(part[half:], "tensor", bit)
            part = (part[:half].astype(f32) + recv.astype(f32)).astype(bf16)
        return part[:rows], exchange(part[rows:], "dp", SUB_BIT), done

    def scatter_weight(partial, gather_axis, gate):
        cut = functools.partial(lax.slice_in_dim, axis=gather_axis)
        first = partial(1, gate).astype(bf16)
        recv = exchange(first, "dp", ROW_BIT)
        part = (partial(0, first) + recv.astype(f32)).astype(bf16)
        done = part
        for bit in reversed(high_bits[1:]):
            half = part.shape[gather_axis] // 2
            recv = exchange(cut(part, half, 2 * half), "dp", bit)
            part = (cut(part, 0, half).astype(f32) + recv.astype(f32)).astype(bf16)
        half = part.shape[gather_axis] // 2
        recv = exchange(cut(part, half, 2 * half), "dp", high_bits[0])
        keep_a, keep_b = cut(part, 0, half // 2), cut(recv, 0, half // 2)
        send = (cut(part, half // 2, half).astype(f32) + cut(recv, half // 2, half).astype(f32)).astype(bf16)
        return (keep_a, keep_b, exchange(send, "dp", SUB_BIT)), done

    halves = [slice(0, D // 2), slice(D // 2, D)]

    def branch(start, stop, gate):
        lhs = after(attended, gate)
        return jnp.dot(lhs[start:stop], dense_full, preferred_element_type=f32) + jnp.dot(
            hidden_act[start:stop], shrink_full, preferred_element_type=f32
        )

    keep, recv, done = scatter_tokens(branch, normed)
    output = out_call(order, me, inputs, keep, recv, params[5:7])

    def weight_part(left, right, spec, on_right):
        def partial(i, gate):
            if on_right:
                return jnp.einsum(spec, after(left, gate), right[:, halves[i]], preferred_element_type=f32)
            return jnp.einsum(spec, left[:, halves[i]], after(right, gate), preferred_element_type=f32)

        return partial

    dense_parts, done = scatter_weight(weight_part(attended, back_rows, "sk,sd->kd", True), 1, done)
    shrink_parts, done = scatter_weight(weight_part(hidden_act, back_rows, "sf,sd->fd", True), 1, done)
    act_back = jnp.einsum("sd,fd->sf", after(back_rows, done), shrink_full, preferred_element_type=f32)
    pre_back = (act_back * gelu_slope.astype(f32)).astype(bf16)
    expand_bias_grad = jnp.sum(pre_back, axis=0, dtype=f32)
    expand_parts, done = scatter_weight(weight_part(normed, pre_back, "sd,sf->df", False), 0, pre_back)

    def normed_back(start, stop, gate):
        return jnp.einsum(
            "se,de->sd", after(proj_back, gate)[start:stop], qkv_wide, preferred_element_type=f32
        ) + jnp.einsum("sf,df->sd", pre_back[start:stop], expand_full, preferred_element_type=f32)

    keep, recv, done = scatter_tokens(normed_back, done)
    input_grad, gain_shift = norm_back_call(order, me, inputs, cotangent, keep, recv, params[0:1])
    qkv_parts, done = scatter_weight(weight_part(normed, proj_back, "sd,se->de", False), 0, done)

    qkv_rows = lax.dynamic_update_slice_in_dim(jnp.zeros((3, D), f32), qkv_bias_grad, head_start, 1)
    expand_rows = lax.dynamic_update_slice_in_dim(
        jnp.zeros((FF,), f32), expand_bias_grad, hidden_start, 0
    ).reshape(FF // D, D)
    params_grad = jnp.concatenate([gain_shift, qkv_rows, back_sum, back_sum, expand_rows], axis=0)
    part = params_grad
    for bit in reversed(range(dbits)):
        half = part.shape[1] // 2
        mine = (d_me >> bit) & 1
        send = lax.dynamic_slice_in_dim(part, (1 - mine) * half, half, 1)
        part = lax.dynamic_slice_in_dim(part, mine * half, half, 1) + exchange(send, "dp", bit)
    for bit in range(tbits):
        part = part + exchange(part, "tensor", bit)

    dense_new = adam_call(me, dense_weight, dense_first, dense_second, *dense_parts, True)
    shrink_new = adam_call(me, shrink_weight, shrink_first, shrink_second, *shrink_parts, True)
    expand_new = adam_call(me, expand_weight, expand_first, expand_second, *expand_parts, False)
    qkv_new = adam_call(me, qkv_weight, qkv_first, qkv_second, *qkv_parts, False)
    small_new = adam_update(small_params, small_first, small_second, part, vector_rate, 0.0)
    return (output, input_grad) + qkv_new + dense_new + expand_new + shrink_new + small_new


def solution(mesh):
    token_spec = P(("dp", "tensor"), None)
    qkv_spec = P(None, "dp", "tensor")
    row_spec = P("tensor", "dp")
    column_spec = P("dp", "tensor")
    small_spec = P(None, "dp")
    weight_specs = (qkv_spec,) * 3 + (row_spec,) * 3 + (column_spec,) * 3 + (row_spec,) * 3 + (small_spec,) * 3
    return jax.shard_map(
        per_device,
        mesh=mesh,
        in_specs=(token_spec, P("dp", "tensor"), token_spec) + weight_specs,
        out_specs=(token_spec, token_spec) + weight_specs,
        check_vma=False,
    )
```

```python
import functools
import jax
import jax.numpy as jnp
from jax import lax
from jax.experimental import pallas as pl
from jax.experimental.pallas import tpu as pltpu
from jax.sharding import PartitionSpec as P

D = 2048
HD = 64
ROT = 32
FF = 8192
STEP = 10

norm_eps = 1e-05
beta_first = 0.9
beta_second = 0.95
adam_eps = 1e-08
weight_decay = 0.1
matrix_rate = 0.05
vector_rate = 1.0
masked_score = -1e30

SUB_BIT = 1
ROW_BIT = 0

bf16 = jnp.bfloat16
f32 = jnp.float32


def exchange(values, axis, bit):
    count = lax.axis_size(axis)
    return lax.ppermute(values, axis, [(i, i ^ (1 << bit)) for i in range(count)])


def place_order(count):
    bits = count.bit_length() - 1
    order = []
    for p in range(count):
        high = (p >> 1) & ((1 << (bits - 2)) - 1)
        order.append(((p & 1) << SUB_BIT) | (high << 2) | ((p >> (bits - 1)) << ROW_BIT))
    return order


def adam_update(weight, first, second, grad, rate, decay):
    first_new = beta_first * first + (1.0 - beta_first) * grad
    second_new = beta_second * second + (1.0 - beta_second) * grad * grad
    first_hat = first_new / (1.0 - beta_first**STEP)
    second_hat = second_new / (1.0 - beta_second**STEP)
    weight_new = weight - rate * (first_hat / (jnp.sqrt(second_hat) + adam_eps) + decay * weight)
    return (weight_new, first_new, second_new)


def after(values, *others):
    return lax.optimization_barrier((values,) + others)[0]


def gelu_value(pre_values):
    return jax.nn.gelu(pre_values, approximate=True)


def vmem_params(mib):
    return pltpu.CompilerParams(vmem_limit_bytes=mib * 2**20)


def place_of(block, count):
    bits = count.bit_length() - 1
    return ((block >> SUB_BIT) & 1) | ((block >> 2) << 1) | (((block >> ROW_BIT) & 1) << (bits - 1))


def move_blocks(count, source, load, store):
    width = D // count
    if width % 128 == 0:
        for j in range(count):
            start = pl.multiple_of(source(j) * width, width)
            store(pl.ds(j * width, width), load(pl.ds(start, width)))
        return
    for unit in range(count // 2):
        parts = []
        for half in range(2):
            block = source(2 * unit + half)
            value = load(pl.ds(pl.multiple_of((block >> 1) * 128, 128), 128))
            parts.append(pltpu.roll(value, ((block & 1) ^ half) * 64, 1))
        lane = lax.broadcasted_iota(jnp.int32, parts[0].shape, 1)
        store(pl.ds(unit * 128, 128), jnp.where(lane < 64, parts[0], parts[1]))


def smem_spec():
    return pl.BlockSpec(memory_space=pltpu.SMEM)


def assemble(order, me, keep_ref, recv_ref, tmp):
    count = len(order)

    def store(lanes, value):
        tmp[:, lanes] = value

    def add(lanes, value):
        tmp[:, lanes] += value

    move_blocks(count, lambda j: place_of(j ^ me, count), lambda lanes: keep_ref[:, lanes].astype(f32), store)
    move_blocks(count, lambda j: place_of(j ^ me, count) ^ 1, lambda lanes: recv_ref[:, lanes].astype(f32), add)


def swap_rotary(values):
    lane = lax.broadcasted_iota(jnp.int32, values.shape, 1)
    half = ROT // 2
    return jnp.where(
        lane % ROT < half, pltpu.roll(values, 128 - half, 1), pltpu.roll(values, half, 1)
    )


def dot_nn(a, b):
    return lax.dot_general(a, b, (((1,), (0,)), ((), ())), preferred_element_type=f32)


def dot_nt(a, b):
    return lax.dot_general(a, b, (((1,), (1,)), ((), ())), preferred_element_type=f32)


def dot_tn(a, b):
    return lax.dot_general(a, b, (((0,), (0,)), ((), ())), preferred_element_type=f32)


def rel_index(rel, seq, tbits):
    index = seq
    for b in range(tbits):
        index = index | (((rel >> b) & 1) << (tbits - b))
    return index


def mask_bias(bias, start_row, qb, rows):
    kend = (qb + 1) * rows
    key = lax.broadcasted_iota(jnp.int32, (kend, rows), 0)
    query = lax.broadcasted_iota(jnp.int32, (kend, rows), 1) + qb * rows
    bias[:kend, :] = jnp.where((key >= start_row) & (key <= query), 0.0, masked_score)


def attend_rows(qkv, lse, bias, o, seq, qb, width, out_rows):
    rows = bias.shape[1]
    kend = (qb + 1) * rows
    place = slice(qb * rows, kend)
    lane = lax.broadcasted_iota(jnp.int32, (rows, 128), 1)
    zero = jnp.zeros((rows, 128), bf16)

    def pair_body(pair, carry):
        base = pl.multiple_of(pair * 128, 128)
        q = qkv[seq, place, pl.ds(base, 128)] * jnp.asarray(HD ** (-0.5), bf16)
        k = qkv[seq, :kend, pl.ds(base + width, 128)]
        v = qkv[seq, :kend, pl.ds(base + 2 * width, 128)]
        vt = v.T
        outs = []
        for h in range(2):
            mine = (lane < HD) if h == 0 else (lane >= HD)
            s = dot_nt(k, jnp.where(mine, q, zero)) + bias[:kend, :]
            peak = jnp.max(s, axis=0, keepdims=True)
            expo = jnp.exp(s - peak)
            total = jnp.sum(expo, axis=0, keepdims=True)
            weights = (expo * (1.0 / total)).astype(bf16)
            outs.append(dot_nn(vt[h * HD : (h + 1) * HD, :], weights))
            lse[seq, pl.ds(pair * 2 + h, 1), place] = peak + jnp.log(total)
        o[out_rows, pl.ds(base, 128)] = jnp.concatenate(outs, axis=0).T.astype(bf16)
        return carry

    lax.fori_loop(0, width // 128, pair_body, 0)


def attend_back_rows(qkv, lse, bias, do, cosb, sinb, dk, dv, dp, sums, seq, qb, width, out_rows):
    rows = bias.shape[1]
    kend = (qb + 1) * rows
    place = slice(qb * rows, kend)
    scale = HD ** (-0.5)
    lane = lax.broadcasted_iota(jnp.int32, (rows, 128), 1)
    zero = jnp.zeros((rows, 128), bf16)

    def pair_body(pair, carry):
        base = pl.multiple_of(pair * 128, 128)
        lanes = pl.ds(base, 128)
        q = qkv[seq, place, lanes]
        k = qkv[seq, :kend, pl.ds(base + width, 128)]
        v = qkv[seq, :kend, pl.ds(base + 2 * width, 128)]
        kt = k.T
        dout = do[out_rows, lanes]
        outs = []
        for h in range(2):
            mine = (lane < HD) if h == 0 else (lane >= HD)
            qm = jnp.where(mine, q, zero) * jnp.asarray(scale, bf16)
            dom = jnp.where(mine, dout, zero)
            s = dot_nt(k, qm) + bias[:kend, :]
            probs = jnp.exp(s - lse[seq, pl.ds(pair * 2 + h, 1), place])
            dprobs = dot_nt(v, dom)
            inner = jnp.sum(probs * dprobs, axis=0, keepdims=True)
            ds = (probs * (dprobs - inner)).astype(bf16)
            dv[:kend, lanes] += dot_nn(probs.astype(bf16), dom)
            dk[:kend, lanes] += dot_nn(ds, qm)
            outs.append(dot_nn(kt[h * HD : (h + 1) * HD, :], ds))
        dq = jnp.concatenate(outs, axis=0).T * scale
        dq = dq * cosb[seq, place, :] - swap_rotary(dq) * sinb[seq, place, :]
        dq = dq.astype(bf16)
        dp[out_rows, lanes] = dq
        sums[0:1, lanes] += jnp.sum(dq.astype(f32), axis=0, keepdims=True)
        return carry

    lax.fori_loop(0, width // 128, pair_body, 0)


def attend_back_keys(cosb, sinb, dk, dv, dp, sums, seq, b, width, out_rows):
    rows = out_rows.size
    place = slice(b * rows, (b + 1) * rows)
    cosine = cosb[seq, place, :]
    sine = sinb[seq, place, :]
    for j in range(width // 128):
        lanes = slice(j * 128, (j + 1) * 128)
        part = dk[place, lanes]
        part = (part * cosine - swap_rotary(part) * sine).astype(bf16)
        kl = slice(width + j * 128, width + (j + 1) * 128)
        dp[out_rows, kl] = part
        sums[0:1, kl] += jnp.sum(part.astype(f32), axis=0, keepdims=True)
        part = dv[place, lanes].astype(bf16)
        vl = slice(2 * width + j * 128, 2 * width + (j + 1) * 128)
        dp[out_rows, vl] = part
        sums[0:1, vl] += jnp.sum(part.astype(f32), axis=0, keepdims=True)


class Links:
    def __init__(self, send_sems, recv_sems, local_sems):
        self.send_sems, self.recv_sems, self.local_sems = send_sems, recv_sems, local_sems
        self.sent, self.count, self.locals = [], 0, 0

    def send(self, src, dst, axis, bit):
        partner = lax.axis_index(axis) ^ (1 << bit)
        i = self.count
        self.count += 1
        copy = pltpu.make_async_remote_copy(
            src_ref=src,
            dst_ref=dst,
            send_sem=self.send_sems.at[i],
            recv_sem=self.recv_sems.at[i],
            device_id={axis: partner},
            device_id_type=pl.DeviceIdType.MESH,
        )
        copy.start()
        self.sent.append(copy)
        return copy

    def local(self, src, dst):
        copy = pltpu.make_async_copy(src, dst, self.local_sems.at[self.locals])
        self.locals += 1
        copy.start()
        return copy

    def local_wait(self, src, dst):
        self.local(src, dst).wait()

    def sent_done(self, copy):
        copy.wait_send()
        self.sent = [other for other in self.sent if other is not copy]

    def finish(self):
        for copy in self.sent:
            copy.wait_send()


def greet(dbits, tbits):
    barrier = pltpu.get_barrier_semaphore()
    partners = [("dp", b) for b in range(dbits)] + [("tensor", b) for b in range(tbits)]
    for axis, bit in partners:
        pl.semaphore_signal(
            barrier,
            inc=1,
            device_id={axis: lax.axis_index(axis) ^ (1 << bit)},
            device_id_type=pl.DeviceIdType.MESH,
        )
    pl.semaphore_wait(barrier, len(partners))


class Gathered:
    def __init__(self, links, slot, count, bits):
        self.links, self.slot, self.bits = links, slot, bits
        self.arrived = {0: None}
        self.steps = []
        size = 1
        for step, bit in enumerate(bits):
            self.steps.append((bit, size))
            size *= 2

    def push(self, p, first=0):
        for step in range(max(first, 1), len(self.steps)):
            bit, size = self.steps[step]
            if p < size:
                self.arrived[p + size] = self.links.send(self.slot(p), self.slot(p + size), "dp", bit)

    def start(self, outgoing):
        self.arrived[1] = self.links.send(outgoing, self.slot(1), "dp", self.bits[0])

    def take(self, p):
        self.arrived[p].wait_recv()
        self.push(p)


class GatheredPairs(Gathered):
    def __init__(self, links, slot, count, bits, own, received):
        super().__init__(links, slot, count, bits)
        self.own, self.received = own, received

    def push(self, p, first=0):
        if p % 2 == 0 and (p > 0 or first > 0):
            unit = p // 2
            for step in range(1, len(self.steps)):
                bit, size = self.steps[step]
                if p < size:
                    other = unit + size // 2
                    self.arrived[2 * other] = self.links.send(self.slot(unit), self.slot(other), "dp", bit)

    def start(self, outgoing):
        self.arrived[1] = self.links.send(outgoing, self.received, "dp", self.bits[0])

    def take(self, p):
        if p == 1:
            self.arrived[1].wait_recv()
            both = [self.own[...].astype(f32), self.received[...].astype(f32)]
            self.slot(0)[...] = jnp.concatenate(both, axis=1).astype(bf16)
            self.push(0, 1)
        elif p % 2 == 0:
            self.arrived[p].wait_recv()
            self.push(p)


def cast_store(dst, src):
    dst[...] = src[...].astype(bf16)


def gather_kernel(
    cfg,
    x_ref, dy_ref, ids_ref, small_ref, freq_ref, qkv_ref, w1_ref, wo_ref, w2_ref,
    n_out, dy_out, wq_out, w1_out, wo_out, w2_out, h_out, gp_out, o_out, dp_out, params_out, dysum_out, sums_out,
    n, dyb, wq, w1, wo, w2, sq, s1, so, s2, sta, stb, stc, std, tmp, nsw, pbuf, idb, cosb, sinb, startb,
    qkvb, lse, bias, o, do, dk, dv, dp, hst, gst, send_sems, recv_sems, local_sems, *pieces
):
    dbits, tbits = cfg
    order = place_order(1 << dbits)
    count = len(order)
    me = lax.axis_index("dp")
    me_t = lax.axis_index("tensor")
    sub = (me >> SUB_BIT) & 1
    rows = x_ref.shape[0]
    width = wo.shape[0]
    hidden = w2.shape[0]
    blk = D // count
    seqs = 2
    blocks = 1 << tbits
    length = rows * blocks
    links = Links(send_sems, recv_sems, local_sems)
    bits = [SUB_BIT] + list(range(2, dbits)) + [ROW_BIT]

    own_q = pl.ds(pl.multiple_of(sub * width, width), width)
    other_q = pl.ds(pl.multiple_of((1 - sub) * width, width), width)
    own_h = pl.ds(pl.multiple_of(sub * hidden, hidden), hidden)
    other_h = pl.ds(pl.multiple_of((1 - sub) * hidden, hidden), hidden)
    loads_q = []
    for j in range(3):
        lanes = pl.ds(j * width, width)
        loads_q.append(links.local(qkv_ref.at[j, :, other_q], std.at[:, lanes]))
        loads_q.append(links.local(qkv_ref.at[j, :, own_q], stc.at[:, lanes]))
    loads_2 = [links.local(w2_ref.at[other_h, :], stb), links.local(w2_ref.at[own_h, :], sta)]

    def row_slot(ref):
        return lambda p: ref.at[pl.ds(p * blk, blk), :]

    def column_gather(ref, own, received):
        unit = max(blk, 128)
        slot = lambda p: ref.at[:, pl.ds(p * unit, unit)]
        if unit == blk:
            return Gathered(links, slot, count, bits), slot(0)
        return GatheredPairs(links, slot, count, bits, own, received), own

    gq = Gathered(links, row_slot(wq), count, bits)
    g1 = Gathered(links, row_slot(w1), count, bits)
    go, wo_own = column_gather(wo, *pieces[0:2])
    g2, w2_own = column_gather(w2, *pieces[2:4])

    pbuf[0] = small_ref[...]
    idb[0] = ids_ref[...]
    greet(dbits, tbits)
    size = 1

    def ring(buf, size, axis, bit):
        return links.send(buf.at[pl.ds(0, size)], buf.at[pl.ds(size, size)], axis, bit)

    hop_p = ring(pbuf, 1, "dp", bits[0])
    hop_i = ring(idb, 1, "dp", SUB_BIT)

    for copy in loads_q:
        copy.wait()
    cast_store(sq, std.at[:, pl.ds(0, 3 * width)])
    gq.start(sq)
    wq[0:blk, :] = stc[:, : 3 * width].astype(bf16)
    gq.push(0)
    loads_1 = [links.local(w1_ref.at[:, other_h], std), links.local(w1_ref.at[:, own_h], stc)]

    x = x_ref[...].astype(f32)
    mean = jnp.mean(x, axis=-1, keepdims=True)
    x = x - mean
    inv = lax.rsqrt(jnp.mean(x * x, axis=-1, keepdims=True) + norm_eps)
    tmp[...] = x * inv

    ihops = [("tensor", bit) for bit in reversed(range(tbits))]
    isize = 2
    for step, bit in enumerate(bits[1:]):
        hop_p.wait_recv()
        size *= 2
        hop_p = ring(pbuf, size, "dp", bit)
        if step < len(ihops):
            hop_i.wait_recv()
            hop_i = ring(idb, isize, *ihops[step])
            isize *= 2
    hop_p.wait_recv()

    for a in range(0, count, max(1, 128 // blk)):
        part = [pbuf[place_of((a + k) ^ me, count)].astype(f32) for k in range(max(1, 128 // blk))]
        lanes = pl.ds(a * blk, max(blk, 128))
        params_out[:, lanes] = part[0] if len(part) == 1 else jnp.concatenate(part, axis=1)

    tmp[...] = tmp[...] * params_out[0:1, :] + params_out[1:2, :]

    def store_to(ref, count_rows):
        def store(lanes, value):
            ref[0:count_rows, lanes] = value.astype(bf16)

        return store

    load_tmp = lambda lanes: tmp[:, lanes]
    move_blocks(count, lambda j: me ^ order[j ^ 1], load_tmp, store_to(nsw, rows))
    tok = lambda ref, i: ref.at[pl.ds(i * rows, rows), :]
    n_in = {1: links.send(nsw, tok(n, 1), "dp", SUB_BIT)}
    move_blocks(count, lambda j: me ^ order[j], load_tmp, store_to(n, rows))

    def push_tokens(ref, arrived, i):
        for step, bit in enumerate(reversed(range(tbits))):
            size = 2 << step
            if i < size:
                arrived[i + size] = links.send(tok(ref, i), tok(ref, i + size), "tensor", bit)

    push_tokens(n, n_in, 0)

    def take_tokens(ref, arrived, i):
        arrived[i].wait_recv()
        push_tokens(ref, arrived, i)

    gq.take(1)
    for copy in loads_1:
        copy.wait()
    cast_store(s1, std)
    g1.start(s1)
    w1[0:blk, :] = stc[...].astype(bf16)
    g1.push(0)

    for copy in loads_2:
        copy.wait()
    cast_store(s2, stb)
    w2_own[...] = sta[...].astype(bf16)
    own_k = pl.ds(pl.multiple_of(sub * width, width), width)
    other_k = pl.ds(pl.multiple_of((1 - sub) * width, width), width)
    loads_o = [
        links.local(wo_ref.at[other_k, :], stb.at[pl.ds(0, width), :]),
        links.local(wo_ref.at[own_k, :], sta.at[pl.ds(0, width), :]),
    ]
    take_tokens(n, n_in, 1)
    g1.take(1)

    load_dy = lambda lanes: dy_ref[:, lanes].astype(f32)
    move_blocks(count, lambda j: me ^ order[j], load_dy, store_to(dyb, rows))
    links.sent_done(n_in[1])
    move_blocks(count, lambda j: me ^ order[j ^ 1], load_dy, store_to(nsw, rows))
    for copy in loads_o:
        copy.wait()
    so[...] = stb[0:width, :].astype(bf16)
    wo_own[...] = sta[0:width, :].astype(bf16)
    dy_in = {1: links.send(nsw, tok(dyb, 1), "dp", SUB_BIT)}
    go.start(so)
    g2.start(s2)
    push_tokens(dyb, dy_in, 0)
    go.push(0)

    for step in range(len(bits) - 1, len(ihops)):
        hop_i.wait_recv()
        hop_i = ring(idb, isize, *ihops[step])
        isize *= 2
    hop_i.wait_recv()
    half = ROT // 2
    for seq in range(seqs):
        row = jnp.concatenate(
            [idb[rel_index(me_t ^ b, seq, tbits)][0:1, :] for b in range(blocks)], axis=1
        ).astype(f32)
        first = jnp.sum(jnp.where(row < 1.0, 1.0, 0.0), axis=1, keepdims=True)
        second = jnp.sum(jnp.where(row < 2.0, 1.0, 0.0), axis=1, keepdims=True)
        begin = jnp.where(row < 1.0, 0.0, jnp.where(row < 2.0, first, second))
        place = lax.broadcasted_iota(jnp.int32, (1, length), 1).astype(f32)
        startb[seq, 0:1, :] = begin.astype(jnp.int32)
        angle = freq_ref[:, 0:1] * (place - begin)
        cosine, sine = jnp.cos(angle), jnp.sin(angle)
        rest = (HD - ROT, length)
        cosine = jnp.concatenate([cosine, cosine, jnp.ones(rest, f32)], axis=0)
        sine = jnp.concatenate([-sine, sine, jnp.zeros(rest, f32)], axis=0)
        cosb[seq] = jnp.concatenate([cosine, cosine], axis=0).T
        sinb[seq] = jnp.concatenate([sine, sine], axis=0).T

    dysum_out[...] = jnp.sum(dy_ref[...].astype(f32), axis=0, keepdims=True)

    head_start = me_t * (2 * width) + sub * width
    hidden_start = me_t * (2 * hidden) + sub * hidden
    lanes = pl.ds(pl.multiple_of(head_start, width), width)
    qkv_bias = [params_out[2 + j : 3 + j, lanes] for j in range(3)]
    row = 7 + hidden_start // D
    hidden_bias = params_out[pl.ds(row, 1), pl.ds(pl.multiple_of(hidden_start % D, hidden), hidden)]

    for p in range(2, count):
        gq.take(p)
    pairs = width // 128
    for c in range(blocks):
        for i in (2 * c, 2 * c + 1):
            if i > 1:
                take_tokens(n, n_in, i)
        rel = sum(((c >> (tbits - 1 - b)) & 1) << b for b in range(tbits))
        block = me_t ^ rel
        place = pl.ds(pl.multiple_of(block * rows, rows), rows)
        part = dot_nn(n[2 * c * rows : (2 * c + 2) * rows, :], wq[...])
        for seq in range(seqs):
            seq_rows = slice(seq * rows, (seq + 1) * rows)
            cosine, sine = cosb[seq, place, :], sinb[seq, place, :]
            for j in range(3 * pairs):
                kind, pair = j // pairs, j % pairs
                value = part[seq_rows, j * 128 : (j + 1) * 128] + qkv_bias[kind][:, pair * 128 : (pair + 1) * 128]
                if kind < 2:
                    value = value * cosine + swap_rotary(value) * sine
                qkvb[seq, place, j * 128 : (j + 1) * 128] = value.astype(bf16)
    stores = [links.local(n, n_out), links.local(wq, wq_out)]

    mid = count // 2

    def seq_rows_of(seq, b):
        return pl.ds(pl.multiple_of(rel_index(me_t ^ b, seq, tbits) * rows, rows), rows)

    def attend(seq):
        for qb in range(blocks):
            mask_bias(bias, startb[seq, 0:1, qb * rows : (qb + 1) * rows], qb, rows)
            attend_rows(qkvb, lse, bias, o, seq, qb, width, seq_rows_of(seq, qb))

    def attend_back(seq):
        dk[...] = jnp.zeros_like(dk)
        dv[...] = jnp.zeros_like(dv)
        for qb in range(blocks):
            mask_bias(bias, startb[seq, 0:1, qb * rows : (qb + 1) * rows], qb, rows)
            attend_back_rows(
                qkvb, lse, bias, do, cosb, sinb, dk, dv, dp, sums_out, seq, qb, width, seq_rows_of(seq, qb)
            )
        for b in range(blocks):
            attend_back_keys(cosb, sinb, dk, dv, dp, sums_out, seq, b, width, seq_rows_of(seq, b))

    sums_out[...] = jnp.zeros_like(sums_out)
    go.take(1)
    g2.push(0)
    g2.take(1)
    g1.take(2)
    attend(0)
    take_tokens(dyb, dy_in, 1)
    for p in range(3, mid):
        g1.take(p)
    attend(1)
    stores.append(links.local(o, o_out))
    for p in range(mid, count):
        g1.take(p)
    stores.append(links.local(w1, w1_out))

    kept = {}
    tile = hst.shape[2]
    for c in range(blocks):
        place = pl.ds(2 * c * rows, 2 * rows)
        for t in range(hidden // tile):
            lanes = pl.ds(t * tile, tile)
            slot = (c * (hidden // tile) + t) % 2
            for copy in kept.pop(slot, ()):
                copy.wait()
            v = dot_nn(n[place, :], w1[:, lanes]) + hidden_bias[:, t * tile : (t + 1) * tile]
            root = 0.7978845608028654
            square = v * v
            th = jnp.tanh(root * (v + 0.044715 * v * square))
            hst[slot] = (0.5 * v * (1.0 + th)).astype(bf16)
            gst[slot] = (
                0.5 * (1.0 + th) + 0.5 * v * (1.0 - th * th) * (root * (1.0 + (3 * 0.044715) * square))
            ).astype(bf16)
            kept[slot] = (
                links.local(hst.at[slot], h_out.at[place, lanes]),
                links.local(gst.at[slot], gp_out.at[place, lanes]),
            )
    for copies in kept.values():
        stores.extend(copies)

    for p in range(2, count):
        go.take(p)
    stores.append(links.local(wo, wo_out))
    for c in range(blocks):
        for i in (2 * c, 2 * c + 1):
            if i > 1:
                take_tokens(dyb, dy_in, i)
        place = slice(2 * c * rows, (2 * c + 2) * rows)
        do[place, :] = dot_nt(dyb[place, :], wo[...]).astype(bf16)
    stores.append(links.local(dyb, dy_out))
    g2.take(2)
    attend_back(0)
    for p in range(3, mid):
        g2.take(p)
    attend_back(1)
    stores.append(links.local(dp, dp_out))
    for p in range(mid, count):
        g2.take(p)
    stores.append(links.local(w2, w2_out))
    for copy in stores:
        copy.wait()
    links.finish()


def gather_call(dbits, tbits, x, dy, ids, small, qkv_weight, expand_weight, dense_weight, shrink_weight):
    count = 1 << dbits
    blk = D // count
    rows = x.shape[0]
    width = qkv_weight.shape[2] // 2
    hidden = expand_weight.shape[1] // 2
    tokens = rows * (2 << tbits)
    length = rows << tbits
    heads = width // HD
    half = ROT // 2
    freqs = (10000.0 ** (-jnp.arange(half, dtype=f32) / half))[:, None] * jnp.ones((1, 128), f32)
    any_spec = pl.BlockSpec(memory_space=pl.ANY)
    vm = pl.BlockSpec(memory_space=pltpu.VMEM)
    shape = lambda s, t=bf16: jax.ShapeDtypeStruct(s, t)
    vmem = lambda s, t=bf16: pltpu.VMEM(s, t)
    weights = 4 * (2 * count - 1) + 2 * 32 + 16
    scratch = [
        vmem((tokens, D)),
        vmem((tokens, D)),
        vmem((D, 3 * width)),
        vmem((D, hidden)),
        vmem((width, D)),
        vmem((hidden, D)),
        vmem((blk, 3 * width)),
        vmem((blk, hidden)),
        vmem((width, blk)),
        vmem((hidden, blk)),
        vmem((hidden, blk), f32),
        vmem((hidden, blk), f32),
        vmem((blk, hidden), f32),
        vmem((blk, hidden), f32),
        vmem((rows, D), f32),
        vmem((rows, D)),
        vmem((count, small.shape[0], blk)),
        vmem((2 << tbits, 8, rows), jnp.int32),
        vmem((2, length, 128), f32),
        vmem((2, length, 128), f32),
        vmem((2, 8, length), jnp.int32),
        vmem((2, length, 3 * width)),
        vmem((2, heads, length), f32),
        vmem((length, rows), f32),
        vmem((tokens, width)),
        vmem((tokens, width)),
        vmem((length, width), f32),
        vmem((length, width), f32),
        vmem((tokens, 3 * width)),
        vmem((2, 2 * rows, min(hidden, 512))),
        vmem((2, 2 * rows, min(hidden, 512))),
        pltpu.SemaphoreType.DMA((weights,)),
        pltpu.SemaphoreType.DMA((weights,)),
        pltpu.SemaphoreType.DMA((40,)),
    ]
    pieces = (vmem((width, blk)), vmem((hidden, blk)))
    scratch += [pieces[0]] * 2 + [pieces[1]] * 2 if blk % 128 else [vmem((16, 128))] * 4
    return pl.pallas_call(
        functools.partial(gather_kernel, (dbits, tbits)),
        out_shape=[
            shape((tokens, D)),
            shape((tokens, D)),
            shape((D, 3 * width)),
            shape((D, hidden)),
            shape((width, D)),
            shape((hidden, D)),
            shape((tokens, hidden)),
            shape((tokens, hidden)),
            shape((tokens, width)),
            shape((tokens, 3 * width)),
            shape((small.shape[0], D), f32),
            shape((1, D), f32),
            shape((8, 3 * width), f32),
        ],
        in_specs=[vm] * 5 + [any_spec] * 4,
        out_specs=[any_spec] * 10 + [vm] * 3,
        scratch_shapes=scratch,
        compiler_params=pltpu.CompilerParams(
            vmem_limit_bytes=62 * 2**20, collective_id=0, has_side_effects=True
        ),
        cost_estimate=pl.CostEstimate(flops=2 * 10**10, bytes_accessed=10**8, transcendentals=10**7),
        name="gather",
    )(x, dy, ids, small, freqs, qkv_weight, expand_weight, dense_weight, shrink_weight)


class Reduced:
    def __init__(self, links, start, rows, send, keep, ry, rz, rl, own_out, own, stage, high_bits, blk):
        self.links, self.start, self.rows = links, start, rows
        self.send, self.keep, self.ry, self.rz, self.rl = send, keep, ry, rz, rl
        self.own_out, self.own, self.stage = own_out, own, stage
        self.high_bits, self.blk = high_bits, blk
        self.here = pl.ds(start, rows)
        self.step, self.done = 0, False

    def dot(self, dst, lhs, first, rhs, side):
        half = dst.shape[1]
        value = dot_tn(lhs[:, pl.ds(first, self.rows)], rhs[:, pl.ds(side * half, half)])
        dst[self.here, :] = value.astype(bf16)

    def away(self, lhs, first, rhs):
        self.dot(self.send, lhs, first, rhs, 1)
        self.hop = self.links.send(self.send.at[self.here, :], self.ry.at[self.here, :], "dp", ROW_BIT)

    def home(self, lhs, first, rhs):
        self.dot(self.keep, lhs, first, rhs, 0)

    def load(self, src, lanes):
        part = self.stage.at[pl.ds(0, self.rows), pl.ds(0, lanes)]
        self.links.local_wait(src.at[self.here, :], part)
        return self.stage[0 : self.rows, 0:lanes].astype(f32)

    def fold(self):
        self.hop.wait_recv()
        src = self.ry if self.step == 0 else self.rz[self.step - 1]
        lanes = src.shape[1]
        value = self.keep[self.here, 0:lanes].astype(f32) + self.load(src, lanes)
        if self.step < len(self.high_bits):
            half = lanes // 2
            self.keep[self.here, 0:lanes] = value.astype(bf16)
            part = self.keep.at[self.here, pl.ds(half, half)]
            bit = self.high_bits[len(self.high_bits) - 1 - self.step]
            self.hop = self.links.send(part, self.rz[self.step].at[self.here, :], "dp", bit)
            self.step += 1
            return
        blk = self.blk
        out = self.own.at[pl.ds(0, self.rows), :]
        self.own[0 : self.rows, :] = value[:, 0:blk]
        copy = self.links.local(out, self.own_out.at[self.here, :])
        self.last[self.here, :] = value[:, blk : 2 * blk].astype(bf16)
        self.hop = self.links.send(self.last.at[self.here, :], self.rl.at[self.here, :], "dp", SUB_BIT)
        copy.wait()
        self.done = True

    def drain(self):
        while not self.done:
            self.fold()


def reduce_kernel(
    cfg,
    x_ref, dy_own_ref, params_ref, back_sum_ref, sums_ref,
    n_hbm, dy_hbm, wq_hbm, w1_hbm, wo_hbm, w2_hbm, h_hbm, gp_hbm, o_hbm, dp_hbm,
    y_out, dx_out, own_out, rl, pg_out, ry, rc1, rx1, rs1, rc2, rx2, rs2, *rest
):
    dbits, tbits = cfg
    highs = dbits - 2
    rz, rest = rest[:highs], rest[highs:]
    (
        big, hw1, gp, w2, wo, wq, o, dp, send, keep, last, own, sx, kx, sz, stage, tmp, pg, hsum,
        send_sems, recv_sems, local_sems, *prb
    ) = rest
    order = place_order(1 << dbits)
    count = len(order)
    me = lax.axis_index("dp")
    me_t = lax.axis_index("tensor")
    sub = (me >> SUB_BIT) & 1
    rows = x_ref.shape[0]
    blk = D // count
    width, hidden = wo.shape[0], w2.shape[0]
    tokens = n_hbm.shape[0]
    links = Links(send_sems, recv_sems, local_sems)
    high_bits = list(range(2, dbits))

    get_o = links.local(o_hbm, o)
    get_dy = links.local(dy_hbm, big)
    get_h = links.local(h_hbm, hw1)
    get_w2 = links.local(w2_hbm, w2)
    get_gp = links.local(gp_hbm, gp)
    get_wo = links.local(wo_hbm, wo)
    get_dp = links.local(dp_hbm, dp)
    get_wq = links.local(wq_hbm, wq)
    greet(dbits, tbits)

    def unit(start, size):
        made = Reduced(links, start, size, send, keep, ry, rz, rl, own_out, own, stage, high_bits, blk)
        made.last = last
        return made

    chunk = min(512, hidden)
    per = hidden // chunk
    u_o = unit(0, width)
    u_2 = [unit(width + i * chunk, chunk) for i in range(per)]
    u_1 = [unit(width + hidden + i * chunk, chunk) for i in range(per)]
    u_q = [unit(width + 2 * hidden + j * width, width) for j in range(3)]

    get_o.wait()
    get_dy.wait()
    u_o.away(o, 0, big)
    get_h.wait()
    for i in range(per):
        u_2[i].away(hw1, i * chunk, big)
    u_o.home(o, 0, big)
    for i in range(per):
        u_2[i].home(hw1, i * chunk, big)

    get_w2.wait()
    get_gp.wait()
    hsum[...] = jnp.zeros_like(hsum)
    tile = 2 * rows

    def back_tile(c, carry):
        place = pl.ds(pl.multiple_of(c * tile, tile), tile)
        for t in range(0, hidden, chunk):
            lanes = slice(t, t + chunk)
            value = (dot_nt(big[place, :], w2[lanes, :]) * gp[place, lanes].astype(f32)).astype(bf16)
            gp[place, lanes] = value
            hsum[0:1, lanes] += jnp.sum(value.astype(f32), axis=0, keepdims=True)
        return carry

    lax.fori_loop(0, tokens // tile, back_tile, 0)
    u_o.fold()

    half = tokens // 2
    quarter = tokens // 4
    get_n = [links.local(n_hbm.at[pl.ds(0, half), :], big.at[pl.ds(0, half), :])]
    get_wo.wait()
    step_lanes = 512

    def branch(place, lanes):
        return dot_nn(o[place, :], wo[:, lanes]) + dot_nn(hw1[place, :], w2[:, lanes])

    def normed_back(place, lanes):
        return dot_nt(dp[place, :], wq[lanes, :]) + dot_nt(gp[place, :], hw1[lanes, :])

    def part_rows(partial, first, dst, dst_first, added):
        place = pl.ds(first, quarter)
        target = pl.ds(dst_first, quarter)

        def body(t, carry):
            lanes = pl.ds(pl.multiple_of(t * step_lanes, step_lanes), step_lanes)
            value = partial(place, lanes)
            if added is not None:
                value = value + added[:, lanes].astype(f32)
            dst[target, lanes] = value.astype(bf16)
            return carry

        lax.fori_loop(0, D // step_lanes, body, 0)

    def far_rows(partial, rc):
        hops = []
        for first in (half + quarter, half):
            part_rows(partial, first, big, first, None)
            there = pl.ds(first - half, quarter)
            hops.append(links.send(big.at[pl.ds(first, quarter), :], rc.at[there, :], "tensor", 0))
        return hops

    def near_rows(partial, rc, hops, sx, sx_first, kx, kx_first, rx):
        hops[0].wait_recv()
        links.local_wait(rc.at[pl.ds(quarter, quarter), :], stage)
        part_rows(partial, quarter, sx, sx_first, stage)
        hop = links.send(sx.at[pl.ds(sx_first, quarter), :], rx, "tensor", 1)
        hops[1].wait_recv()
        links.local_wait(rc.at[pl.ds(0, quarter), :], stage)
        part_rows(partial, 0, kx, kx_first, stage)
        return hop

    def own_rows(hop, rx, kx, kx_first, sz, rs):
        hop.wait_recv()
        links.local_wait(rx, stage)
        here, there = pl.ds(kx_first, rows), pl.ds(kx_first + rows, rows)
        sz[0:rows, :] = (kx[there, :].astype(f32) + stage[rows : 2 * rows, :].astype(f32)).astype(bf16)
        hop = links.send(sz.at[pl.ds(0, rows), :], rs, "dp", SUB_BIT)
        kx[here, :] = (kx[here, :].astype(f32) + stage[0:rows, :].astype(f32)).astype(bf16)
        return hop

    def last_rows(hop, rs, kx, kx_first):
        hop.wait_recv()
        received = stage.at[pl.ds(0, rows), :]
        links.local_wait(rs, received)
        assemble(order, me, kx.at[pl.ds(kx_first, rows), :], received, tmp)

    hops = far_rows(branch, rc1)
    x_hop1 = near_rows(branch, rc1, hops, sx, 0, kx, 0, rx1)
    get_w1 = links.local(w1_hbm, hw1)
    u_2[0].fold()
    for hop in hops:
        links.sent_done(hop)
    get_n.append(links.local(n_hbm.at[pl.ds(half, half), :], big.at[pl.ds(half, half), :]))
    u_o.drain()
    for copy in get_n:
        copy.wait()
    for i in range(per):
        u_1[i].away(gp, i * chunk, big)
    get_dp.wait()
    for j in range(3):
        u_q[j].away(dp, j * width, big)
    for i in range(1, per):
        u_2[i].fold()
    for i in range(per):
        u_1[i].home(gp, i * chunk, big)
    for j in range(3):
        u_q[j].home(dp, j * width, big)
    u_2[0].drain()

    get_wq.wait()
    get_w1.wait()
    hops = far_rows(normed_back, rc2)
    x_hop2 = near_rows(normed_back, rc2, hops, big, quarter, big, 0, rx2)

    s_hop1 = own_rows(x_hop1, rx1, kx, 0, sz, rs1)
    u_1[0].fold()
    for i in range(1, per):
        u_2[i].drain()
    last_rows(s_hop1, rs1, kx, 0)
    links.sent_done(x_hop1)
    sx[0:rows, :] = (x_ref[...].astype(f32) + tmp[...] + params_ref[5:6, :] + params_ref[6:7, :]).astype(bf16)
    y_copy = links.local(sx.at[pl.ds(0, rows), :], y_out)
    for i in range(1, per):
        u_1[i].fold()
    u_1[0].drain()
    u_q[0].fold()
    s_hop2 = own_rows(x_hop2, rx2, big, 0, w2, rs2)
    u_q[1].fold()
    u_q[2].fold()
    for i in range(1, per):
        u_1[i].drain()

    last_rows(s_hop2, rs2, big, 0)
    pg[...] = jnp.zeros_like(pg)
    strip = 64

    def norm_back(i, carry):
        place = pl.ds(pl.multiple_of(i * strip, strip), strip)
        x = x_ref[place, :].astype(f32)
        x = x - jnp.mean(x, axis=-1, keepdims=True)
        inv = lax.rsqrt(jnp.mean(x * x, axis=-1, keepdims=True) + norm_eps)
        x = x * inv
        back = tmp[place, :]
        pg[0:1, :] += jnp.sum(back * x, axis=0, keepdims=True)
        pg[1:2, :] += jnp.sum(back, axis=0, keepdims=True)
        e = back * params_ref[0:1, :]
        tmp[place, :] = dy_own_ref[place, :].astype(f32) + inv * (
            e - jnp.mean(e, axis=-1, keepdims=True) - x * jnp.mean(e * x, axis=-1, keepdims=True)
        )
        return carry

    lax.fori_loop(0, rows // strip, norm_back, 0)
    dx_copy = links.local(tmp, dx_out)

    head_start = me_t * (2 * width) + sub * width
    hidden_start = me_t * (2 * hidden) + sub * hidden
    lanes = pl.ds(pl.multiple_of(head_start, width), width)
    for j in range(3):
        pg[2 + j : 3 + j, lanes] = sums_ref[0:1, j * width : (j + 1) * width]
    pg[5:6, :] = back_sum_ref[...]
    pg[6:7, :] = back_sum_ref[...]
    pg[pl.ds(7 + hidden_start // D, 1), pl.ds(pl.multiple_of(hidden_start % D, hidden), hidden)] = hsum[0:1, :]
    base, size, slot = 0, D, 0
    for bit in reversed(range(dbits)):
        mine = (me >> bit) & 1
        if size >= 256:
            size //= 2
            there = pl.ds(pl.multiple_of(base + (1 - mine) * size, size), size)
            base = base + mine * size
        else:
            there = pl.ds(pl.multiple_of(base, size), size)
        here = pl.ds(pl.multiple_of(base, size), size)
        hop = links.send(pg.at[:, there], prb[slot], "dp", bit)
        hop.wait_recv()
        links.sent_done(hop)
        pg[:, here] += prb[slot][...]
        slot += 1
    for bit in range(tbits):
        here = pl.ds(pl.multiple_of(base, size), size)
        hop = links.send(pg.at[:, here], prb[slot], "tensor", bit)
        hop.wait_recv()
        links.sent_done(hop)
        pg[:, here] += prb[slot][...]
        slot += 1
    pg_out[...] = pg[:, pl.ds(pl.multiple_of(base, size), size)]

    for j in range(3):
        u_q[j].drain()
    for made in [u_o] + u_2 + u_1 + u_q:
        made.hop.wait_recv()
    y_copy.wait()
    dx_copy.wait()
    links.finish()


def reduce_call(dbits, tbits, x, dy, params, back_sum, sums, gathered):
    normed, back_rows, wq, w1, wo, w2, hidden_act, slope, attended, proj_back = gathered
    count = 1 << dbits
    blk = D // count
    rows = x.shape[0]
    tokens = normed.shape[0]
    width, hidden = wo.shape[0], w2.shape[0]
    total = 4 * width + 2 * hidden
    half, quarter = tokens // 2, tokens // 4
    any_spec = pl.BlockSpec(memory_space=pl.ANY)
    vm = pl.BlockSpec(memory_space=pltpu.VMEM)
    shape = lambda s, t=bf16: jax.ShapeDtypeStruct(s, t)
    vmem = lambda s, t=bf16: pltpu.VMEM(s, t)
    prb, size = [], D
    for _ in range(dbits):
        size = size // 2 if size >= 256 else size
        prb.append(vmem((16, size), f32))
    prb += [vmem((16, size), f32)] * tbits
    outs = [
        shape((rows, D)),
        shape((rows, D), f32),
        shape((total, blk), f32),
        shape((total, blk)),
        shape((16, size), f32),
        shape((total, D // 2)),
    ]
    outs += [shape((half, D)), shape((quarter, D)), shape((rows, D))] * 2
    outs += [shape((total, D >> (2 + k))) for k in range(dbits - 2)]
    scratch = [
        vmem((tokens, D)),
        vmem((tokens, hidden)),
        vmem((tokens, hidden)),
        vmem((hidden, D)),
        vmem((width, D)),
        vmem((D, 3 * width)),
        vmem((tokens, width)),
        vmem((tokens, 3 * width)),
        vmem((total, D // 2)),
        vmem((total, D // 2)),
        vmem((total, blk)),
        vmem((512, blk), f32),
        vmem((quarter, D)),
        vmem((quarter, D)),
        vmem((rows, D)),
        vmem((quarter, D)),
        vmem((rows, D), f32),
        vmem((16, D), f32),
        vmem((8, hidden), f32),
        pltpu.SemaphoreType.DMA((80,)),
        pltpu.SemaphoreType.DMA((80,)),
        pltpu.SemaphoreType.DMA((96,)),
    ] + prb
    return pl.pallas_call(
        functools.partial(reduce_kernel, (dbits, tbits)),
        out_shape=outs,
        in_specs=[vm] * 5 + [any_spec] * 10,
        out_specs=[any_spec] * 4 + [vm] + [any_spec] * (len(outs) - 5),
        scratch_shapes=scratch,
        compiler_params=pltpu.CompilerParams(
            vmem_limit_bytes=62 * 2**20, collective_id=1, has_side_effects=True
        ),
        cost_estimate=pl.CostEstimate(flops=5 * 10**10, bytes_accessed=10**8, transcendentals=10**6),
        name="reduce",
    )(x, dy, params, back_sum, sums, *gathered)


def adam_kernel(turned, split, me_ref, w_ref, m_ref, v_ref, own_ref, recv_ref, wo_ref, mo_ref, vo_ref):
    sub = (me_ref[0] >> SUB_BIT) & 1
    grad = jnp.where(pl.program_id(0) // split == sub, own_ref[...], recv_ref[...].astype(f32))
    grad = grad.T if turned else grad
    grad = grad.reshape(w_ref.shape)
    wo_ref[...], mo_ref[...], vo_ref[...] = adam_update(
        w_ref[...], m_ref[...], v_ref[...], grad, matrix_rate, weight_decay
    )


def adam_call(me, weight, first, second, own, recv, start, rows, turned):
    shape = weight.shape
    blk = own.shape[1]
    if len(shape) == 3:
        split = shape[0]
        full = pl.BlockSpec((1, blk, rows), lambda i: (i % split, 0, i // split))
    elif turned:
        split = shape[1] // (2 * rows)
        full = pl.BlockSpec((blk, rows), lambda i: (0, i))
    else:
        split = shape[0] // (2 * rows)
        full = pl.BlockSpec((rows, blk), lambda i: (i, 0))
    part = pl.BlockSpec((rows, blk), lambda i: (start // rows + i % split, 0))
    return tuple(
        pl.pallas_call(
            functools.partial(adam_kernel, turned, split),
            grid=(2 * split,),
            out_shape=[jax.ShapeDtypeStruct(shape, f32)] * 3,
            in_specs=[smem_spec()] + [full] * 3 + [part] * 2,
            out_specs=[full] * 3,
            compiler_params=vmem_params(32),
            name="adam",
        )(me, weight, first, second, own, recv)
    )


def per_device(
    inputs,
    segments,
    cotangent,
    qkv_weight,
    qkv_first,
    qkv_second,
    dense_weight,
    dense_first,
    dense_second,
    expand_weight,
    expand_first,
    expand_second,
    shrink_weight,
    shrink_first,
    shrink_second,
    small_params,
    small_first,
    small_second,
):
    dp = lax.axis_size("dp")
    tensor_count = lax.axis_size("tensor")
    dbits = dp.bit_length() - 1
    tbits = tensor_count.bit_length() - 1
    d_me = lax.axis_index("dp")
    t_me = lax.axis_index("tensor")
    sub = (d_me >> SUB_BIT) & 1
    order = place_order(dp)
    high_bits = list(range(2, dbits))
    gather_bits = high_bits + [ROW_BIT]
    rows = inputs.shape[0]
    me = jnp.stack([d_me, t_me]).astype(jnp.int32)

    small_low = jnp.pad(small_params.astype(bf16), ((0, 16 - small_params.shape[0]), (0, 0)))
    ids = jnp.broadcast_to(segments, (8, rows))
    (
        normed, back_rows, qkv_wide, expand_full, dense_full, shrink_full, hidden_act, gelu_slope, attended, proj_back,
        params, back_sum, sums,
    ) = gather_call(
        dbits, tbits, inputs, cotangent, ids, small_low, qkv_weight, expand_weight, dense_weight, shrink_weight
    )
    width, hidden = dense_full.shape[0], shrink_full.shape[0]
    gathered = (
        normed, back_rows, qkv_wide, expand_full, dense_full, shrink_full, hidden_act, gelu_slope, attended, proj_back,
    )
    output, input_grad, own, recv, small_sum, *_ = reduce_call(
        dbits, tbits, inputs, cotangent, params, back_sum, sums, gathered
    )
    blk = D // dp
    if small_sum.shape[1] > blk:
        small_sum = lax.dynamic_slice_in_dim(small_sum, (d_me % (small_sum.shape[1] // blk)) * blk, blk, 1)
    small_sum = small_sum[: small_params.shape[0]]
    dense_new = adam_call(me, dense_weight, dense_first, dense_second, own, recv, 0, width, False)
    shrink_new = adam_call(me, shrink_weight, shrink_first, shrink_second, own, recv, width, width, False)
    expand_new = adam_call(me, expand_weight, expand_first, expand_second, own, recv, width + hidden, width, True)
    qkv_new = adam_call(me, qkv_weight, qkv_first, qkv_second, own, recv, width + 2 * hidden, width, True)
    small_new = adam_update(small_params, small_first, small_second, small_sum, vector_rate, 0.0)
    return (output, input_grad) + qkv_new + dense_new + expand_new + shrink_new + small_new


def solution(mesh):
    token_spec = P(("dp", "tensor"), None)
    qkv_spec = P(None, "dp", "tensor")
    row_spec = P("tensor", "dp")
    column_spec = P("dp", "tensor")
    small_spec = P(None, "dp")
    weight_specs = (qkv_spec,) * 3 + (row_spec,) * 3 + (column_spec,) * 3 + (row_spec,) * 3 + (small_spec,) * 3
    return jax.shard_map(
        per_device,
        mesh=mesh,
        in_specs=(token_spec, P("dp", "tensor"), token_spec) + weight_specs,
        out_specs=(token_spec, token_spec) + weight_specs,
        check_vma=False,
    )
```

```python
import functools
import jax
import numpy as np
import jax.numpy as jnp
from jax import lax
from jax.experimental import pallas as pl
from jax.experimental.pallas import tpu as pltpu
from jax.sharding import PartitionSpec as P

D = 2048
HD = 64
ROT = 32
FF = 8192
STEP = 10

norm_eps = 1e-05
beta_first = 0.9
beta_second = 0.95
adam_eps = 1e-08
weight_decay = 0.1
matrix_rate = 0.05
vector_rate = 1.0
masked_score = -1e30

SUB_BIT = 1
ROW_BIT = 0

bf16 = jnp.bfloat16
f32 = jnp.float32


def exchange(values, axis, bit):
    count = lax.axis_size(axis)
    return lax.ppermute(values, axis, [(i, i ^ (1 << bit)) for i in range(count)])


def place_order(count):
    bits = count.bit_length() - 1
    order = []
    for p in range(count):
        high = (p >> 1) & ((1 << (bits - 2)) - 1)
        order.append(((p & 1) << SUB_BIT) | (high << 2) | ((p >> (bits - 1)) << ROW_BIT))
    return order


def adam_update(weight, first, second, grad, rate, decay):
    first_new = beta_first * first + (1.0 - beta_first) * grad
    second_new = beta_second * second + (1.0 - beta_second) * grad * grad
    first_hat = first_new / (1.0 - beta_first**STEP)
    second_hat = second_new / (1.0 - beta_second**STEP)
    weight_new = weight - rate * (first_hat / (jnp.sqrt(second_hat) + adam_eps) + decay * weight)
    return (weight_new, first_new, second_new)


def after(values, *others):
    return lax.optimization_barrier((values,) + others)[0]


def gelu_value(pre_values):
    return jax.nn.gelu(pre_values, approximate=True)


def vmem_params(mib):
    return pltpu.CompilerParams(vmem_limit_bytes=mib * 2**20)


def place_of(block, count):
    bits = count.bit_length() - 1
    return ((block >> SUB_BIT) & 1) | ((block >> 2) << 1) | (((block >> ROW_BIT) & 1) << (bits - 1))


def move_blocks(count, source, load, store):
    width = D // count
    if width % 128 == 0:
        for j in range(count):
            start = pl.multiple_of(source(j) * width, width)
            store(pl.ds(j * width, width), load(pl.ds(start, width)))
        return
    for unit in range(count // 2):
        parts = []
        for half in range(2):
            block = source(2 * unit + half)
            value = load(pl.ds(pl.multiple_of((block >> 1) * 128, 128), 128))
            parts.append(pltpu.roll(value, ((block & 1) ^ half) * 64, 1))
        lane = lax.broadcasted_iota(jnp.int32, parts[0].shape, 1)
        store(pl.ds(unit * 128, 128), jnp.where(lane < 64, parts[0], parts[1]))


def smem_spec():
    return pl.BlockSpec(memory_space=pltpu.SMEM)


def assemble(order, me, keep_ref, recv_ref, tmp):
    count = len(order)

    def store(lanes, value):
        tmp[:, lanes] = value

    def add(lanes, value):
        tmp[:, lanes] += value

    move_blocks(count, lambda j: place_of(j ^ me, count), lambda lanes: keep_ref[:, lanes].astype(f32), store)
    move_blocks(count, lambda j: place_of(j ^ me, count) ^ 1, lambda lanes: recv_ref[:, lanes].astype(f32), add)


def swap_rotary(values):
    lane = lax.broadcasted_iota(jnp.int32, values.shape, 1)
    half = ROT // 2
    return jnp.where(
        lane % ROT < half, pltpu.roll(values, 128 - half, 1), pltpu.roll(values, half, 1)
    )


def dot_nn(a, b):
    return lax.dot_general(a, b, (((1,), (0,)), ((), ())), preferred_element_type=f32)


def dot_nt(a, b):
    return lax.dot_general(a, b, (((1,), (1,)), ((), ())), preferred_element_type=f32)


def dot_tn(a, b):
    return lax.dot_general(a, b, (((0,), (0,)), ((), ())), preferred_element_type=f32)


def rel_index(rel, seq, tbits):
    index = seq
    for b in range(tbits):
        index = index | (((rel >> b) & 1) << (tbits - b))
    return index


def mask_bias(bias, start_row, qb, rows):
    kend = (qb + 1) * rows
    key = lax.broadcasted_iota(jnp.int32, (kend, rows), 0)
    query = lax.broadcasted_iota(jnp.int32, (kend, rows), 1) + qb * rows
    bias[:kend, :] = jnp.where((key >= start_row) & (key <= query), 0.0, masked_score)


def attend_rows(qkv, lse, bias, o, seq, qb, width, out_rows):
    rows = bias.shape[1]
    kend = (qb + 1) * rows
    place = slice(qb * rows, kend)
    lane = lax.broadcasted_iota(jnp.int32, (rows, 128), 1)
    zero = jnp.zeros((rows, 128), bf16)

    def pair_body(pair, carry):
        base = pl.multiple_of(pair * 128, 128)
        q = qkv[seq, place, pl.ds(base, 128)] * jnp.asarray(HD ** (-0.5), bf16)
        k = qkv[seq, :kend, pl.ds(base + width, 128)]
        v = qkv[seq, :kend, pl.ds(base + 2 * width, 128)]
        vt = v.T
        outs = []
        for h in range(2):
            mine = (lane < HD) if h == 0 else (lane >= HD)
            s = dot_nt(k, jnp.where(mine, q, zero)) + bias[:kend, :]
            peak = jnp.max(s, axis=0, keepdims=True)
            expo = jnp.exp(s - peak)
            total = jnp.sum(expo, axis=0, keepdims=True)
            weights = (expo * (1.0 / total)).astype(bf16)
            outs.append(dot_nn(vt[h * HD : (h + 1) * HD, :], weights))
            lse[seq, pl.ds(pair * 2 + h, 1), place] = peak + jnp.log(total)
        o[out_rows, pl.ds(base, 128)] = jnp.concatenate(outs, axis=0).T.astype(bf16)
        return carry

    lax.fori_loop(0, width // 128, pair_body, 0)


def attend_back_rows(qkv, lse, bias, do, cosb, sinb, dk, dv, dp, sums, seq, qb, width, out_rows):
    rows = bias.shape[1]
    kend = (qb + 1) * rows
    place = slice(qb * rows, kend)
    scale = HD ** (-0.5)
    lane = lax.broadcasted_iota(jnp.int32, (rows, 128), 1)
    zero = jnp.zeros((rows, 128), bf16)

    def pair_body(pair, carry):
        base = pl.multiple_of(pair * 128, 128)
        lanes = pl.ds(base, 128)
        q = qkv[seq, place, lanes]
        k = qkv[seq, :kend, pl.ds(base + width, 128)]
        v = qkv[seq, :kend, pl.ds(base + 2 * width, 128)]
        kt = k.T
        dout = do[out_rows, lanes]
        outs = []
        for h in range(2):
            mine = (lane < HD) if h == 0 else (lane >= HD)
            qm = jnp.where(mine, q, zero) * jnp.asarray(scale, bf16)
            dom = jnp.where(mine, dout, zero)
            s = dot_nt(k, qm) + bias[:kend, :]
            probs = jnp.exp(s - lse[seq, pl.ds(pair * 2 + h, 1), place])
            dprobs = dot_nt(v, dom)
            inner = jnp.sum(probs * dprobs, axis=0, keepdims=True)
            ds = (probs * (dprobs - inner)).astype(bf16)
            dv[:kend, lanes] += dot_nn(probs.astype(bf16), dom)
            dk[:kend, lanes] += dot_nn(ds, qm)
            outs.append(dot_nn(kt[h * HD : (h + 1) * HD, :], ds))
        dq = jnp.concatenate(outs, axis=0).T * scale
        dq = dq * cosb[seq, place, :] - swap_rotary(dq) * sinb[seq, place, :]
        dq = dq.astype(bf16)
        dp[out_rows, lanes] = dq
        sums[0:1, lanes] += jnp.sum(dq.astype(f32), axis=0, keepdims=True)
        return carry

    lax.fori_loop(0, width // 128, pair_body, 0)


def attend_back_keys(cosb, sinb, dk, dv, dp, sums, seq, b, width, out_rows):
    rows = out_rows.size
    place = slice(b * rows, (b + 1) * rows)
    cosine = cosb[seq, place, :]
    sine = sinb[seq, place, :]
    for j in range(width // 128):
        lanes = slice(j * 128, (j + 1) * 128)
        part = dk[place, lanes]
        part = (part * cosine - swap_rotary(part) * sine).astype(bf16)
        kl = slice(width + j * 128, width + (j + 1) * 128)
        dp[out_rows, kl] = part
        sums[0:1, kl] += jnp.sum(part.astype(f32), axis=0, keepdims=True)
        part = dv[place, lanes].astype(bf16)
        vl = slice(2 * width + j * 128, 2 * width + (j + 1) * 128)
        dp[out_rows, vl] = part
        sums[0:1, vl] += jnp.sum(part.astype(f32), axis=0, keepdims=True)


class Links:
    def __init__(self, send_sems, recv_sems, local_sems):
        self.send_sems, self.recv_sems, self.local_sems = send_sems, recv_sems, local_sems
        self.sent, self.count, self.locals = [], 0, 0

    def send(self, src, dst, axis, bit):
        partner = lax.axis_index(axis) ^ (1 << bit)
        i = self.count
        self.count += 1
        copy = pltpu.make_async_remote_copy(
            src_ref=src,
            dst_ref=dst,
            send_sem=self.send_sems.at[i],
            recv_sem=self.recv_sems.at[i],
            device_id={axis: partner},
            device_id_type=pl.DeviceIdType.MESH,
        )
        copy.start()
        self.sent.append(copy)
        return copy

    def local(self, src, dst):
        copy = pltpu.make_async_copy(src, dst, self.local_sems.at[self.locals])
        self.locals += 1
        copy.start()
        return copy

    def local_wait(self, src, dst):
        self.local(src, dst).wait()

    def sent_done(self, copy):
        copy.wait_send()
        self.sent = [other for other in self.sent if other is not copy]

    def finish(self):
        for copy in self.sent:
            copy.wait_send()


def greet(dbits, tbits):
    barrier = pltpu.get_barrier_semaphore()
    partners = [("dp", b) for b in range(dbits)] + [("tensor", b) for b in range(tbits)]
    for axis, bit in partners:
        pl.semaphore_signal(
            barrier,
            inc=1,
            device_id={axis: lax.axis_index(axis) ^ (1 << bit)},
            device_id_type=pl.DeviceIdType.MESH,
        )
    pl.semaphore_wait(barrier, len(partners))


class Gathered:
    def __init__(self, links, slot, count, bits, outgoing):
        self.links, self.slot, self.bits, self.outgoing = links, slot, bits, outgoing
        self.left = count - 1
        self.coming = {}

    def source(self, p):
        size = 1 << (p.bit_length() - 1)
        return p - size, self.bits[p.bit_length() - 1]

    def send(self, p):
        src, bit = self.source(p)
        ref = self.outgoing if p == 1 else self.slot(src)
        self.coming[p] = self.links.send(ref, self.slot(p), "dp", bit)

    def wait(self, p):
        self.coming[p].wait_recv()
        self.left -= 1


class GatheredPairs(Gathered):
    def __init__(self, links, slot, count, bits, outgoing, own, received):
        super().__init__(links, slot, count, bits, outgoing)
        self.own, self.received = own, received

    def send(self, p):
        src, bit = self.source(p)
        if p == 1:
            self.coming[p] = self.links.send(self.outgoing, self.received, "dp", bit)
        elif p % 2 == 0 and src > 0:
            self.coming[p] = self.links.send(self.slot(src // 2), self.slot(p // 2), "dp", bit)

    def wait(self, p):
        if p == 1:
            self.coming[p].wait_recv()
            both = [self.own[...].astype(f32), self.received[...].astype(f32)]
            self.slot(0)[...] = jnp.concatenate(both, axis=1).astype(bf16)
            for later in range(1, len(self.bits)):
                bit = self.bits[later]
                self.coming[1 << later] = self.links.send(self.slot(0), self.slot(1 << (later - 1)), "dp", bit)
        elif p % 2 == 0:
            self.coming[p].wait_recv()
        self.left -= 1


def cast_store(dst, src):
    dst[...] = src[...].astype(bf16)


def gather_kernel(
    cfg,
    x_ref, dy_ref, ids_ref, small_ref, freq_ref, qkv_ref, w1_ref, wo_ref, w2_ref,
    n_out, dy_out, wq_out, w1_out, wo_out, w2_out, h_out, gp_out, o_out, dp_out, params_out, dysum_out, sums_out,
    n, dyb, wq, w1, wo, w2, sq, s1, so, s2, sta, stb, stc, std, tmp, nsw, pbuf, idb, cosb, sinb, startb,
    qkvb, lse, bias, o, do, dk, dv, dp, hst, gst, send_sems, recv_sems, local_sems, *pieces
):
    dbits, tbits = cfg
    order = place_order(1 << dbits)
    count = len(order)
    me = lax.axis_index("dp")
    me_t = lax.axis_index("tensor")
    sub = (me >> SUB_BIT) & 1
    rows = x_ref.shape[0]
    width = wo.shape[0]
    hidden = w2.shape[0]
    blk = D // count
    seqs = 2
    blocks = 1 << tbits
    length = rows * blocks
    links = Links(send_sems, recv_sems, local_sems)
    bits = [SUB_BIT] + list(range(2, dbits)) + [ROW_BIT]

    own_q = pl.ds(pl.multiple_of(sub * width, width), width)
    other_q = pl.ds(pl.multiple_of((1 - sub) * width, width), width)
    own_h = pl.ds(pl.multiple_of(sub * hidden, hidden), hidden)
    other_h = pl.ds(pl.multiple_of((1 - sub) * hidden, hidden), hidden)
    loads = {"q": [], "1": [], "2": [], "o": []}
    for j in range(3):
        lanes = pl.ds(j * width, width)
        loads["q"].append(links.local(qkv_ref.at[j, :, other_q], std.at[:, lanes]))
        loads["q"].append(links.local(qkv_ref.at[j, :, own_q], stc.at[:, lanes]))
    loads["2"].append(links.local(w2_ref.at[other_h, :], stb))
    loads["2"].append(links.local(w2_ref.at[own_h, :], sta))

    def row_gather(ref, outgoing):
        return Gathered(links, lambda p: ref.at[pl.ds(p * blk, blk), :], count, bits, outgoing)

    def column_gather(ref, outgoing, own, received):
        unit = max(blk, 128)
        slot = lambda p: ref.at[:, pl.ds(p * unit, unit)]
        if unit == blk:
            return Gathered(links, slot, count, bits, outgoing), slot(0)
        return GatheredPairs(links, slot, count, bits, outgoing, own, received), own

    gathers = {"q": row_gather(wq, sq), "1": row_gather(w1, s1)}
    gathers["o"], wo_own = column_gather(wo, so, *pieces[0:2])
    gathers["2"], w2_own = column_gather(w2, s2, *pieces[2:4])
    outs = {"q": (wq, wq_out), "1": (w1, w1_out), "o": (wo, wo_out), "2": (w2, w2_out), "n": (n, n_out), "d": (dyb, dy_out)}
    token_bufs = {"n": n, "d": dyb}
    token_left = {"n": 2 * blocks - 1, "d": 2 * blocks - 1}
    coming, stores, kept, attended, begun = {}, [], {}, set(), set()

    def tok(ref, i):
        return ref.at[pl.ds(i * rows, rows), :]

    def send(kind, i):
        if kind in gathers:
            gathers[kind].send(i)
        elif kind in token_bufs:
            ref = token_bufs[kind]
            if i == 1:
                coming[kind, i] = links.send(nsw, tok(ref, 1), "dp", SUB_BIT)
            else:
                step = i.bit_length() - 1
                coming[kind, i] = links.send(tok(ref, i - (1 << step)), tok(ref, i), "tensor", tbits - step)
        else:
            buf = pbuf if kind == "P" else idb
            axis, bit = ("dp", bits[i - 1]) if kind == "P" or i == 1 else ("tensor", tbits + 1 - i)
            size = 1 << (i - 1)
            coming[kind, i] = links.send(buf.at[pl.ds(0, size)], buf.at[pl.ds(size, size)], axis, bit)

    def wait(kind, i):
        if kind in gathers:
            gathers[kind].wait(i)
            complete = gathers[kind].left == 0
        else:
            coming[kind, i].wait_recv()
            complete = False
            if kind in token_bufs:
                token_left[kind] -= 1
                complete = token_left[kind] == 0
        if complete:
            stores.append(links.local(*outs[kind]))

    def arrived(name):
        for copy in loads[name]:
            copy.wait()

    def cast_q():
        arrived("q")
        sq[...] = std[:, 0 : 3 * width].astype(bf16)
        wq[0:blk, :] = stc[:, 0 : 3 * width].astype(bf16)
        loads["1"].append(links.local(w1_ref.at[:, other_h], std))
        loads["1"].append(links.local(w1_ref.at[:, own_h], stc))

    def cast_1():
        arrived("1")
        s1[...] = std[...].astype(bf16)
        w1[0:blk, :] = stc[...].astype(bf16)

    def cast_2():
        arrived("2")
        s2[...] = stb[...].astype(bf16)
        w2_own[...] = sta[...].astype(bf16)
        loads["o"].append(links.local(wo_ref.at[other_q, :], stb.at[pl.ds(0, width), :]))
        loads["o"].append(links.local(wo_ref.at[own_q, :], sta.at[pl.ds(0, width), :]))

    def cast_o():
        arrived("o")
        so[...] = stb[0:width, :].astype(bf16)
        wo_own[...] = sta[0:width, :].astype(bf16)

    def statistics():
        x = x_ref[...].astype(f32)
        x = x - jnp.mean(x, axis=-1, keepdims=True)
        inv = lax.rsqrt(jnp.mean(x * x, axis=-1, keepdims=True) + norm_eps)
        tmp[...] = x * inv

    def store_to(ref):
        def store(lanes, value):
            ref[0:rows, lanes] = value.astype(bf16)

        return store

    load_tmp = lambda lanes: tmp[:, lanes]
    load_dy = lambda lanes: dy_ref[:, lanes].astype(f32)

    def norm():
        per = max(1, 128 // blk)
        for a in range(0, count, per):
            part = [pbuf[place_of((a + k) ^ me, count)].astype(f32) for k in range(per)]
            lanes = pl.ds(a * blk, per * blk)
            params_out[:, lanes] = part[0] if per == 1 else jnp.concatenate(part, axis=1)
        tmp[...] = tmp[...] * params_out[0:1, :] + params_out[1:2, :]
        move_blocks(count, lambda j: me ^ order[j ^ 1], load_tmp, store_to(nsw))
        move_blocks(count, lambda j: me ^ order[j], load_tmp, store_to(n))

    def back_own():
        move_blocks(count, lambda j: me ^ order[j], load_dy, store_to(dyb))
        dysum_out[...] = jnp.sum(dy_ref[...].astype(f32), axis=0, keepdims=True)

    def back_swapped():
        links.sent_done(coming["n", 1])
        move_blocks(count, lambda j: me ^ order[j ^ 1], load_dy, store_to(nsw))

    def tables():
        for seq in range(seqs):
            row = jnp.concatenate(
                [idb[rel_index(me_t ^ b, seq, tbits)][0:1, :] for b in range(blocks)], axis=1
            ).astype(f32)
            first = jnp.sum(jnp.where(row < 1.0, 1.0, 0.0), axis=1, keepdims=True)
            second = jnp.sum(jnp.where(row < 2.0, 1.0, 0.0), axis=1, keepdims=True)
            begin = jnp.where(row < 1.0, 0.0, jnp.where(row < 2.0, first, second))
            place = lax.broadcasted_iota(jnp.int32, (1, length), 1).astype(f32)
            startb[seq, 0:1, :] = begin.astype(jnp.int32)
            angle = freq_ref[:, 0:1] * (place - begin)
            cosine, sine = jnp.cos(angle), jnp.sin(angle)
            rest = (HD - ROT, length)
            cosine = jnp.concatenate([cosine, cosine, jnp.ones(rest, f32)], axis=0)
            sine = jnp.concatenate([-sine, sine, jnp.zeros(rest, f32)], axis=0)
            cosb[seq] = jnp.concatenate([cosine, cosine], axis=0).T
            sinb[seq] = jnp.concatenate([sine, sine], axis=0).T

    head_start = me_t * (2 * width) + sub * width
    hidden_start = me_t * (2 * hidden) + sub * hidden
    pairs = width // 128

    def two_blocks(c):
        return pl.ds(2 * c * rows, 2 * rows)

    def project(c):
        lanes = pl.ds(pl.multiple_of(head_start, width), width)
        qkv_bias = [params_out[2 + j : 3 + j, lanes] for j in range(3)]
        rel = sum(((c >> (tbits - 1 - b)) & 1) << b for b in range(tbits))
        block = me_t ^ rel
        place = pl.ds(pl.multiple_of(block * rows, rows), rows)
        part = dot_nn(n[two_blocks(c), :], wq[...])
        for seq in range(seqs):
            seq_rows = slice(seq * rows, (seq + 1) * rows)
            cosine, sine = cosb[seq, place, :], sinb[seq, place, :]
            for j in range(3 * pairs):
                kind, pair = j // pairs, j % pairs
                value = part[seq_rows, j * 128 : (j + 1) * 128] + qkv_bias[kind][:, pair * 128 : (pair + 1) * 128]
                if kind < 2:
                    value = value * cosine + swap_rotary(value) * sine
                qkvb[seq, place, j * 128 : (j + 1) * 128] = value.astype(bf16)

    def seq_rows_of(seq, b):
        return pl.ds(pl.multiple_of(rel_index(me_t ^ b, seq, tbits) * rows, rows), rows)

    def attend(seq, qb):
        mask_bias(bias, startb[seq, 0:1, qb * rows : (qb + 1) * rows], qb, rows)
        attend_rows(qkvb, lse, bias, o, seq, qb, width, seq_rows_of(seq, qb))
        attended.add((seq, qb))
        if len(attended) == seqs * blocks:
            stores.append(links.local(o, o_out))

    def attend_back(seq, qb):
        if seq not in begun:
            begun.add(seq)
            dk[...] = jnp.zeros_like(dk)
            dv[...] = jnp.zeros_like(dv)
        mask_bias(bias, startb[seq, 0:1, qb * rows : (qb + 1) * rows], qb, rows)
        attend_back_rows(
            qkvb, lse, bias, do, cosb, sinb, dk, dv, dp, sums_out, seq, qb, width, seq_rows_of(seq, qb)
        )

    def attend_keys(seq):
        for b in range(blocks):
            attend_back_keys(cosb, sinb, dk, dv, dp, sums_out, seq, b, width, seq_rows_of(seq, b))

    tile = hst.shape[2]

    def hide(c):
        row = 7 + hidden_start // D
        hidden_bias = params_out[pl.ds(row, 1), pl.ds(pl.multiple_of(hidden_start % D, hidden), hidden)]
        for t in range(hidden // tile):
            lanes = pl.ds(t * tile, tile)
            slot = t % 2
            for copy in kept.pop(slot, ()):
                copy.wait()
            v = dot_nn(n[two_blocks(c), :], w1[:, lanes]) + hidden_bias[:, t * tile : (t + 1) * tile]
            root = 0.7978845608028654
            square = v * v
            th = jnp.tanh(root * (v + 0.044715 * v * square))
            hst[slot] = (0.5 * v * (1.0 + th)).astype(bf16)
            gst[slot] = (
                0.5 * (1.0 + th) + 0.5 * v * (1.0 - th * th) * (root * (1.0 + (3 * 0.044715) * square))
            ).astype(bf16)
            kept[slot] = (
                links.local(hst.at[slot], h_out.at[two_blocks(c), lanes]),
                links.local(gst.at[slot], gp_out.at[two_blocks(c), lanes]),
            )

    def output_back(c):
        do[two_blocks(c), :] = dot_nt(dyb[two_blocks(c), :], wo[...]).astype(bf16)

    def end():
        stores.append(links.local(dp, dp_out))
        for copies in kept.values():
            stores.extend(copies)
        for copy in stores:
            copy.wait()
        links.finish()

    pbuf[0] = small_ref[...]
    idb[0] = ids_ref[...]
    sums_out[...] = jnp.zeros_like(sums_out)
    greet(dbits, tbits)
    steps = {
        "castq": cast_q, "cast1": cast_1, "cast2": cast_2, "casto": cast_o, "stat": statistics, "ln": norm,
        "dyr": back_own, "dys": back_swapped, "table": tables, "end": end,
    }
    indexed = {"Q": project, "A": attend, "B": attend_back, "K": attend_keys, "H": hide, "D": output_back}
    for name in gather_schedule(count, blocks):
        if name in steps:
            steps[name]()
        elif name[0] == "S":
            send(name[1], int(name[2:]))
        elif name[0] == "W":
            wait(name[1], int(name[2:]))
        else:
            indexed[name[0]](*[int(i) for i in name[1:]])


GATHER_ORDER = [
    6, 0, 14, 29, 1, 2, 30, 7, 75, 90, 91, 93, 8, 12, 44, 3, 4, 5, 9, 31, 13, 78, 32, 34, 15, 47, 94, 33, 45,
    16, 49, 63, 35, 36, 21, 40, 48, 10, 18, 11, 22, 101, 37, 38, 86, 19, 20, 17, 46, 61, 42, 25, 27, 41, 62,
    43, 50, 23, 51, 39, 57, 53, 52, 54, 26, 105, 92, 24, 76, 107, 28, 108, 96, 106, 112, 95, 116, 55, 56,
    111, 113, 77, 110, 67, 64, 58, 97, 65, 59, 98, 114, 115, 66, 60, 119, 99, 100, 68, 117, 103, 120, 102,
    73, 79, 80, 81, 109, 104, 72, 69, 82, 121, 70, 118, 71, 123, 74, 122, 83, 124, 126, 128, 127, 125, 129,
    84, 88, 85, 131, 130, 132, 133, 134, 87, 89, 135,
]


def gather_schedule(count, blocks):
    names = []

    def take(kind, places, first):
        def push(p):
            size = first
            while size < places:
                if p < size:
                    names.append("S%s%d" % (kind, p + size))
                size *= 2

        names.append("S%s1" % kind)
        push(0)
        for p in range(1, places):
            names.append("W%s%d" % (kind, p))
            push(p)

    for i in range(1, count.bit_length()):
        names.extend(["SP%d" % i, "WP%d" % i])
    for i in range(1, blocks.bit_length() + 1):
        names.extend(["SI%d" % i, "WI%d" % i])
    names.extend(["stat", "ln", "castq"])
    take("n", 2 * blocks, 2)
    take("q", count, 2)
    names.extend(["table", "cast1", "dyr", "dys"])
    take("1", count, 2)
    take("d", 2 * blocks, 2)
    names.append("cast2")
    take("2", count, 2)
    names.append("casto")
    take("o", count, 2)
    names.extend("Q%d" % c for c in range(blocks))
    names.extend("A%d%d" % (s, b) for s in range(2) for b in range(blocks))
    names.extend("H%d" % c for c in range(blocks))
    names.extend("D%d" % c for c in range(blocks))
    for s in range(2):
        names.extend("B%d%d" % (s, b) for b in range(blocks))
        names.append("K%d" % s)
    names.append("end")
    if (count, blocks) == (8, 4):
        return [names[i] for i in GATHER_ORDER]
    return names


def gather_call(dbits, tbits, x, dy, ids, small, qkv_weight, expand_weight, dense_weight, shrink_weight):
    count = 1 << dbits
    blk = D // count
    rows = x.shape[0]
    width = qkv_weight.shape[2] // 2
    hidden = expand_weight.shape[1] // 2
    tokens = rows * (2 << tbits)
    length = rows << tbits
    heads = width // HD
    half = ROT // 2
    powers = (10000.0 ** (-np.arange(half) / half)).astype(np.float32)
    freqs = jnp.asarray(np.repeat(powers[:, None], 128, axis=1))
    any_spec = pl.BlockSpec(memory_space=pl.ANY)
    vm = pl.BlockSpec(memory_space=pltpu.VMEM)
    shape = lambda s, t=bf16: jax.ShapeDtypeStruct(s, t)
    vmem = lambda s, t=bf16: pltpu.VMEM(s, t)
    weights = 4 * (2 * count - 1) + 2 * 32 + 16
    scratch = [
        vmem((tokens, D)),
        vmem((tokens, D)),
        vmem((D, 3 * width)),
        vmem((D, hidden)),
        vmem((width, D)),
        vmem((hidden, D)),
        vmem((blk, 3 * width)),
        vmem((blk, hidden)),
        vmem((width, blk)),
        vmem((hidden, blk)),
        vmem((hidden, blk), f32),
        vmem((hidden, blk), f32),
        vmem((blk, hidden), f32),
        vmem((blk, hidden), f32),
        vmem((rows, D), f32),
        vmem((rows, D)),
        vmem((count, small.shape[0], blk)),
        vmem((2 << tbits, 8, rows), jnp.int32),
        vmem((2, length, 128), f32),
        vmem((2, length, 128), f32),
        vmem((2, 8, length), jnp.int32),
        vmem((2, length, 3 * width)),
        vmem((2, heads, length), f32),
        vmem((length, rows), f32),
        vmem((tokens, width)),
        vmem((tokens, width)),
        vmem((length, width), f32),
        vmem((length, width), f32),
        vmem((tokens, 3 * width)),
        vmem((2, 2 * rows, min(hidden, 512))),
        vmem((2, 2 * rows, min(hidden, 512))),
        pltpu.SemaphoreType.DMA((weights,)),
        pltpu.SemaphoreType.DMA((weights,)),
        pltpu.SemaphoreType.DMA((48,)),
    ]
    pieces = (vmem((width, blk)), vmem((hidden, blk)))
    scratch += [pieces[0]] * 2 + [pieces[1]] * 2 if blk % 128 else [vmem((16, 128))] * 4
    return pl.pallas_call(
        functools.partial(gather_kernel, (dbits, tbits)),
        out_shape=[
            shape((tokens, D)),
            shape((tokens, D)),
            shape((D, 3 * width)),
            shape((D, hidden)),
            shape((width, D)),
            shape((hidden, D)),
            shape((tokens, hidden)),
            shape((tokens, hidden)),
            shape((tokens, width)),
            shape((tokens, 3 * width)),
            shape((small.shape[0], D), f32),
            shape((1, D), f32),
            shape((8, 3 * width), f32),
        ],
        in_specs=[vm] * 5 + [any_spec] * 4,
        out_specs=[any_spec] * 10 + [vm] * 3,
        scratch_shapes=scratch,
        compiler_params=pltpu.CompilerParams(
            vmem_limit_bytes=62 * 2**20, collective_id=0, has_side_effects=True
        ),
        cost_estimate=pl.CostEstimate(flops=2 * 10**10, bytes_accessed=10**8, transcendentals=10**7),
        name="gather",
    )(x, dy, ids, small, freqs, qkv_weight, expand_weight, dense_weight, shrink_weight)


class Unit:
    def __init__(self, start, rows, lhs, first, rhs, send_start, frees):
        self.here, self.rows = pl.ds(start, rows), rows
        self.lhs, self.first, self.rhs = lhs, first, rhs
        self.out = pl.ds(send_start, rows)
        self.frees, self.hop, self.load, self.slot = frees, None, None, None


class TokenSum:
    def __init__(self, partial, far, near, keep, rc, rx, rs):
        self.partial, self.far, self.near, self.keep = partial, far, near, keep
        self.rc, self.rx, self.rs = rc, rx, rs
        self.hops = {}


def reduce_kernel(
    cfg,
    x_ref, dy_own_ref, params_ref, back_sum_ref, sums_ref,
    n_hbm, dy_hbm, wq_hbm, w1_hbm, wo_hbm, w2_hbm, h_hbm, gp_hbm, o_hbm, dp_hbm,
    y_out, dx_out, own_out, rl, pg_out, ry, rc1, rx1, rs1, rc2, rx2, rs2, *rest
):
    dbits, tbits = cfg
    highs = dbits - 2
    rz, rest = rest[:highs], rest[highs:]
    (
        big, hw1, gp, w2, wo, wq, o, dp, outgoing, keep, own, came, sx, kx, sz, sc, stage, tmp, pg, hsum,
        send_sems, recv_sems, local_sems, *rest
    ) = rest
    prb, last = rest[: dbits + tbits], rest[dbits + tbits :]
    order = place_order(1 << dbits)
    count = len(order)
    me = lax.axis_index("dp")
    me_t = lax.axis_index("tensor")
    sub = (me >> SUB_BIT) & 1
    rows = x_ref.shape[0]
    blk = D // count
    width, hidden = wo.shape[0], w2.shape[0]
    tokens = n_hbm.shape[0]
    links = Links(send_sems, recv_sems, local_sems)
    high_bits = list(range(2, dbits))
    side = D // 2
    half, quarter = tokens // 2, tokens // 4
    step_lanes = 512

    pending = {}

    def fetch(name, src, dst):
        pending.setdefault(name, []).append(links.local(src, dst))

    def need(*names):
        for name in names:
            for copy in pending.pop(name, ()):
                copy.wait()

    fetch("o", o_hbm, o)
    fetch("dy", dy_hbm, big)
    fetch("h", h_hbm, hw1)

    def load_more():
        fetch("w2", w2_hbm, w2)
        fetch("gp", gp_hbm, gp)
        fetch("dp", dp_hbm, dp)
        fetch("wq", wq_hbm, wq)
        fetch("wo", wo_hbm, wo)

    def load_n():
        for i in range(2):
            links.sent_done(sums["dn"].hops["c", i])
        for i in range(2):
            part = pl.ds(i * half, half)
            fetch("n", n_hbm.at[part, :], big.at[part, :])

    units = {"o": Unit(2 * hidden + 3 * width, width, o, 0, "dy", hidden + 3 * width, None)}
    per = hidden // width
    for i in range(per):
        at = i * width
        units["a%d" % i] = Unit(at, width, hw1, at, "dy", at, None)
        units["c%d" % i] = Unit(at + hidden, width, gp, at, "n", at, "a%d" % i)
    for j in range(3):
        at = hidden + j * width
        units["q%d" % j] = Unit(at + hidden, width, dp, j * width, "n", at, None)

    def product(unit, part):
        need(unit.rhs, *(["dp"] if unit.lhs is dp else ["h"] if unit.lhs is hw1 else ["o"]))
        lhs = unit.lhs[:, pl.ds(unit.first, unit.rows)]
        return dot_tn(lhs, big[:, pl.ds(part * side, side)]).astype(bf16)

    def away(unit):
        if unit.frees:
            links.sent_done(units[unit.frees].first_hop)
        outgoing[unit.out, :] = product(unit, 1)

    def home(unit):
        keep[unit.here, :] = product(unit, 0)

    def send_y(unit):
        unit.hop = links.send(outgoing.at[unit.out, :], ry.at[unit.here, :], "dp", ROW_BIT)
        unit.first_hop = unit.hop

    free = list(range(came.shape[0]))

    def load_received(unit, src):
        if free:
            unit.slot = free.pop()
            part = came.at[unit.slot, :, pl.ds(0, src.shape[1])]
            unit.load = links.local(src.at[unit.here, :], part)

    def add_received(unit, src):
        lanes = src.shape[1]
        value = keep[unit.here, 0:lanes].astype(f32)
        if unit.load is None:
            part = stage.at[pl.ds(0, unit.rows), pl.ds(0, lanes)]
            links.local_wait(src.at[unit.here, :], part)
            return value + part[...].astype(f32)
        unit.load.wait()
        unit.load = None
        free.append(unit.slot)
        return value + came[unit.slot, :, 0:lanes].astype(f32)

    def fold_first(unit):
        keep[unit.here, :] = add_received(unit, ry).astype(bf16)

    def send_high(unit, k=0):
        lanes = side >> (k + 1)
        part = keep.at[unit.here, pl.ds(lanes, lanes)]
        unit.hop = links.send(part, rz[k].at[unit.here, :], "dp", high_bits[highs - 1 - k])

    slots = []

    def fold_last(unit):
        for k in range(highs - 1):
            keep[unit.here, 0 : side >> (k + 1)] = add_received(unit, rz[k]).astype(bf16)
            send_high(unit, k + 1)
            unit.hop.wait_recv()
        value = add_received(unit, rz[highs - 1])
        slot = len(slots) % own.shape[0]
        if len(slots) >= own.shape[0]:
            slots[-own.shape[0]].wait()
        own[slot] = value[:, 0:blk]
        slots.append(links.local(own.at[slot], own_out.at[unit.here, :]))
        if last:
            last[0][unit.here, :] = value[:, blk : 2 * blk].astype(bf16)
        else:
            keep[unit.here, blk : 2 * blk] = value[:, blk : 2 * blk].astype(bf16)

    def send_sub(unit):
        part = last[0].at[unit.here, :] if last else keep.at[unit.here, pl.ds(blk, blk)]
        unit.hop = links.send(part, rl.at[unit.here, :], "dp", SUB_BIT)

    hsum[...] = jnp.zeros_like(hsum)

    def hidden_back(c):
        need("dy", "w2", "gp")
        place = pl.ds(c * quarter, quarter)
        for t in range(0, hidden, 512):
            lanes = slice(t, t + 512)
            value = (dot_nt(big[place, :], w2[lanes, :]) * gp[place, lanes].astype(f32)).astype(bf16)
            gp[place, lanes] = value
            hsum[0:1, lanes] += jnp.sum(value.astype(f32), axis=0, keepdims=True)

    def branch(place, lanes):
        return dot_nn(o[place, :], wo[:, lanes]) + dot_nn(hw1[place, :], w2[:, lanes])

    def normed_back(place, lanes):
        return dot_nt(dp[place, :], wq[lanes, :]) + dot_nt(gp[place, :], hw1[lanes, :])

    def part_rows(partial, first, dst, added):
        place = pl.ds(first, quarter)

        def body(t, carry):
            lanes = pl.ds(pl.multiple_of(t * step_lanes, step_lanes), step_lanes)
            value = partial(place, lanes)
            if added is not None:
                value = value + added[:, lanes].astype(f32)
            dst[:, lanes] = value.astype(bf16)
            return carry

        lax.fori_loop(0, D // step_lanes, body, 0)

    big_rows = lambda first: big.at[pl.ds(first, quarter), :]
    sums = {
        "dn": TokenSum(normed_back, (big_rows(half), big_rows(half + quarter)), sx, kx, rc1, rx1, rs1),
        "br": TokenSum(branch, (sc, sc), sc, sx, rc2, rx2, rs2),
    }

    def far_rows(t, i):
        need("wo", "w2", "o", "h") if t is sums["br"] else need("dp", "wq", "w1")
        if t is sums["br"] and i == 0:
            links.sent_done(t.hops["c", 1])
        part_rows(t.partial, half + i * quarter, t.far[i], None)

    def send_core(t, i):
        there = pl.ds(i * quarter, quarter)
        t.hops["c", i] = links.send(t.far[i], t.rc.at[there, :], "tensor", 0)

    def near_rows(t):
        if t is sums["br"]:
            links.sent_done(t.hops["c", 0])
        links.local_wait(t.rc.at[pl.ds(quarter, quarter), :], stage)
        part_rows(t.partial, quarter, t.near, stage)

    def send_x(t, i):
        part = pl.ds(i * rows, rows)
        t.hops["x", i] = links.send(t.near.at[part, :], t.rx.at[part, :], "tensor", 1)

    def keep_rows(t):
        if t is sums["br"]:
            for i in range(2):
                links.sent_done(sums["dn"].hops["x", i])
        links.local_wait(t.rc.at[pl.ds(0, quarter), :], stage)
        part_rows(t.partial, 0, t.keep, stage)

    def partner_rows(t):
        if t is sums["br"]:
            links.sent_done(sums["dn"].hops["s"])
        links.local_wait(t.rx.at[pl.ds(rows, rows), :], stage.at[pl.ds(0, rows), :])
        sz[...] = (t.keep[rows : 2 * rows, :].astype(f32) + stage[0:rows, :].astype(f32)).astype(bf16)

    def send_last(t):
        t.hops["s"] = links.send(sz, t.rs, "dp", SUB_BIT)

    def own_rows(t):
        links.local_wait(t.rx.at[pl.ds(0, rows), :], stage.at[pl.ds(0, rows), :])
        t.keep[0:rows, :] = (t.keep[0:rows, :].astype(f32) + stage[0:rows, :].astype(f32)).astype(bf16)
        received = stage.at[pl.ds(rows, rows), :]
        links.local_wait(t.rs, received)
        assemble(order, me, t.keep.at[pl.ds(0, rows), :], received, tmp)

    def norm_back():
        own_rows(sums["dn"])
        pg[...] = jnp.zeros_like(pg)
        strip = 64

        def body(i, carry):
            place = pl.ds(pl.multiple_of(i * strip, strip), strip)
            x = x_ref[place, :].astype(f32)
            x = x - jnp.mean(x, axis=-1, keepdims=True)
            inv = lax.rsqrt(jnp.mean(x * x, axis=-1, keepdims=True) + norm_eps)
            x = x * inv
            back = tmp[place, :]
            pg[0:1, :] += jnp.sum(back * x, axis=0, keepdims=True)
            pg[1:2, :] += jnp.sum(back, axis=0, keepdims=True)
            e = back * params_ref[0:1, :]
            tmp[place, :] = dy_own_ref[place, :].astype(f32) + inv * (
                e - jnp.mean(e, axis=-1, keepdims=True) - x * jnp.mean(e * x, axis=-1, keepdims=True)
            )
            return carry

        lax.fori_loop(0, rows // strip, body, 0)
        fetch("dx", tmp, dx_out)
        head_start = me_t * (2 * width) + sub * width
        hidden_start = me_t * (2 * hidden) + sub * hidden
        lanes = pl.ds(pl.multiple_of(head_start, width), width)
        for j in range(3):
            pg[2 + j : 3 + j, lanes] = sums_ref[0:1, j * width : (j + 1) * width]
        pg[5:6, :] = back_sum_ref[...]
        pg[6:7, :] = back_sum_ref[...]
        pg[pl.ds(7 + hidden_start // D, 1), pl.ds(pl.multiple_of(hidden_start % D, hidden), hidden)] = hsum[0:1, :]

    hops, base, size = [], 0, D
    for bit in reversed(range(dbits)):
        mine = (me >> bit) & 1
        if size >= 256:
            size //= 2
            there = (base + (1 - mine) * size, size)
            base = base + mine * size
        else:
            there = (base, size)
        hops.append(("dp", bit, there, (base, size)))
    for bit in range(tbits):
        hops.append(("tensor", bit, (base, size), (base, size)))
    lanes_of = lambda at: pl.ds(pl.multiple_of(at[0], at[1]), at[1])
    small_hops = {}

    def send_small(i):
        axis, bit, there, _ = hops[i]
        small_hops[i] = links.send(pg.at[:, lanes_of(there)], prb[i], axis, bit)

    def add_small(i):
        links.sent_done(small_hops[i])
        pg[:, lanes_of(hops[i][3])] += prb[i][...]

    def block_output():
        need("dx")
        own_rows(sums["br"])
        kx[0:rows, :] = (x_ref[...].astype(f32) + tmp[...] + params_ref[5:6, :] + params_ref[6:7, :]).astype(bf16)
        fetch("y", kx.at[pl.ds(0, rows), :], y_out)

    def end():
        pg_out[...] = pg[:, lanes_of((base, size))]
        need("y")
        for copy in slots[-own.shape[0] :]:
            copy.wait()
        links.finish()

    greet(dbits, tbits)
    plain = {
        "load0": lambda: need("o", "dy", "h"),
        "load1": load_more,
        "w1load": lambda: fetch("w1", w1_hbm, hw1),
        "hload": lambda: fetch("h", h_hbm, hw1),
        "nload": load_n,
        "dnout": norm_back,
        "brout": block_output,
        "end": end,
    }
    of_unit = {"away": away, "home": home, "f1": fold_first, "f2": fold_last}
    send_unit = {"y": send_y, "h": send_high, "z": send_sub}
    of_sum = {
        "31": lambda t: far_rows(t, 1), "30": lambda t: far_rows(t, 0), "01": near_rows, "00": keep_rows,
        "own": partner_rows,
    }
    send_sum = {
        "c1": lambda t: send_core(t, 1), "c0": lambda t: send_core(t, 0), "b": lambda t: send_x(t, 1),
        "a": lambda t: send_x(t, 0), "s": send_last,
    }
    wait_sum = {"c1": ("c", 1), "c0": ("c", 0), "b": ("x", 1), "a": ("x", 0), "s": "s"}
    for name in reduce_schedule(count, units, len(hops)):
        kind, _, rest = name.partition("_")
        if name in plain:
            plain[name]()
        elif kind in of_unit:
            of_unit[kind](units[rest])
        elif name[:2] == "dh":
            hidden_back(int(name[2:]))
        elif name[0] == "g":
            add_small(int(name[1:]))
        elif name[:2] == "SG":
            send_small(int(name[2:]))
        elif name[:2] == "WG":
            small_hops[int(name[2:])].wait_recv()
        elif name[0] == "S" and name[1:3] in sums:
            send_sum[name[3:]](sums[name[1:3]])
        elif name[0] == "W" and name[1:3] in sums:
            sums[name[1:3]].hops[wait_sum[name[3:]]].wait_recv()
        elif name[0] == "S":
            send_unit[name[1]](units[name[2:]])
        elif name[0] == "W":
            unit = units[name[2:]]
            unit.hop.wait_recv()
            if name[1] in "yh":
                load_received(unit, ry if name[1] == "y" else rz[0])
        else:
            of_sum[name[2:]](sums[name[:2]])


REDUCE_ORDER = [
    0, 11, 12, 8, 9, 5, 7, 14, 4, 1, 20, 18, 2, 49, 13, 50, 51, 15, 19, 6, 17, 10, 3, 46, 16, 47, 48, 21, 22,
    23, 64, 24, 52, 65, 66, 53, 54, 25, 26, 28, 29, 27, 61, 43, 39, 44, 70, 45, 85, 86, 31, 40, 67, 71, 38,
    62, 30, 63, 41, 42, 68, 69, 91, 92, 82, 87, 32, 33, 34, 167, 122, 88, 123, 83, 124, 58, 95, 93, 94, 59,
    60, 78, 79, 76, 80, 84, 96, 97, 98, 119, 89, 120, 107, 121, 72, 143, 75, 90, 55, 56, 81, 144, 145, 108,
    57, 109, 99, 36, 77, 100, 169, 125, 126, 127, 73, 35, 140, 74, 116, 101, 102, 103, 37, 171, 149, 113,
    110, 128, 117, 118, 150, 174, 165, 151, 146, 152, 129, 114, 111, 112, 137, 130, 115, 131, 147, 132, 133,
    153, 138, 148, 154, 139, 155, 164, 166, 156, 105, 157, 158, 159, 160, 141, 142, 134, 161, 104, 135, 136,
    106, 172, 162, 163, 175, 170, 173, 168, 176,
]


def reduce_schedule(count, units, hops):
    names = ["load0", "load1"]
    early = [u for u in units if u[0] in "oa"]
    late = [u for u in units if u[0] in "cq"]

    def start(group):
        for u in group:
            names.extend(["away_" + u, "Sy" + u, "home_" + u])

    def fold(group):
        for u in group:
            names.extend(["Wy" + u, "f1_" + u, "Sh" + u])
        for u in group:
            names.extend(["Wh" + u, "f2_" + u, "Sz" + u])

    def total(k):
        for part in ("31", "Sc1", "30", "Sc0", "Wc1", "Wc0", "01", "Sb", "Sa", "00", "Wb", "own", "Ss", "Ws", "Wa", "out"):
            names.append(part[0] + k + part[1:] if part[0] in "SW" else k + part)

    start(early)
    names.extend("dh%d" % c for c in range(4))
    names.append("w1load")
    total("dn")
    names.extend(["hload", "nload"])
    fold(early)
    start(late)
    total("br")
    fold(late)
    for i in range(hops):
        names.extend(["SG%d" % i, "WG%d" % i, "g%d" % i])
    names.extend("Wz" + u for u in units)
    names.append("end")
    if count == 8 and len(units) == 12 and hops == 5:
        return [names[i] for i in REDUCE_ORDER]
    return names


def reduce_call(dbits, tbits, x, dy, params, back_sum, sums, gathered):
    normed, back_rows, wq, w1, wo, w2, hidden_act, slope, attended, proj_back = gathered
    count = 1 << dbits
    blk = D // count
    rows = x.shape[0]
    tokens = normed.shape[0]
    width, hidden = wo.shape[0], w2.shape[0]
    total = 4 * width + 2 * hidden
    half, quarter = tokens // 2, tokens // 4
    any_spec = pl.BlockSpec(memory_space=pl.ANY)
    vm = pl.BlockSpec(memory_space=pltpu.VMEM)
    shape = lambda s, t=bf16: jax.ShapeDtypeStruct(s, t)
    vmem = lambda s, t=bf16: pltpu.VMEM(s, t)
    prb, size = [], D
    for _ in range(dbits):
        size = size // 2 if size >= 256 else size
        prb.append(vmem((16, size), f32))
    prb += [vmem((16, size), f32)] * tbits
    outs = [
        shape((rows, D)),
        shape((rows, D), f32),
        shape((total, blk), f32),
        shape((total, blk)),
        shape((16, size), f32),
        shape((total, D // 2)),
    ]
    outs += [shape((half, D)), shape((quarter, D)), shape((rows, D))] * 2
    outs += [shape((total, D >> (2 + k))) for k in range(dbits - 2)]
    scratch = [
        vmem((tokens, D)),
        vmem((tokens, hidden)),
        vmem((tokens, hidden)),
        vmem((hidden, D)),
        vmem((width, D)),
        vmem((D, 3 * width)),
        vmem((tokens, width)),
        vmem((tokens, 3 * width)),
        vmem((total - hidden, D // 2)),
        vmem((total, D // 2)),
        vmem((2, width, blk), f32),
        vmem((3, width, D // 2)),
        vmem((quarter, D)),
        vmem((quarter, D)),
        vmem((rows, D)),
        vmem((quarter, D)),
        vmem((quarter, D)),
        vmem((rows, D), f32),
        vmem((16, D), f32),
        vmem((8, hidden), f32),
        pltpu.SemaphoreType.DMA((80,)),
        pltpu.SemaphoreType.DMA((80,)),
        pltpu.SemaphoreType.DMA((160,)),
    ] + prb
    if blk % 128:
        scratch.append(vmem((total, blk)))
    return pl.pallas_call(
        functools.partial(reduce_kernel, (dbits, tbits)),
        out_shape=outs,
        in_specs=[vm] * 5 + [any_spec] * 10,
        out_specs=[any_spec] * 4 + [vm] + [any_spec] * (len(outs) - 5),
        scratch_shapes=scratch,
        compiler_params=pltpu.CompilerParams(
            vmem_limit_bytes=62 * 2**20, collective_id=1, has_side_effects=True
        ),
        cost_estimate=pl.CostEstimate(flops=5 * 10**10, bytes_accessed=10**8, transcendentals=10**6),
        name="reduce",
    )(x, dy, params, back_sum, sums, *gathered)


def adam_kernel(plans, me_ref, *refs):
    sub = (me_ref[0] >> SUB_BIT) & 1
    step = pl.program_id(0)
    count = len(plans)
    ins, outs = refs[: 5 * count], refs[5 * count :]
    for k, (begin, half, turned) in enumerate(plans):
        w_ref, m_ref, v_ref, own_ref, recv_ref = ins[5 * k : 5 * k + 5]
        wo_ref, mo_ref, vo_ref = outs[3 * k : 3 * k + 3]

        @pl.when((step >= begin) & (step < begin + 2 * half))
        def _():
            mine = ((step - begin) // half) == sub
            grad = jnp.where(mine, own_ref[...], recv_ref[...].astype(f32))
            grad = (grad.T if turned else grad).reshape(w_ref.shape)
            wo_ref[...], mo_ref[...], vo_ref[...] = adam_update(
                w_ref[...], m_ref[...], v_ref[...], grad, matrix_rate, weight_decay
            )


def adam_call(me, matrices, own, recv):
    blk = own.shape[1]
    plans, operands, in_specs, out_specs, out_shape = [], [], [], [], []
    begin = 0
    for weight, first, second, start, rows, turned in matrices:
        shape = weight.shape
        half = shape[0] if len(shape) == 3 else shape[1 if turned else 0] // (2 * rows)

        def at(i, begin=begin, half=half):
            return jnp.clip(i - begin, 0, 2 * half - 1)

        if len(shape) == 3:
            full = pl.BlockSpec((1, blk, rows), lambda i, at=at, half=half: (at(i) % half, 0, at(i) // half))
        elif turned:
            full = pl.BlockSpec((blk, rows), lambda i, at=at: (0, at(i)))
        else:
            full = pl.BlockSpec((rows, blk), lambda i, at=at: (at(i), 0))
        base = start // rows
        part = pl.BlockSpec((rows, blk), lambda i, at=at, half=half, base=base: (base + at(i) % half, 0))
        plans.append((begin, half, turned))
        operands += [weight, first, second, own, recv]
        in_specs += [full] * 3 + [part] * 2
        out_specs += [full] * 3
        out_shape += [jax.ShapeDtypeStruct(shape, f32)] * 3
        begin += 2 * half
    return tuple(
        pl.pallas_call(
            functools.partial(adam_kernel, plans),
            grid=(begin,),
            out_shape=out_shape,
            in_specs=[smem_spec()] + in_specs,
            out_specs=out_specs,
            compiler_params=vmem_params(60),
            name="adam",
        )(me, *operands)
    )


def per_device(
    inputs,
    segments,
    cotangent,
    qkv_weight,
    qkv_first,
    qkv_second,
    dense_weight,
    dense_first,
    dense_second,
    expand_weight,
    expand_first,
    expand_second,
    shrink_weight,
    shrink_first,
    shrink_second,
    small_params,
    small_first,
    small_second,
):
    dp = lax.axis_size("dp")
    tensor_count = lax.axis_size("tensor")
    dbits = dp.bit_length() - 1
    tbits = tensor_count.bit_length() - 1
    d_me = lax.axis_index("dp")
    t_me = lax.axis_index("tensor")
    sub = (d_me >> SUB_BIT) & 1
    order = place_order(dp)
    high_bits = list(range(2, dbits))
    gather_bits = high_bits + [ROW_BIT]
    rows = inputs.shape[0]
    me = jnp.stack([d_me, t_me]).astype(jnp.int32)

    small_low = jnp.pad(small_params.astype(bf16), ((0, 16 - small_params.shape[0]), (0, 0)))
    ids = jnp.broadcast_to(segments, (8, rows))
    (
        normed, back_rows, qkv_wide, expand_full, dense_full, shrink_full, hidden_act, gelu_slope, attended, proj_back,
        params, back_sum, sums,
    ) = gather_call(
        dbits, tbits, inputs, cotangent, ids, small_low, qkv_weight, expand_weight, dense_weight, shrink_weight
    )
    width, hidden = dense_full.shape[0], shrink_full.shape[0]
    gathered = (
        normed, back_rows, qkv_wide, expand_full, dense_full, shrink_full, hidden_act, gelu_slope, attended, proj_back,
    )
    output, input_grad, own, recv, small_sum, *_ = reduce_call(
        dbits, tbits, inputs, cotangent, params, back_sum, sums, gathered
    )
    blk = D // dp
    if small_sum.shape[1] > blk:
        small_sum = lax.dynamic_slice_in_dim(small_sum, (d_me % (small_sum.shape[1] // blk)) * blk, blk, 1)
    small_sum = small_sum[: small_params.shape[0]]
    block = min(512, hidden)
    new = adam_call(
        me,
        [
            (shrink_weight, shrink_first, shrink_second, 0, block, False),
            (expand_weight, expand_first, expand_second, hidden, block, True),
            (qkv_weight, qkv_first, qkv_second, 2 * hidden, width, True),
            (dense_weight, dense_first, dense_second, 2 * hidden + 3 * width, width, False),
        ],
        own,
        recv,
    )
    shrink_new, expand_new, qkv_new, dense_new = new[0:3], new[3:6], new[6:9], new[9:12]
    small_new = adam_update(small_params, small_first, small_second, small_sum, vector_rate, 0.0)
    return (output, input_grad) + qkv_new + dense_new + expand_new + shrink_new + small_new


def solution(mesh):
    token_spec = P(("dp", "tensor"), None)
    qkv_spec = P(None, "dp", "tensor")
    row_spec = P("tensor", "dp")
    column_spec = P("dp", "tensor")
    small_spec = P(None, "dp")
    weight_specs = (qkv_spec,) * 3 + (row_spec,) * 3 + (column_spec,) * 3 + (row_spec,) * 3 + (small_spec,) * 3
    return jax.shard_map(
        per_device,
        mesh=mesh,
        in_specs=(token_spec, P("dp", "tensor"), token_spec) + weight_specs,
        out_specs=(token_spec, token_spec) + weight_specs,
        check_vma=False,
    )
```

```python
import functools
import jax
import numpy as np
import jax.numpy as jnp
from jax import lax
from jax.experimental import pallas as pl
from jax.experimental.pallas import tpu as pltpu
from jax.sharding import PartitionSpec as P

D = 2048
HD = 64
ROT = 32
FF = 8192
STEP = 10

norm_eps = 1e-05
beta_first = 0.9
beta_second = 0.95
adam_eps = 1e-08
weight_decay = 0.1
matrix_rate = 0.05
vector_rate = 1.0
masked_score = -1e30

SUB_BIT = 1
ROW_BIT = 0

bf16 = jnp.bfloat16
f32 = jnp.float32


def exchange(values, axis, bit):
    count = lax.axis_size(axis)
    return lax.ppermute(values, axis, [(i, i ^ (1 << bit)) for i in range(count)])


def place_order(count):
    bits = count.bit_length() - 1
    order = []
    for p in range(count):
        high = (p >> 1) & ((1 << (bits - 2)) - 1)
        order.append(((p & 1) << SUB_BIT) | (high << 2) | ((p >> (bits - 1)) << ROW_BIT))
    return order


def adam_update(weight, first, second, grad, rate, decay):
    first_new = beta_first * first + (1.0 - beta_first) * grad
    second_new = beta_second * second + (1.0 - beta_second) * grad * grad
    first_hat = first_new / (1.0 - beta_first**STEP)
    second_hat = second_new / (1.0 - beta_second**STEP)
    weight_new = weight - rate * (first_hat / (jnp.sqrt(second_hat) + adam_eps) + decay * weight)
    return (weight_new, first_new, second_new)


def after(values, *others):
    return lax.optimization_barrier((values,) + others)[0]


def gelu_value(pre_values):
    return jax.nn.gelu(pre_values, approximate=True)


def vmem_params(mib):
    return pltpu.CompilerParams(vmem_limit_bytes=mib * 2**20)


def place_of(block, count):
    bits = count.bit_length() - 1
    return ((block >> SUB_BIT) & 1) | ((block >> 2) << 1) | (((block >> ROW_BIT) & 1) << (bits - 1))


def move_blocks(count, source, load, store):
    width = D // count
    if width % 128 == 0:
        for j in range(count):
            start = pl.multiple_of(source(j) * width, width)
            store(pl.ds(j * width, width), load(pl.ds(start, width)))
        return
    for unit in range(count // 2):
        parts = []
        for half in range(2):
            block = source(2 * unit + half)
            value = load(pl.ds(pl.multiple_of((block >> 1) * 128, 128), 128))
            parts.append(pltpu.roll(value, ((block & 1) ^ half) * 64, 1))
        lane = lax.broadcasted_iota(jnp.int32, parts[0].shape, 1)
        store(pl.ds(unit * 128, 128), jnp.where(lane < 64, parts[0], parts[1]))


def smem_spec():
    return pl.BlockSpec(memory_space=pltpu.SMEM)


def assemble(order, me, keep_ref, recv_ref, tmp):
    count = len(order)

    def store(lanes, value):
        tmp[:, lanes] = value

    def add(lanes, value):
        tmp[:, lanes] += value

    move_blocks(count, lambda j: place_of(j ^ me, count), lambda lanes: keep_ref[:, lanes].astype(f32), store)
    move_blocks(count, lambda j: place_of(j ^ me, count) ^ 1, lambda lanes: recv_ref[:, lanes].astype(f32), add)


def swap_rotary(values):
    lane = lax.broadcasted_iota(jnp.int32, values.shape, 1)
    half = ROT // 2
    return jnp.where(
        lane % ROT < half, pltpu.roll(values, 128 - half, 1), pltpu.roll(values, half, 1)
    )


def dot_nn(a, b):
    return lax.dot_general(a, b, (((1,), (0,)), ((), ())), preferred_element_type=f32)


def dot_nt(a, b):
    return lax.dot_general(a, b, (((1,), (1,)), ((), ())), preferred_element_type=f32)


def dot_tn(a, b):
    return lax.dot_general(a, b, (((0,), (0,)), ((), ())), preferred_element_type=f32)


def rel_index(rel, seq, tbits):
    index = seq
    for b in range(tbits):
        index = index | (((rel >> b) & 1) << (tbits - b))
    return index


def mask_bias(bias, start_row, qb, rows):
    kend = (qb + 1) * rows
    key = lax.broadcasted_iota(jnp.int32, (kend, rows), 0)
    query = lax.broadcasted_iota(jnp.int32, (kend, rows), 1) + qb * rows
    bias[:kend, :] = jnp.where((key >= start_row) & (key <= query), 0.0, masked_score)


def attend_rows(qkv, lse, bias, o, seq, qb, width, out_rows):
    rows = bias.shape[1]
    kend = (qb + 1) * rows
    place = slice(qb * rows, kend)
    lane = lax.broadcasted_iota(jnp.int32, (rows, 128), 1)
    zero = jnp.zeros((rows, 128), bf16)

    def pair_body(pair, carry):
        base = pl.multiple_of(pair * 128, 128)
        q = qkv[seq, place, pl.ds(base, 128)] * jnp.asarray(HD ** (-0.5), bf16)
        k = qkv[seq, :kend, pl.ds(base + width, 128)]
        v = qkv[seq, :kend, pl.ds(base + 2 * width, 128)]
        vt = v.T
        outs = []
        for h in range(2):
            mine = (lane < HD) if h == 0 else (lane >= HD)
            s = dot_nt(k, jnp.where(mine, q, zero)) + bias[:kend, :]
            peak = jnp.max(s, axis=0, keepdims=True)
            expo = jnp.exp(s - peak)
            total = jnp.sum(expo, axis=0, keepdims=True)
            weights = (expo * (1.0 / total)).astype(bf16)
            outs.append(dot_nn(vt[h * HD : (h + 1) * HD, :], weights))
            lse[seq, pl.ds(pair * 2 + h, 1), place] = peak + jnp.log(total)
        o[out_rows, pl.ds(base, 128)] = jnp.concatenate(outs, axis=0).T.astype(bf16)
        return carry

    lax.fori_loop(0, width // 128, pair_body, 0)


def attend_back_rows(qkv, lse, bias, do, cosb, sinb, dk, dv, dp, sums, seq, qb, width, out_rows):
    rows = bias.shape[1]
    kend = (qb + 1) * rows
    place = slice(qb * rows, kend)
    scale = HD ** (-0.5)
    lane = lax.broadcasted_iota(jnp.int32, (rows, 128), 1)
    zero = jnp.zeros((rows, 128), bf16)

    def pair_body(pair, carry):
        base = pl.multiple_of(pair * 128, 128)
        lanes = pl.ds(base, 128)
        q = qkv[seq, place, lanes]
        k = qkv[seq, :kend, pl.ds(base + width, 128)]
        v = qkv[seq, :kend, pl.ds(base + 2 * width, 128)]
        kt = k.T
        dout = do[out_rows, lanes]
        outs = []
        for h in range(2):
            mine = (lane < HD) if h == 0 else (lane >= HD)
            qm = jnp.where(mine, q, zero) * jnp.asarray(scale, bf16)
            dom = jnp.where(mine, dout, zero)
            s = dot_nt(k, qm) + bias[:kend, :]
            probs = jnp.exp(s - lse[seq, pl.ds(pair * 2 + h, 1), place])
            dprobs = dot_nt(v, dom)
            inner = jnp.sum(probs * dprobs, axis=0, keepdims=True)
            ds = (probs * (dprobs - inner)).astype(bf16)
            dv[:kend, lanes] += dot_nn(probs.astype(bf16), dom)
            dk[:kend, lanes] += dot_nn(ds, qm)
            outs.append(dot_nn(kt[h * HD : (h + 1) * HD, :], ds))
        dq = jnp.concatenate(outs, axis=0).T * scale
        dq = dq * cosb[seq, place, :] - swap_rotary(dq) * sinb[seq, place, :]
        dq = dq.astype(bf16)
        dp[out_rows, lanes] = dq
        sums[0:1, lanes] += jnp.sum(dq.astype(f32), axis=0, keepdims=True)
        return carry

    lax.fori_loop(0, width // 128, pair_body, 0)


def attend_back_keys(cosb, sinb, dk, dv, dp, sums, seq, b, width, out_rows):
    rows = out_rows.size
    place = slice(b * rows, (b + 1) * rows)
    cosine = cosb[seq, place, :]
    sine = sinb[seq, place, :]
    for j in range(width // 128):
        lanes = slice(j * 128, (j + 1) * 128)
        part = dk[place, lanes]
        part = (part * cosine - swap_rotary(part) * sine).astype(bf16)
        kl = slice(width + j * 128, width + (j + 1) * 128)
        dp[out_rows, kl] = part
        sums[0:1, kl] += jnp.sum(part.astype(f32), axis=0, keepdims=True)
        part = dv[place, lanes].astype(bf16)
        vl = slice(2 * width + j * 128, 2 * width + (j + 1) * 128)
        dp[out_rows, vl] = part
        sums[0:1, vl] += jnp.sum(part.astype(f32), axis=0, keepdims=True)


class Links:
    def __init__(self, send_sems, recv_sems, local_sems):
        self.send_sems, self.recv_sems, self.local_sems = send_sems, recv_sems, local_sems
        self.sent, self.count, self.locals = [], 0, 0

    def send(self, src, dst, axis, bit):
        partner = lax.axis_index(axis) ^ (1 << bit)
        i = self.count
        self.count += 1
        copy = pltpu.make_async_remote_copy(
            src_ref=src,
            dst_ref=dst,
            send_sem=self.send_sems.at[i],
            recv_sem=self.recv_sems.at[i],
            device_id={axis: partner},
            device_id_type=pl.DeviceIdType.MESH,
        )
        copy.start()
        self.sent.append(copy)
        return copy

    def local(self, src, dst):
        copy = pltpu.make_async_copy(src, dst, self.local_sems.at[self.locals])
        self.locals += 1
        copy.start()
        return copy

    def local_wait(self, src, dst):
        self.local(src, dst).wait()

    def sent_done(self, copy):
        copy.wait_send()
        self.sent = [other for other in self.sent if other is not copy]

    def finish(self):
        for copy in self.sent:
            copy.wait_send()


def greet(dbits, tbits):
    barrier = pltpu.get_barrier_semaphore()
    partners = [("dp", b) for b in range(dbits)] + [("tensor", b) for b in range(tbits)]
    for axis, bit in partners:
        pl.semaphore_signal(
            barrier,
            inc=1,
            device_id={axis: lax.axis_index(axis) ^ (1 << bit)},
            device_id_type=pl.DeviceIdType.MESH,
        )
    pl.semaphore_wait(barrier, len(partners))


class Gathered:
    def __init__(self, links, slot, count, bits, outgoing):
        self.links, self.slot, self.bits, self.outgoing = links, slot, bits, outgoing
        self.left = count - 1
        self.coming = {}

    def source(self, p):
        size = 1 << (p.bit_length() - 1)
        return p - size, self.bits[p.bit_length() - 1]

    def send(self, p):
        src, bit = self.source(p)
        ref = self.outgoing if p == 1 else self.slot(src)
        self.coming[p] = self.links.send(ref, self.slot(p), "dp", bit)

    def wait(self, p):
        self.coming[p].wait_recv()
        self.left -= 1


class GatheredPairs(Gathered):
    def __init__(self, links, slot, count, bits, outgoing, own, received):
        super().__init__(links, slot, count, bits, outgoing)
        self.own, self.received = own, received

    def send(self, p):
        src, bit = self.source(p)
        if p == 1:
            self.coming[p] = self.links.send(self.outgoing, self.received, "dp", bit)
        elif p % 2 == 0 and src > 0:
            self.coming[p] = self.links.send(self.slot(src // 2), self.slot(p // 2), "dp", bit)

    def wait(self, p):
        if p == 1:
            self.coming[p].wait_recv()
            both = [self.own[...].astype(f32), self.received[...].astype(f32)]
            self.slot(0)[...] = jnp.concatenate(both, axis=1).astype(bf16)
            for later in range(1, len(self.bits)):
                bit = self.bits[later]
                self.coming[1 << later] = self.links.send(self.slot(0), self.slot(1 << (later - 1)), "dp", bit)
        elif p % 2 == 0:
            self.coming[p].wait_recv()
        self.left -= 1


def cast_store(dst, src):
    dst[...] = src[...].astype(bf16)


def gather_kernel(
    cfg,
    x_ref, dy_ref, ids_ref, small_ref, freq_ref, qkv_ref, w1_ref, wo_ref, w2_ref,
    n_out, dy_out, wq_out, w1_out, wo_out, w2_out, h_out, gp_out, o_out, dp_out, params_out, dysum_out, sums_out,
    n, dyb, wq, w1, wo, w2, sq, s1, so, s2, sta, stb, stc, std, tmp, nsw, pbuf, idb, cosb, sinb, startb,
    qkvb, lse, bias, o, do, dk, dv, dp, hst, gst, send_sems, recv_sems, local_sems, *pieces
):
    dbits, tbits = cfg
    order = place_order(1 << dbits)
    count = len(order)
    me = lax.axis_index("dp")
    me_t = lax.axis_index("tensor")
    sub = (me >> SUB_BIT) & 1
    rows = x_ref.shape[0]
    width = wo.shape[0]
    hidden = w2.shape[0]
    blk = D // count
    seqs = 2
    blocks = 1 << tbits
    length = rows * blocks
    links = Links(send_sems, recv_sems, local_sems)
    bits = [SUB_BIT] + list(range(2, dbits)) + [ROW_BIT]

    own_q = pl.ds(pl.multiple_of(sub * width, width), width)
    other_q = pl.ds(pl.multiple_of((1 - sub) * width, width), width)
    own_h = pl.ds(pl.multiple_of(sub * hidden, hidden), hidden)
    other_h = pl.ds(pl.multiple_of((1 - sub) * hidden, hidden), hidden)
    loads = {"q": [], "1": [], "2": [], "o": []}
    for j in range(3):
        lanes = pl.ds(j * width, width)
        loads["q"].append(links.local(qkv_ref.at[j, :, other_q], std.at[:, lanes]))
        loads["q"].append(links.local(qkv_ref.at[j, :, own_q], stc.at[:, lanes]))
    loads["2"].append(links.local(w2_ref.at[other_h, :], stb))
    loads["2"].append(links.local(w2_ref.at[own_h, :], sta))

    def row_gather(ref, outgoing):
        return Gathered(links, lambda p: ref.at[pl.ds(p * blk, blk), :], count, bits, outgoing)

    def column_gather(ref, outgoing, own, received):
        unit = max(blk, 128)
        slot = lambda p: ref.at[:, pl.ds(p * unit, unit)]
        if unit == blk:
            return Gathered(links, slot, count, bits, outgoing)
        return GatheredPairs(links, slot, count, bits, outgoing, own, received)

    gathers = {"q": row_gather(wq, sq), "1": row_gather(w1, s1)}
    gathers["o"] = column_gather(wo, so, *pieces[0:2])
    wo_own, w2_own = (wo.at[:, pl.ds(0, blk)], w2.at[:, pl.ds(0, blk)]) if blk % 128 == 0 else (pieces[0], pieces[2])
    outs = {"q": (wq, wq_out), "1": (w1, w1_out), "o": (wo, wo_out), "n": (n, n_out), "d": (dyb, dy_out)}
    for i in range(2):
        part = pl.ds(i * (hidden // 2), hidden // 2)
        extra = [piece.at[part, :] for piece in pieces[2:4]] if blk % 128 else [None, None]
        gathers["23"[i]] = column_gather(w2.at[part, :], s2.at[part, :], *extra)
        outs["23"[i]] = (w2.at[part, :], w2_out.at[part, :])
    token_bufs = {"n": n, "d": dyb}
    token_left = {"n": 2 * blocks - 1, "d": 2 * blocks - 1}
    coming, stores, kept, attended, begun = {}, [], {}, set(), set()

    def tok(ref, i):
        return ref.at[pl.ds(i * rows, rows), :]

    def send(kind, i):
        if kind in gathers:
            gathers[kind].send(i)
        elif kind in token_bufs:
            ref = token_bufs[kind]
            if i == 1:
                coming[kind, i] = links.send(nsw, tok(ref, 1), "dp", SUB_BIT)
            else:
                step = i.bit_length() - 1
                coming[kind, i] = links.send(tok(ref, i - (1 << step)), tok(ref, i), "tensor", tbits - step)
        else:
            buf = pbuf if kind == "P" else idb
            axis, bit = ("dp", bits[i - 1]) if kind == "P" or i == 1 else ("tensor", tbits + 1 - i)
            size = 1 << (i - 1)
            coming[kind, i] = links.send(buf.at[pl.ds(0, size)], buf.at[pl.ds(size, size)], axis, bit)

    def wait(kind, i):
        if kind in gathers:
            gathers[kind].wait(i)
            complete = gathers[kind].left == 0
        else:
            coming[kind, i].wait_recv()
            complete = False
            if kind in token_bufs:
                token_left[kind] -= 1
                complete = token_left[kind] == 0
        if complete:
            stores.append(links.local(*outs[kind]))

    def arrived(name):
        for copy in loads[name]:
            copy.wait()

    def cast_q():
        arrived("q")
        sq[...] = std[:, 0 : 3 * width].astype(bf16)
        wq[0:blk, :] = stc[:, 0 : 3 * width].astype(bf16)
        loads["1"].append(links.local(w1_ref.at[:, other_h], std))
        loads["1"].append(links.local(w1_ref.at[:, own_h], stc))

    def cast_1():
        arrived("1")
        s1[...] = std[...].astype(bf16)
        w1[0:blk, :] = stc[...].astype(bf16)

    def cast_2():
        arrived("2")
        s2[...] = stb[...].astype(bf16)
        w2_own[...] = sta[...].astype(bf16)
        loads["o"].append(links.local(wo_ref.at[other_q, :], stb.at[pl.ds(0, width), :]))
        loads["o"].append(links.local(wo_ref.at[own_q, :], sta.at[pl.ds(0, width), :]))

    def cast_o():
        arrived("o")
        so[...] = stb[0:width, :].astype(bf16)
        wo_own[...] = sta[0:width, :].astype(bf16)

    def statistics():
        x = x_ref[...].astype(f32)
        x = x - jnp.mean(x, axis=-1, keepdims=True)
        inv = lax.rsqrt(jnp.mean(x * x, axis=-1, keepdims=True) + norm_eps)
        tmp[...] = x * inv

    def store_to(ref):
        def store(lanes, value):
            ref[0:rows, lanes] = value.astype(bf16)

        return store

    load_tmp = lambda lanes: tmp[:, lanes]
    load_dy = lambda lanes: dy_ref[:, lanes].astype(f32)

    def norm():
        per = max(1, 128 // blk)
        for a in range(0, count, per):
            part = [pbuf[place_of((a + k) ^ me, count)].astype(f32) for k in range(per)]
            lanes = pl.ds(a * blk, per * blk)
            params_out[:, lanes] = part[0] if per == 1 else jnp.concatenate(part, axis=1)
        tmp[...] = tmp[...] * params_out[0:1, :] + params_out[1:2, :]
        move_blocks(count, lambda j: me ^ order[j ^ 1], load_tmp, store_to(nsw))
        move_blocks(count, lambda j: me ^ order[j], load_tmp, store_to(n))

    def back_own():
        move_blocks(count, lambda j: me ^ order[j], load_dy, store_to(dyb))
        dysum_out[...] = jnp.sum(dy_ref[...].astype(f32), axis=0, keepdims=True)

    def back_swapped():
        links.sent_done(coming["n", 1])
        move_blocks(count, lambda j: me ^ order[j ^ 1], load_dy, store_to(nsw))

    def tables():
        for seq in range(seqs):
            row = jnp.concatenate(
                [idb[rel_index(me_t ^ b, seq, tbits)][0:1, :] for b in range(blocks)], axis=1
            ).astype(f32)
            first = jnp.sum(jnp.where(row < 1.0, 1.0, 0.0), axis=1, keepdims=True)
            second = jnp.sum(jnp.where(row < 2.0, 1.0, 0.0), axis=1, keepdims=True)
            begin = jnp.where(row < 1.0, 0.0, jnp.where(row < 2.0, first, second))
            place = lax.broadcasted_iota(jnp.int32, (1, length), 1).astype(f32)
            startb[seq, 0:1, :] = begin.astype(jnp.int32)
            angle = freq_ref[:, 0:1] * (place - begin)
            cosine, sine = jnp.cos(angle), jnp.sin(angle)
            rest = (HD - ROT, length)
            cosine = jnp.concatenate([cosine, cosine, jnp.ones(rest, f32)], axis=0)
            sine = jnp.concatenate([-sine, sine, jnp.zeros(rest, f32)], axis=0)
            cosb[seq] = jnp.concatenate([cosine, cosine], axis=0).T
            sinb[seq] = jnp.concatenate([sine, sine], axis=0).T

    head_start = me_t * (2 * width) + sub * width
    hidden_start = me_t * (2 * hidden) + sub * hidden
    pairs = width // 128

    def two_blocks(c):
        return pl.ds(2 * c * rows, 2 * rows)

    def project(c):
        lanes = pl.ds(pl.multiple_of(head_start, width), width)
        qkv_bias = [params_out[2 + j : 3 + j, lanes] for j in range(3)]
        rel = sum(((c >> (tbits - 1 - b)) & 1) << b for b in range(tbits))
        block = me_t ^ rel
        place = pl.ds(pl.multiple_of(block * rows, rows), rows)
        part = dot_nn(n[two_blocks(c), :], wq[...])
        for seq in range(seqs):
            seq_rows = slice(seq * rows, (seq + 1) * rows)
            cosine, sine = cosb[seq, place, :], sinb[seq, place, :]
            for j in range(3 * pairs):
                kind, pair = j // pairs, j % pairs
                value = part[seq_rows, j * 128 : (j + 1) * 128] + qkv_bias[kind][:, pair * 128 : (pair + 1) * 128]
                if kind < 2:
                    value = value * cosine + swap_rotary(value) * sine
                qkvb[seq, place, j * 128 : (j + 1) * 128] = value.astype(bf16)

    def seq_rows_of(seq, b):
        return pl.ds(pl.multiple_of(rel_index(me_t ^ b, seq, tbits) * rows, rows), rows)

    def attend(seq, qb):
        mask_bias(bias, startb[seq, 0:1, qb * rows : (qb + 1) * rows], qb, rows)
        attend_rows(qkvb, lse, bias, o, seq, qb, width, seq_rows_of(seq, qb))
        attended.add((seq, qb))
        if len(attended) == seqs * blocks:
            stores.append(links.local(o, o_out))

    def attend_back(seq, qb):
        if seq not in begun:
            begun.add(seq)
            dk[...] = jnp.zeros_like(dk)
            dv[...] = jnp.zeros_like(dv)
        mask_bias(bias, startb[seq, 0:1, qb * rows : (qb + 1) * rows], qb, rows)
        attend_back_rows(
            qkvb, lse, bias, do, cosb, sinb, dk, dv, dp, sums_out, seq, qb, width, seq_rows_of(seq, qb)
        )

    def attend_keys(seq):
        for b in range(blocks):
            attend_back_keys(cosb, sinb, dk, dv, dp, sums_out, seq, b, width, seq_rows_of(seq, b))

    tile = hst.shape[2]

    def hide(c):
        row = 7 + hidden_start // D
        hidden_bias = params_out[pl.ds(row, 1), pl.ds(pl.multiple_of(hidden_start % D, hidden), hidden)]
        for t in range(hidden // tile):
            lanes = pl.ds(t * tile, tile)
            slot = t % 2
            for copy in kept.pop(slot, ()):
                copy.wait()
            v = dot_nn(n[two_blocks(c), :], w1[:, lanes]) + hidden_bias[:, t * tile : (t + 1) * tile]
            root = 0.7978845608028654
            square = v * v
            th = jnp.tanh(root * (v + 0.044715 * v * square))
            hst[slot] = (0.5 * v * (1.0 + th)).astype(bf16)
            gst[slot] = (
                0.5 * (1.0 + th) + 0.5 * v * (1.0 - th * th) * (root * (1.0 + (3 * 0.044715) * square))
            ).astype(bf16)
            kept[slot] = (
                links.local(hst.at[slot], h_out.at[two_blocks(c), lanes]),
                links.local(gst.at[slot], gp_out.at[two_blocks(c), lanes]),
            )

    def output_back(c):
        do[two_blocks(c), :] = dot_nt(dyb[two_blocks(c), :], wo[...]).astype(bf16)

    def end():
        stores.append(links.local(dp, dp_out))
        for copies in kept.values():
            stores.extend(copies)
        for copy in stores:
            copy.wait()
        links.finish()

    pbuf[0] = small_ref[...]
    idb[0] = ids_ref[...]
    sums_out[...] = jnp.zeros_like(sums_out)
    greet(dbits, tbits)
    steps = {
        "castq": cast_q, "cast1": cast_1, "cast2": cast_2, "casto": cast_o, "stat": statistics, "ln": norm,
        "dyr": back_own, "dys": back_swapped, "table": tables, "end": end,
    }
    indexed = {"Q": project, "A": attend, "B": attend_back, "K": attend_keys, "H": hide, "D": output_back}
    for name in gather_schedule(count, blocks):
        if name in steps:
            steps[name]()
        elif name[0] == "S":
            send(name[1], int(name[2:]))
        elif name[0] == "W":
            wait(name[1], int(name[2:]))
        else:
            indexed[name[0]](*[int(i) for i in name[1:]])


GATHER_ORDER = [
    0, 6, 14, 1, 29, 2, 44, 47, 7, 8, 48, 49, 9, 3, 4, 5, 12, 32, 13, 15, 57, 45, 75, 10, 31, 62, 50, 104,
    51, 53, 105, 78, 16, 30, 54, 52, 11, 43, 55, 56, 33, 34, 18, 67, 17, 68, 58, 19, 35, 63, 36, 21, 106, 20,
    46, 61, 59, 92, 22, 25, 60, 108, 26, 131, 133, 90, 109, 37, 76, 38, 110, 41, 23, 39, 40, 27, 24, 107,
    132, 28, 134, 42, 121, 71, 119, 73, 111, 77, 91, 120, 113, 64, 114, 65, 116, 112, 122, 123, 126, 125, 82,
    66, 118, 117, 86, 124, 83, 115, 135, 93, 94, 130, 129, 95, 79, 81, 127, 72, 69, 70, 96, 137, 97, 128,
    136, 74, 138, 80, 139, 142, 140, 98, 99, 141, 87, 143, 147, 88, 84, 85, 100, 145, 146, 103, 144, 148,
    102, 101, 89, 149,
]


def gather_schedule(count, blocks):
    names = []

    def take(kind, places, first):
        def push(p):
            size = first
            while size < places:
                if p < size:
                    names.append("S%s%d" % (kind, p + size))
                size *= 2

        names.append("S%s1" % kind)
        push(0)
        for p in range(1, places):
            names.append("W%s%d" % (kind, p))
            push(p)

    for i in range(1, count.bit_length()):
        names.extend(["SP%d" % i, "WP%d" % i])
    for i in range(1, blocks.bit_length() + 1):
        names.extend(["SI%d" % i, "WI%d" % i])
    names.extend(["stat", "ln", "castq"])
    take("n", 2 * blocks, 2)
    take("q", count, 2)
    names.extend(["table", "cast1", "dyr", "dys"])
    take("1", count, 2)
    take("d", 2 * blocks, 2)
    names.append("cast2")
    take("2", count, 2)
    take("3", count, 2)
    names.append("casto")
    take("o", count, 2)
    names.extend("Q%d" % c for c in range(blocks))
    names.extend("A%d%d" % (s, b) for s in range(2) for b in range(blocks))
    names.extend("H%d" % c for c in range(blocks))
    names.extend("D%d" % c for c in range(blocks))
    for s in range(2):
        names.extend("B%d%d" % (s, b) for b in range(blocks))
        names.append("K%d" % s)
    names.append("end")
    if (count, blocks) == (8, 4):
        return [names[i] for i in GATHER_ORDER]
    return names


def gather_call(dbits, tbits, x, dy, ids, small, qkv_weight, expand_weight, dense_weight, shrink_weight):
    count = 1 << dbits
    blk = D // count
    rows = x.shape[0]
    width = qkv_weight.shape[2] // 2
    hidden = expand_weight.shape[1] // 2
    tokens = rows * (2 << tbits)
    length = rows << tbits
    heads = width // HD
    half = ROT // 2
    powers = (10000.0 ** (-np.arange(half) / half)).astype(np.float32)
    freqs = jnp.asarray(np.repeat(powers[:, None], 128, axis=1))
    any_spec = pl.BlockSpec(memory_space=pl.ANY)
    vm = pl.BlockSpec(memory_space=pltpu.VMEM)
    shape = lambda s, t=bf16: jax.ShapeDtypeStruct(s, t)
    vmem = lambda s, t=bf16: pltpu.VMEM(s, t)
    weights = 5 * (count - 1) + 4 * (2 << tbits) + 2 * (dbits + tbits) + 8
    scratch = [
        vmem((tokens, D)),
        vmem((tokens, D)),
        vmem((D, 3 * width)),
        vmem((D, hidden)),
        vmem((width, D)),
        vmem((hidden, D)),
        vmem((blk, 3 * width)),
        vmem((blk, hidden)),
        vmem((width, blk)),
        vmem((hidden, blk)),
        vmem((hidden, blk), f32),
        vmem((hidden, blk), f32),
        vmem((blk, hidden), f32),
        vmem((blk, hidden), f32),
        vmem((rows, D), f32),
        vmem((rows, D)),
        vmem((count, small.shape[0], blk)),
        vmem((2 << tbits, 8, rows), jnp.int32),
        vmem((2, length, 128), f32),
        vmem((2, length, 128), f32),
        vmem((2, 8, length), jnp.int32),
        vmem((2, length, 3 * width)),
        vmem((2, heads, length), f32),
        vmem((length, rows), f32),
        vmem((tokens, width)),
        vmem((tokens, width)),
        vmem((length, width), f32),
        vmem((length, width), f32),
        vmem((tokens, 3 * width)),
        vmem((2, 2 * rows, min(hidden, 512))),
        vmem((2, 2 * rows, min(hidden, 512))),
        pltpu.SemaphoreType.DMA((weights,)),
        pltpu.SemaphoreType.DMA((weights,)),
        pltpu.SemaphoreType.DMA((48,)),
    ]
    pieces = (vmem((width, blk)), vmem((hidden, blk)))
    scratch += [pieces[0]] * 2 + [pieces[1]] * 2 if blk % 128 else [vmem((16, 128))] * 4
    return pl.pallas_call(
        functools.partial(gather_kernel, (dbits, tbits)),
        out_shape=[
            shape((tokens, D)),
            shape((tokens, D)),
            shape((D, 3 * width)),
            shape((D, hidden)),
            shape((width, D)),
            shape((hidden, D)),
            shape((tokens, hidden)),
            shape((tokens, hidden)),
            shape((tokens, width)),
            shape((tokens, 3 * width)),
            shape((small.shape[0], D), f32),
            shape((1, D), f32),
            shape((8, 3 * width), f32),
        ],
        in_specs=[vm] * 5 + [any_spec] * 4,
        out_specs=[any_spec] * 10 + [vm] * 3,
        scratch_shapes=scratch,
        compiler_params=pltpu.CompilerParams(
            vmem_limit_bytes=62 * 2**20, collective_id=0, has_side_effects=True
        ),
        cost_estimate=pl.CostEstimate(flops=2 * 10**10, bytes_accessed=10**8, transcendentals=10**7),
        name="gather",
    )(x, dy, ids, small, freqs, qkv_weight, expand_weight, dense_weight, shrink_weight)


class Unit:
    def __init__(self, start, rows, lhs, first, rhs, send_start, frees):
        self.here, self.rows = pl.ds(start, rows), rows
        self.lhs, self.first, self.rhs = lhs, first, rhs
        self.out = pl.ds(send_start, rows)
        self.frees, self.hop, self.load, self.slot = frees, None, None, None


class TokenSum:
    def __init__(self, partial, far, near, keep, rc, rx, rs):
        self.partial, self.far, self.near, self.keep = partial, far, near, keep
        self.rc, self.rx, self.rs = rc, rx, rs
        self.hops = {}


def reduce_kernel(
    cfg,
    x_ref, dy_own_ref, params_ref, back_sum_ref, sums_ref,
    n_hbm, dy_hbm, wq_hbm, w1_hbm, wo_hbm, w2_hbm, h_hbm, gp_hbm, o_hbm, dp_hbm,
    y_out, dx_out, own_out, rl, pg_out, ry, rc1, rx1, rs1, rc2, rx2, rs2, *rest
):
    dbits, tbits = cfg
    highs = dbits - 2
    rz, rest = rest[:highs], rest[highs:]
    (
        big, hw1, gp, w2, wo, wq, o, dp, outgoing, keep, own, came, sx, kx, sz, sc, stage, tmp, pg, hsum,
        send_sems, recv_sems, local_sems, *rest
    ) = rest
    prb, last = rest[: dbits + tbits], rest[dbits + tbits :]
    order = place_order(1 << dbits)
    count = len(order)
    me = lax.axis_index("dp")
    me_t = lax.axis_index("tensor")
    sub = (me >> SUB_BIT) & 1
    rows = x_ref.shape[0]
    blk = D // count
    width, hidden = wo.shape[0], w2.shape[0]
    tokens = n_hbm.shape[0]
    links = Links(send_sems, recv_sems, local_sems)
    high_bits = list(range(2, dbits))
    side = D // 2
    half, quarter = tokens // 2, tokens // 4
    step_lanes = 512

    pending = {}

    def fetch(name, src, dst):
        pending.setdefault(name, []).append(links.local(src, dst))

    def need(*names):
        for name in names:
            for copy in pending.pop(name, ()):
                copy.wait()

    fetch("o", o_hbm, o)
    fetch("dy", dy_hbm, big)
    fetch("h", h_hbm, hw1)

    def load_more():
        fetch("w2", w2_hbm, w2)
        fetch("gp", gp_hbm, gp)
        fetch("dp", dp_hbm, dp)
        fetch("wq", wq_hbm, wq)
        fetch("wo", wo_hbm, wo)

    def load_n():
        for i in range(2):
            links.sent_done(sums["dn"].hops["c", i])
        for i in range(2):
            part = pl.ds(i * half, half)
            fetch("n", n_hbm.at[part, :], big.at[part, :])

    units = {"o": Unit(2 * hidden + 3 * width, width, o, 0, "dy", hidden + 3 * width, None)}
    per = hidden // width
    for i in range(per):
        at = i * width
        units["a%d" % i] = Unit(at, width, hw1, at, "dy", at, None)
        units["c%d" % i] = Unit(at + hidden, width, gp, at, "n", at, "a%d" % i)
    for j in range(3):
        at = hidden + j * width
        units["q%d" % j] = Unit(at + hidden, width, dp, j * width, "n", at, None)

    def product(unit, part):
        need(unit.rhs, *(["dp"] if unit.lhs is dp else ["h"] if unit.lhs is hw1 else ["o"]))
        lhs = unit.lhs[:, pl.ds(unit.first, unit.rows)]
        return dot_tn(lhs, big[:, pl.ds(part * side, side)]).astype(bf16)

    def away(unit):
        if unit.frees:
            links.sent_done(units[unit.frees].first_hop)
        outgoing[unit.out, :] = product(unit, 1)

    def home(unit):
        keep[unit.here, :] = product(unit, 0)

    def send_y(unit):
        unit.hop = links.send(outgoing.at[unit.out, :], ry.at[unit.here, :], "dp", ROW_BIT)
        unit.first_hop = unit.hop

    free = list(range(came.shape[0]))

    def load_received(unit, src):
        if free:
            unit.slot = free.pop()
            part = came.at[unit.slot, :, pl.ds(0, src.shape[1])]
            unit.load = links.local(src.at[unit.here, :], part)

    def add_received(unit, src):
        lanes = src.shape[1]
        value = keep[unit.here, 0:lanes].astype(f32)
        if unit.load is None:
            part = stage.at[pl.ds(0, unit.rows), pl.ds(0, lanes)]
            links.local_wait(src.at[unit.here, :], part)
            return value + part[...].astype(f32)
        unit.load.wait()
        unit.load = None
        free.append(unit.slot)
        return value + came[unit.slot, :, 0:lanes].astype(f32)

    def fold_first(unit):
        keep[unit.here, :] = add_received(unit, ry).astype(bf16)

    def send_high(unit, k=0):
        lanes = side >> (k + 1)
        part = keep.at[unit.here, pl.ds(lanes, lanes)]
        unit.hop = links.send(part, rz[k].at[unit.here, :], "dp", high_bits[highs - 1 - k])

    slots = []

    def fold_last(unit):
        for k in range(highs - 1):
            keep[unit.here, 0 : side >> (k + 1)] = add_received(unit, rz[k]).astype(bf16)
            send_high(unit, k + 1)
            unit.hop.wait_recv()
        value = add_received(unit, rz[highs - 1])
        slot = len(slots) % own.shape[0]
        if len(slots) >= own.shape[0]:
            slots[-own.shape[0]].wait()
        own[slot] = value[:, 0:blk]
        slots.append(links.local(own.at[slot], own_out.at[unit.here, :]))
        if last:
            last[0][unit.here, :] = value[:, blk : 2 * blk].astype(bf16)
        else:
            keep[unit.here, blk : 2 * blk] = value[:, blk : 2 * blk].astype(bf16)

    def send_sub(unit):
        part = last[0].at[unit.here, :] if last else keep.at[unit.here, pl.ds(blk, blk)]
        unit.hop = links.send(part, rl.at[unit.here, :], "dp", SUB_BIT)

    hsum[...] = jnp.zeros_like(hsum)

    def hidden_back(c):
        need("dy", "w2", "gp")
        place = pl.ds(c * quarter, quarter)
        for t in range(0, hidden, 512):
            lanes = slice(t, t + 512)
            value = (dot_nt(big[place, :], w2[lanes, :]) * gp[place, lanes].astype(f32)).astype(bf16)
            gp[place, lanes] = value
            hsum[0:1, lanes] += jnp.sum(value.astype(f32), axis=0, keepdims=True)

    def branch(place, lanes):
        return dot_nn(o[place, :], wo[:, lanes]) + dot_nn(hw1[place, :], w2[:, lanes])

    def normed_back(place, lanes):
        return dot_nt(dp[place, :], wq[lanes, :]) + dot_nt(gp[place, :], hw1[lanes, :])

    def part_rows(partial, first, dst, added):
        place = pl.ds(first, quarter)

        def body(t, carry):
            lanes = pl.ds(pl.multiple_of(t * step_lanes, step_lanes), step_lanes)
            value = partial(place, lanes)
            if added is not None:
                value = value + added[:, lanes].astype(f32)
            dst[:, lanes] = value.astype(bf16)
            return carry

        lax.fori_loop(0, D // step_lanes, body, 0)

    big_rows = lambda first: big.at[pl.ds(first, quarter), :]
    sums = {
        "dn": TokenSum(normed_back, (big_rows(half), big_rows(half + quarter)), sx, kx, rc1, rx1, rs1),
        "br": TokenSum(branch, (sc, sc), sc, sx, rc2, rx2, rs2),
    }

    def far_rows(t, i):
        need("wo", "w2", "o", "h") if t is sums["br"] else need("dp", "wq", "w1")
        if t is sums["br"] and i == 0:
            links.sent_done(t.hops["c", 1])
        part_rows(t.partial, half + i * quarter, t.far[i], None)

    def send_core(t, i):
        there = pl.ds(i * quarter, quarter)
        t.hops["c", i] = links.send(t.far[i], t.rc.at[there, :], "tensor", 0)

    def near_rows(t):
        if t is sums["br"]:
            links.sent_done(t.hops["c", 0])
        links.local_wait(t.rc.at[pl.ds(quarter, quarter), :], stage)
        part_rows(t.partial, quarter, t.near, stage)

    def send_x(t, i):
        part = pl.ds(i * rows, rows)
        t.hops["x", i] = links.send(t.near.at[part, :], t.rx.at[part, :], "tensor", 1)

    def keep_rows(t):
        if t is sums["br"]:
            for i in range(2):
                links.sent_done(sums["dn"].hops["x", i])
        links.local_wait(t.rc.at[pl.ds(0, quarter), :], stage)
        part_rows(t.partial, 0, t.keep, stage)

    def partner_rows(t):
        if t is sums["br"]:
            links.sent_done(sums["dn"].hops["s"])
        links.local_wait(t.rx.at[pl.ds(rows, rows), :], stage.at[pl.ds(0, rows), :])
        sz[...] = (t.keep[rows : 2 * rows, :].astype(f32) + stage[0:rows, :].astype(f32)).astype(bf16)

    def send_last(t):
        t.hops["s"] = links.send(sz, t.rs, "dp", SUB_BIT)

    def own_rows(t):
        links.local_wait(t.rx.at[pl.ds(0, rows), :], stage.at[pl.ds(0, rows), :])
        t.keep[0:rows, :] = (t.keep[0:rows, :].astype(f32) + stage[0:rows, :].astype(f32)).astype(bf16)
        received = stage.at[pl.ds(rows, rows), :]
        links.local_wait(t.rs, received)
        assemble(order, me, t.keep.at[pl.ds(0, rows), :], received, tmp)

    def norm_back():
        own_rows(sums["dn"])
        pg[...] = jnp.zeros_like(pg)
        strip = 64

        def body(i, carry):
            place = pl.ds(pl.multiple_of(i * strip, strip), strip)
            x = x_ref[place, :].astype(f32)
            x = x - jnp.mean(x, axis=-1, keepdims=True)
            inv = lax.rsqrt(jnp.mean(x * x, axis=-1, keepdims=True) + norm_eps)
            x = x * inv
            back = tmp[place, :]
            pg[0:1, :] += jnp.sum(back * x, axis=0, keepdims=True)
            pg[1:2, :] += jnp.sum(back, axis=0, keepdims=True)
            e = back * params_ref[0:1, :]
            tmp[place, :] = dy_own_ref[place, :].astype(f32) + inv * (
                e - jnp.mean(e, axis=-1, keepdims=True) - x * jnp.mean(e * x, axis=-1, keepdims=True)
            )
            return carry

        lax.fori_loop(0, rows // strip, body, 0)
        fetch("dx", tmp, dx_out)
        head_start = me_t * (2 * width) + sub * width
        hidden_start = me_t * (2 * hidden) + sub * hidden
        lanes = pl.ds(pl.multiple_of(head_start, width), width)
        for j in range(3):
            pg[2 + j : 3 + j, lanes] = sums_ref[0:1, j * width : (j + 1) * width]
        pg[5:6, :] = back_sum_ref[...]
        pg[6:7, :] = back_sum_ref[...]
        pg[pl.ds(7 + hidden_start // D, 1), pl.ds(pl.multiple_of(hidden_start % D, hidden), hidden)] = hsum[0:1, :]

    hops, base, size = [], 0, D
    for bit in reversed(range(dbits)):
        mine = (me >> bit) & 1
        if size >= 256:
            size //= 2
            there = (base + (1 - mine) * size, size)
            base = base + mine * size
        else:
            there = (base, size)
        hops.append(("dp", bit, there, (base, size)))
    for bit in range(tbits):
        hops.append(("tensor", bit, (base, size), (base, size)))
    lanes_of = lambda at: pl.ds(pl.multiple_of(at[0], at[1]), at[1])
    small_hops = {}

    def send_small(i):
        axis, bit, there, _ = hops[i]
        small_hops[i] = links.send(pg.at[:, lanes_of(there)], prb[i], axis, bit)

    def add_small(i):
        links.sent_done(small_hops[i])
        pg[:, lanes_of(hops[i][3])] += prb[i][...]

    def block_output():
        need("dx")
        own_rows(sums["br"])
        kx[0:rows, :] = (x_ref[...].astype(f32) + tmp[...] + params_ref[5:6, :] + params_ref[6:7, :]).astype(bf16)
        fetch("y", kx.at[pl.ds(0, rows), :], y_out)

    def end():
        pg_out[...] = pg[:, lanes_of((base, size))]
        need("y")
        for copy in slots[-own.shape[0] :]:
            copy.wait()
        links.finish()

    greet(dbits, tbits)
    plain = {
        "load0": lambda: need("o", "dy", "h"),
        "load1": load_more,
        "w1load": lambda: fetch("w1", w1_hbm, hw1),
        "hload": lambda: fetch("h", h_hbm, hw1),
        "nload": load_n,
        "dnout": norm_back,
        "brout": block_output,
        "end": end,
    }
    of_unit = {"away": away, "home": home, "f1": fold_first, "f2": fold_last}
    send_unit = {"y": send_y, "h": send_high, "z": send_sub}
    of_sum = {
        "31": lambda t: far_rows(t, 1), "30": lambda t: far_rows(t, 0), "01": near_rows, "00": keep_rows,
        "own": partner_rows,
    }
    send_sum = {
        "c1": lambda t: send_core(t, 1), "c0": lambda t: send_core(t, 0), "b": lambda t: send_x(t, 1),
        "a": lambda t: send_x(t, 0), "s": send_last,
    }
    wait_sum = {"c1": ("c", 1), "c0": ("c", 0), "b": ("x", 1), "a": ("x", 0), "s": "s"}
    for name in reduce_schedule(count, units, len(hops)):
        kind, _, rest = name.partition("_")
        if name in plain:
            plain[name]()
        elif kind in of_unit:
            of_unit[kind](units[rest])
        elif name[:2] == "dh":
            hidden_back(int(name[2:]))
        elif name[0] == "g":
            add_small(int(name[1:]))
        elif name[:2] == "SG":
            send_small(int(name[2:]))
        elif name[:2] == "WG":
            small_hops[int(name[2:])].wait_recv()
        elif name[0] == "S" and name[1:3] in sums:
            send_sum[name[3:]](sums[name[1:3]])
        elif name[0] == "W" and name[1:3] in sums:
            sums[name[1:3]].hops[wait_sum[name[3:]]].wait_recv()
        elif name[0] == "S":
            send_unit[name[1]](units[name[2:]])
        elif name[0] == "W":
            unit = units[name[2:]]
            unit.hop.wait_recv()
            if name[1] in "yh":
                load_received(unit, ry if name[1] == "y" else rz[0])
        else:
            of_sum[name[2:]](sums[name[:2]])


REDUCE_ORDER = [
    0, 5, 6, 8, 11, 1, 4, 2, 17, 9, 19, 7, 43, 13, 44, 45, 16, 20, 3, 18, 14, 46, 10, 21, 47, 48, 12, 22, 15,
    23, 58, 24, 40, 59, 60, 26, 41, 42, 25, 28, 29, 27, 49, 39, 61, 73, 50, 51, 74, 62, 63, 31, 55, 52, 30,
    79, 56, 53, 54, 75, 57, 38, 80, 91, 70, 92, 32, 33, 34, 64, 71, 110, 81, 111, 112, 76, 95, 93, 116, 82,
    94, 117, 65, 118, 96, 83, 107, 77, 97, 98, 66, 67, 72, 108, 36, 85, 164, 131, 86, 109, 84, 68, 165, 69,
    87, 88, 100, 119, 120, 99, 121, 132, 78, 35, 101, 137, 102, 103, 37, 128, 122, 149, 123, 89, 124, 150,
    151, 138, 152, 113, 114, 129, 90, 115, 171, 125, 133, 105, 126, 143, 167, 127, 153, 154, 155, 144, 145,
    134, 156, 139, 157, 158, 159, 104, 160, 140, 161, 141, 142, 130, 172, 135, 136, 162, 163, 173, 174, 146,
    169, 147, 148, 106, 166, 170, 175, 168, 176,
]


def reduce_schedule(count, units, hops):
    names = ["load0", "load1"]
    early = [u for u in units if u[0] in "oa"]
    late = [u for u in units if u[0] in "cq"]

    def start(group):
        for u in group:
            names.extend(["away_" + u, "Sy" + u, "home_" + u])

    def fold(group):
        for u in group:
            names.extend(["Wy" + u, "f1_" + u, "Sh" + u])
        for u in group:
            names.extend(["Wh" + u, "f2_" + u, "Sz" + u])

    def total(k):
        for part in ("31", "Sc1", "30", "Sc0", "Wc1", "Wc0", "01", "Sb", "Sa", "00", "Wb", "own", "Ss", "Ws", "Wa", "out"):
            names.append(part[0] + k + part[1:] if part[0] in "SW" else k + part)

    start(early)
    names.extend("dh%d" % c for c in range(4))
    names.append("w1load")
    total("dn")
    names.extend(["hload", "nload"])
    fold(early)
    start(late)
    total("br")
    fold(late)
    for i in range(hops):
        names.extend(["SG%d" % i, "WG%d" % i, "g%d" % i])
    names.extend("Wz" + u for u in units)
    names.append("end")
    if count == 8 and len(units) == 12 and hops == 5:
        return [names[i] for i in REDUCE_ORDER]
    return names


def reduce_call(dbits, tbits, x, dy, params, back_sum, sums, gathered):
    normed, back_rows, wq, w1, wo, w2, hidden_act, slope, attended, proj_back = gathered
    count = 1 << dbits
    blk = D // count
    rows = x.shape[0]
    tokens = normed.shape[0]
    width, hidden = wo.shape[0], w2.shape[0]
    total = 4 * width + 2 * hidden
    half, quarter = tokens // 2, tokens // 4
    any_spec = pl.BlockSpec(memory_space=pl.ANY)
    vm = pl.BlockSpec(memory_space=pltpu.VMEM)
    shape = lambda s, t=bf16: jax.ShapeDtypeStruct(s, t)
    vmem = lambda s, t=bf16: pltpu.VMEM(s, t)
    prb, size = [], D
    for _ in range(dbits):
        size = size // 2 if size >= 256 else size
        prb.append(vmem((16, size), f32))
    prb += [vmem((16, size), f32)] * tbits
    outs = [
        shape((rows, D)),
        shape((rows, D), f32),
        shape((total, blk), f32),
        shape((total, blk)),
        shape((16, size), f32),
        shape((total, D // 2)),
    ]
    outs += [shape((half, D)), shape((quarter, D)), shape((rows, D))] * 2
    outs += [shape((total, D >> (2 + k))) for k in range(dbits - 2)]
    scratch = [
        vmem((tokens, D)),
        vmem((tokens, hidden)),
        vmem((tokens, hidden)),
        vmem((hidden, D)),
        vmem((width, D)),
        vmem((D, 3 * width)),
        vmem((tokens, width)),
        vmem((tokens, 3 * width)),
        vmem((total - hidden, D // 2)),
        vmem((total, D // 2)),
        vmem((2, width, blk), f32),
        vmem((3, width, D // 2)),
        vmem((quarter, D)),
        vmem((quarter, D)),
        vmem((rows, D)),
        vmem((quarter, D)),
        vmem((quarter, D)),
        vmem((rows, D), f32),
        vmem((16, D), f32),
        vmem((8, hidden), f32),
        pltpu.SemaphoreType.DMA((80,)),
        pltpu.SemaphoreType.DMA((80,)),
        pltpu.SemaphoreType.DMA((160,)),
    ] + prb
    if blk % 128:
        scratch.append(vmem((total, blk)))
    return pl.pallas_call(
        functools.partial(reduce_kernel, (dbits, tbits)),
        out_shape=outs,
        in_specs=[vm] * 5 + [any_spec] * 10,
        out_specs=[any_spec] * 4 + [vm] + [any_spec] * (len(outs) - 5),
        scratch_shapes=scratch,
        compiler_params=pltpu.CompilerParams(
            vmem_limit_bytes=62 * 2**20, collective_id=1, has_side_effects=True
        ),
        cost_estimate=pl.CostEstimate(flops=5 * 10**10, bytes_accessed=10**8, transcendentals=10**6),
        name="reduce",
    )(x, dy, params, back_sum, sums, *gathered)


def adam_matrix(weight, first, second, grad):
    first_new = beta_first * first + (1.0 - beta_first) * grad
    second_new = beta_second * second + (1.0 - beta_second) * grad * grad
    root = jnp.sqrt(second_new * (1.0 / (1.0 - beta_second**STEP))) + adam_eps
    change = (first_new * (matrix_rate / (1.0 - beta_first**STEP))) / root
    return (weight * (1.0 - matrix_rate * weight_decay) - change, first_new, second_new)


def adam_kernel(plans, me_ref, *refs):
    sub = (me_ref[0] >> SUB_BIT) & 1
    step = pl.program_id(0)
    count = len(plans)
    ins, outs = refs[: 5 * count], refs[5 * count :]
    for k, (begin, half, turned) in enumerate(plans):
        w_ref, m_ref, v_ref, own_ref, recv_ref = ins[5 * k : 5 * k + 5]
        wo_ref, mo_ref, vo_ref = outs[3 * k : 3 * k + 3]

        @pl.when((step >= begin) & (step < begin + 2 * half))
        def _():
            mine = ((step - begin) // half) == sub
            grad = jnp.where(mine, own_ref[...], recv_ref[...].astype(f32))
            grad = (grad.T if turned else grad).reshape(w_ref.shape)
            wo_ref[...], mo_ref[...], vo_ref[...] = adam_matrix(w_ref[...], m_ref[...], v_ref[...], grad)


def adam_call(me, matrices, own, recv):
    blk = own.shape[1]
    plans, operands, in_specs, out_specs, out_shape = [], [], [], [], []
    begin = 0
    for weight, first, second, start, rows, turned in matrices:
        shape = weight.shape
        half = shape[0] if len(shape) == 3 else shape[1 if turned else 0] // (2 * rows)

        def at(i, begin=begin, half=half):
            return jnp.clip(i - begin, 0, 2 * half - 1)

        def grad_at(own, base=start // rows, at=at, half=half):
            def index(i, me_ref):
                sub = (me_ref[0] >> SUB_BIT) & 1
                skip = sub * half if own else (1 - sub) * half
                return (base + jnp.clip(at(i) - skip, 0, half - 1), 0)

            return pl.BlockSpec((rows, blk), index)

        if len(shape) == 3:
            full = pl.BlockSpec((1, blk, rows), lambda i, _, at=at, half=half: (at(i) % half, 0, at(i) // half))
        elif turned:
            full = pl.BlockSpec((blk, rows), lambda i, _, at=at: (0, at(i)))
        else:
            full = pl.BlockSpec((rows, blk), lambda i, _, at=at: (at(i), 0))
        plans.append((begin, half, turned))
        operands += [weight, first, second, own, recv]
        in_specs += [full] * 3 + [grad_at(True), grad_at(False)]
        out_specs += [full] * 3
        out_shape += [jax.ShapeDtypeStruct(shape, f32)] * 3
        begin += 2 * half
    return tuple(
        pl.pallas_call(
            functools.partial(adam_kernel, plans),
            grid_spec=pltpu.PrefetchScalarGridSpec(
                num_scalar_prefetch=1, grid=(begin,), in_specs=in_specs, out_specs=out_specs
            ),
            out_shape=out_shape,
            compiler_params=vmem_params(60),
            name="adam",
        )(me, *operands)
    )


def per_device(
    inputs,
    segments,
    cotangent,
    qkv_weight,
    qkv_first,
    qkv_second,
    dense_weight,
    dense_first,
    dense_second,
    expand_weight,
    expand_first,
    expand_second,
    shrink_weight,
    shrink_first,
    shrink_second,
    small_params,
    small_first,
    small_second,
):
    dp = lax.axis_size("dp")
    tensor_count = lax.axis_size("tensor")
    dbits = dp.bit_length() - 1
    tbits = tensor_count.bit_length() - 1
    d_me = lax.axis_index("dp")
    t_me = lax.axis_index("tensor")
    sub = (d_me >> SUB_BIT) & 1
    order = place_order(dp)
    high_bits = list(range(2, dbits))
    gather_bits = high_bits + [ROW_BIT]
    rows = inputs.shape[0]
    me = jnp.stack([d_me, t_me]).astype(jnp.int32)

    small_low = jnp.pad(small_params.astype(bf16), ((0, 16 - small_params.shape[0]), (0, 0)))
    ids = jnp.broadcast_to(segments, (8, rows))
    (
        normed, back_rows, qkv_wide, expand_full, dense_full, shrink_full, hidden_act, gelu_slope, attended, proj_back,
        params, back_sum, sums,
    ) = gather_call(
        dbits, tbits, inputs, cotangent, ids, small_low, qkv_weight, expand_weight, dense_weight, shrink_weight
    )
    width, hidden = dense_full.shape[0], shrink_full.shape[0]
    gathered = (
        normed, back_rows, qkv_wide, expand_full, dense_full, shrink_full, hidden_act, gelu_slope, attended, proj_back,
    )
    output, input_grad, own, recv, small_sum, *_ = reduce_call(
        dbits, tbits, inputs, cotangent, params, back_sum, sums, gathered
    )
    blk = D // dp
    if small_sum.shape[1] > blk:
        small_sum = lax.dynamic_slice_in_dim(small_sum, (d_me % (small_sum.shape[1] // blk)) * blk, blk, 1)
    small_sum = small_sum[: small_params.shape[0]]
    block = min(512, hidden)
    new = adam_call(
        me,
        [
            (shrink_weight, shrink_first, shrink_second, 0, block, False),
            (expand_weight, expand_first, expand_second, hidden, block, True),
            (qkv_weight, qkv_first, qkv_second, 2 * hidden, width, True),
            (dense_weight, dense_first, dense_second, 2 * hidden + 3 * width, width, False),
        ],
        own,
        recv,
    )
    shrink_new, expand_new, qkv_new, dense_new = new[0:3], new[3:6], new[6:9], new[9:12]
    small_new = adam_update(small_params, small_first, small_second, small_sum, vector_rate, 0.0)
    return (output, input_grad) + qkv_new + dense_new + expand_new + shrink_new + small_new


def solution(mesh):
    token_spec = P(("dp", "tensor"), None)
    qkv_spec = P(None, "dp", "tensor")
    row_spec = P("tensor", "dp")
    column_spec = P("dp", "tensor")
    small_spec = P(None, "dp")
    weight_specs = (qkv_spec,) * 3 + (row_spec,) * 3 + (column_spec,) * 3 + (row_spec,) * 3 + (small_spec,) * 3
    return jax.shard_map(
        per_device,
        mesh=mesh,
        in_specs=(token_spec, P("dp", "tensor"), token_spec) + weight_specs,
        out_specs=(token_spec, token_spec) + weight_specs,
        check_vma=False,
    )
```

```python
import functools
import jax
import numpy as np
import jax.numpy as jnp
from jax import lax
from jax.experimental import pallas as pl
from jax.experimental.pallas import tpu as pltpu
from jax.sharding import PartitionSpec as P

D = 2048
HD = 64
ROT = 32
FF = 8192
STEP = 10

norm_eps = 1e-05
beta_first = 0.9
beta_second = 0.95
adam_eps = 1e-08
weight_decay = 0.1
matrix_rate = 0.05
vector_rate = 1.0
masked_score = -1e30

SUB_BIT = 1
ROW_BIT = 0

bf16 = jnp.bfloat16
f32 = jnp.float32


def exchange(values, axis, bit):
    count = lax.axis_size(axis)
    return lax.ppermute(values, axis, [(i, i ^ (1 << bit)) for i in range(count)])


def place_order(count):
    bits = count.bit_length() - 1
    order = []
    for p in range(count):
        high = (p >> 1) & ((1 << (bits - 2)) - 1)
        order.append(((p & 1) << SUB_BIT) | (high << 2) | ((p >> (bits - 1)) << ROW_BIT))
    return order


def adam_update(weight, first, second, grad, rate, decay):
    first_new = beta_first * first + (1.0 - beta_first) * grad
    second_new = beta_second * second + (1.0 - beta_second) * grad * grad
    first_hat = first_new / (1.0 - beta_first**STEP)
    second_hat = second_new / (1.0 - beta_second**STEP)
    weight_new = weight - rate * (first_hat / (jnp.sqrt(second_hat) + adam_eps) + decay * weight)
    return (weight_new, first_new, second_new)


def after(values, *others):
    return lax.optimization_barrier((values,) + others)[0]


def gelu_value(pre_values):
    return jax.nn.gelu(pre_values, approximate=True)


def vmem_params(mib):
    return pltpu.CompilerParams(vmem_limit_bytes=mib * 2**20)


def place_of(block, count):
    bits = count.bit_length() - 1
    return ((block >> SUB_BIT) & 1) | ((block >> 2) << 1) | (((block >> ROW_BIT) & 1) << (bits - 1))


def move_blocks(count, source, load, store):
    width = D // count
    if width % 128 == 0:
        for j in range(count):
            start = pl.multiple_of(source(j) * width, width)
            store(pl.ds(j * width, width), load(pl.ds(start, width)))
        return
    for unit in range(count // 2):
        parts = []
        for half in range(2):
            block = source(2 * unit + half)
            value = load(pl.ds(pl.multiple_of((block >> 1) * 128, 128), 128))
            parts.append(pltpu.roll(value, ((block & 1) ^ half) * 64, 1))
        lane = lax.broadcasted_iota(jnp.int32, parts[0].shape, 1)
        store(pl.ds(unit * 128, 128), jnp.where(lane < 64, parts[0], parts[1]))


def smem_spec():
    return pl.BlockSpec(memory_space=pltpu.SMEM)


def assemble(order, me, keep_ref, recv_ref, tmp):
    count = len(order)

    def store(lanes, value):
        tmp[:, lanes] = value

    def add(lanes, value):
        tmp[:, lanes] += value

    move_blocks(count, lambda j: place_of(j ^ me, count), lambda lanes: keep_ref[:, lanes].astype(f32), store)
    move_blocks(count, lambda j: place_of(j ^ me, count) ^ 1, lambda lanes: recv_ref[:, lanes].astype(f32), add)


def swap_rotary(values):
    lane = lax.broadcasted_iota(jnp.int32, values.shape, 1)
    half = ROT // 2
    return jnp.where(
        lane % ROT < half, pltpu.roll(values, 128 - half, 1), pltpu.roll(values, half, 1)
    )


def dot_nn(a, b):
    return lax.dot_general(a, b, (((1,), (0,)), ((), ())), preferred_element_type=f32)


def dot_nt(a, b):
    return lax.dot_general(a, b, (((1,), (1,)), ((), ())), preferred_element_type=f32)


def dot_tn(a, b):
    return lax.dot_general(a, b, (((0,), (0,)), ((), ())), preferred_element_type=f32)


def rel_index(rel, seq, tbits):
    index = seq
    for b in range(tbits):
        index = index | (((rel >> b) & 1) << (tbits - b))
    return index


def mask_bias(bias, start_row, qb, rows):
    kend = (qb + 1) * rows
    key = lax.broadcasted_iota(jnp.int32, (kend, rows), 0)
    query = lax.broadcasted_iota(jnp.int32, (kend, rows), 1) + qb * rows
    bias[:kend, :] = jnp.where((key >= start_row) & (key <= query), 0.0, masked_score)


def attend_rows(qkv, lse, bias, o, seq, qb, width, out_rows):
    rows = bias.shape[1]
    kend = (qb + 1) * rows
    place = slice(qb * rows, kend)
    lane = lax.broadcasted_iota(jnp.int32, (rows, 128), 1)
    zero = jnp.zeros((rows, 128), bf16)

    def pair_body(pair, carry):
        base = pl.multiple_of(pair * 128, 128)
        q = qkv[seq, place, pl.ds(base, 128)] * jnp.asarray(HD ** (-0.5), bf16)
        k = qkv[seq, :kend, pl.ds(base + width, 128)]
        v = qkv[seq, :kend, pl.ds(base + 2 * width, 128)]
        vt = v.T
        outs = []
        for h in range(2):
            mine = (lane < HD) if h == 0 else (lane >= HD)
            s = dot_nt(k, jnp.where(mine, q, zero)) + bias[:kend, :]
            peak = jnp.max(s, axis=0, keepdims=True)
            expo = jnp.exp(s - peak)
            total = jnp.sum(expo, axis=0, keepdims=True)
            weights = (expo * (1.0 / total)).astype(bf16)
            outs.append(dot_nn(vt[h * HD : (h + 1) * HD, :], weights))
            lse[seq, pl.ds(pair * 2 + h, 1), place] = peak + jnp.log(total)
        o[out_rows, pl.ds(base, 128)] = jnp.concatenate(outs, axis=0).T.astype(bf16)
        return carry

    lax.fori_loop(0, width // 128, pair_body, 0)


def attend_back_rows(qkv, lse, bias, do, cosb, sinb, dk, dv, dp, sums, seq, qb, width, out_rows):
    rows = bias.shape[1]
    kend = (qb + 1) * rows
    place = slice(qb * rows, kend)
    scale = HD ** (-0.5)
    lane = lax.broadcasted_iota(jnp.int32, (rows, 128), 1)
    zero = jnp.zeros((rows, 128), bf16)

    def pair_body(pair, carry):
        base = pl.multiple_of(pair * 128, 128)
        lanes = pl.ds(base, 128)
        q = qkv[seq, place, lanes]
        k = qkv[seq, :kend, pl.ds(base + width, 128)]
        v = qkv[seq, :kend, pl.ds(base + 2 * width, 128)]
        kt = k.T
        dout = do[out_rows, lanes]
        outs = []
        for h in range(2):
            mine = (lane < HD) if h == 0 else (lane >= HD)
            qm = jnp.where(mine, q, zero) * jnp.asarray(scale, bf16)
            dom = jnp.where(mine, dout, zero)
            s = dot_nt(k, qm) + bias[:kend, :]
            probs = jnp.exp(s - lse[seq, pl.ds(pair * 2 + h, 1), place])
            dprobs = dot_nt(v, dom)
            inner = jnp.sum(probs * dprobs, axis=0, keepdims=True)
            ds = (probs * (dprobs - inner)).astype(bf16)
            dv[:kend, lanes] += dot_nn(probs.astype(bf16), dom)
            dk[:kend, lanes] += dot_nn(ds, qm)
            outs.append(dot_nn(kt[h * HD : (h + 1) * HD, :], ds))
        dq = jnp.concatenate(outs, axis=0).T * scale
        dq = dq * cosb[seq, place, :] - swap_rotary(dq) * sinb[seq, place, :]
        dq = dq.astype(bf16)
        dp[out_rows, lanes] = dq
        sums[0:1, lanes] += jnp.sum(dq.astype(f32), axis=0, keepdims=True)
        return carry

    lax.fori_loop(0, width // 128, pair_body, 0)


def attend_back_keys(cosb, sinb, dk, dv, dp, sums, seq, b, width, out_rows):
    rows = out_rows.size
    place = slice(b * rows, (b + 1) * rows)
    cosine = cosb[seq, place, :]
    sine = sinb[seq, place, :]
    for j in range(width // 128):
        lanes = slice(j * 128, (j + 1) * 128)
        part = dk[place, lanes]
        part = (part * cosine - swap_rotary(part) * sine).astype(bf16)
        kl = slice(width + j * 128, width + (j + 1) * 128)
        dp[out_rows, kl] = part
        sums[0:1, kl] += jnp.sum(part.astype(f32), axis=0, keepdims=True)
        part = dv[place, lanes].astype(bf16)
        vl = slice(2 * width + j * 128, 2 * width + (j + 1) * 128)
        dp[out_rows, vl] = part
        sums[0:1, vl] += jnp.sum(part.astype(f32), axis=0, keepdims=True)


class Links:
    def __init__(self, send_sems, recv_sems, local_sems):
        self.send_sems, self.recv_sems, self.local_sems = send_sems, recv_sems, local_sems
        self.sent, self.count, self.locals = [], 0, 0

    def send(self, src, dst, axis, bit):
        partner = lax.axis_index(axis) ^ (1 << bit)
        i = self.count
        self.count += 1
        copy = pltpu.make_async_remote_copy(
            src_ref=src,
            dst_ref=dst,
            send_sem=self.send_sems.at[i],
            recv_sem=self.recv_sems.at[i],
            device_id={axis: partner},
            device_id_type=pl.DeviceIdType.MESH,
        )
        copy.start()
        self.sent.append(copy)
        return copy

    def local(self, src, dst):
        copy = pltpu.make_async_copy(src, dst, self.local_sems.at[self.locals])
        self.locals += 1
        copy.start()
        return copy

    def local_wait(self, src, dst):
        self.local(src, dst).wait()

    def sent_done(self, copy):
        copy.wait_send()
        self.sent = [other for other in self.sent if other is not copy]

    def finish(self):
        for copy in self.sent:
            copy.wait_send()


def greet(dbits, tbits):
    barrier = pltpu.get_barrier_semaphore()
    partners = [("dp", b) for b in range(dbits)] + [("tensor", b) for b in range(tbits)]
    for axis, bit in partners:
        pl.semaphore_signal(
            barrier,
            inc=1,
            device_id={axis: lax.axis_index(axis) ^ (1 << bit)},
            device_id_type=pl.DeviceIdType.MESH,
        )
    pl.semaphore_wait(barrier, len(partners))


class Gathered:
    def __init__(self, links, slot, count, bits, outgoing):
        self.links, self.slot, self.bits, self.outgoing = links, slot, bits, outgoing
        self.left = count - 1
        self.coming = {}

    def source(self, p):
        size = 1 << (p.bit_length() - 1)
        return p - size, self.bits[p.bit_length() - 1]

    def send(self, p):
        src, bit = self.source(p)
        ref = self.outgoing if p == 1 else self.slot(src)
        self.coming[p] = self.links.send(ref, self.slot(p), "dp", bit)

    def wait(self, p):
        self.coming[p].wait_recv()
        self.left -= 1


class GatheredPairs(Gathered):
    def __init__(self, links, slot, count, bits, outgoing, own, received):
        super().__init__(links, slot, count, bits, outgoing)
        self.own, self.received = own, received

    def send(self, p):
        src, bit = self.source(p)
        if p == 1:
            self.coming[p] = self.links.send(self.outgoing, self.received, "dp", bit)
        elif p % 2 == 0 and src > 0:
            self.coming[p] = self.links.send(self.slot(src // 2), self.slot(p // 2), "dp", bit)

    def wait(self, p):
        if p == 1:
            self.coming[p].wait_recv()
            both = [self.own[...].astype(f32), self.received[...].astype(f32)]
            self.slot(0)[...] = jnp.concatenate(both, axis=1).astype(bf16)
            for later in range(1, len(self.bits)):
                bit = self.bits[later]
                self.coming[1 << later] = self.links.send(self.slot(0), self.slot(1 << (later - 1)), "dp", bit)
        elif p % 2 == 0:
            self.coming[p].wait_recv()
        self.left -= 1


def cast_store(dst, src):
    dst[...] = src[...].astype(bf16)


def gather_kernel(
    cfg,
    x_ref, dy_ref, ids_ref, small_ref, freq_ref, qkv_ref, w1_ref, wo_ref, w2_ref,
    n_out, dy_out, wq_out, w1_out, wo_out, w2_out, h_out, gp_out, o_out, dp_out, params_out, dysum_out, sums_out,
    n, dyb, wq, w1, wo, w2, sq, s1, so, s2, sta, stb, stc, std, tmp, nsw, pbuf, idb, cosb, sinb, startb,
    qkvb, lse, bias, o, do, dk, dv, dp, hst, gst, send_sems, recv_sems, local_sems, *pieces
):
    dbits, tbits = cfg
    order = place_order(1 << dbits)
    count = len(order)
    me = lax.axis_index("dp")
    me_t = lax.axis_index("tensor")
    sub = (me >> SUB_BIT) & 1
    rows = x_ref.shape[0]
    width = wo.shape[0]
    hidden = w2.shape[0]
    blk = D // count
    seqs = 2
    blocks = 1 << tbits
    length = rows * blocks
    links = Links(send_sems, recv_sems, local_sems)
    bits = [SUB_BIT] + list(range(2, dbits)) + [ROW_BIT]

    own_q = pl.ds(pl.multiple_of(sub * width, width), width)
    other_q = pl.ds(pl.multiple_of((1 - sub) * width, width), width)
    own_h = pl.ds(pl.multiple_of(sub * hidden, hidden), hidden)
    other_h = pl.ds(pl.multiple_of((1 - sub) * hidden, hidden), hidden)
    loads = {"q": [], "1": [], "2": [], "o": []}
    for j in range(3):
        lanes = pl.ds(j * width, width)
        loads["q"].append(links.local(qkv_ref.at[j, :, other_q], std.at[:, lanes]))
        loads["q"].append(links.local(qkv_ref.at[j, :, own_q], stc.at[:, lanes]))
    loads["2"].append(links.local(w2_ref.at[other_h, :], stb))
    loads["2"].append(links.local(w2_ref.at[own_h, :], sta))

    def row_gather(ref, outgoing):
        return Gathered(links, lambda p: ref.at[pl.ds(p * blk, blk), :], count, bits, outgoing)

    def column_gather(ref, outgoing, own, received):
        unit = max(blk, 128)
        slot = lambda p: ref.at[:, pl.ds(p * unit, unit)]
        if unit == blk:
            return Gathered(links, slot, count, bits, outgoing)
        return GatheredPairs(links, slot, count, bits, outgoing, own, received)

    gathers = {"q": row_gather(wq, sq), "1": row_gather(w1, s1)}
    gathers["o"] = column_gather(wo, so, *pieces[0:2])
    wo_own, w2_own = (wo.at[:, pl.ds(0, blk)], w2.at[:, pl.ds(0, blk)]) if blk % 128 == 0 else (pieces[0], pieces[2])
    outs = {"q": (wq, wq_out), "1": (w1, w1_out), "o": (wo, wo_out), "n": (n, n_out), "d": (dyb, dy_out)}
    for i in range(2):
        part = pl.ds(i * (hidden // 2), hidden // 2)
        extra = [piece.at[part, :] for piece in pieces[2:4]] if blk % 128 else [None, None]
        gathers["23"[i]] = column_gather(w2.at[part, :], s2.at[part, :], *extra)
        outs["23"[i]] = (w2.at[part, :], w2_out.at[part, :])
    token_bufs = {"n": n, "d": dyb}
    token_left = {"n": 2 * blocks - 1, "d": 2 * blocks - 1}
    coming, stores, kept, attended, begun = {}, [], {}, set(), set()

    def tok(ref, i):
        return ref.at[pl.ds(i * rows, rows), :]

    def send(kind, i):
        if kind in gathers:
            gathers[kind].send(i)
        elif kind in token_bufs:
            ref = token_bufs[kind]
            if i == 1:
                coming[kind, i] = links.send(nsw, tok(ref, 1), "dp", SUB_BIT)
            else:
                step = i.bit_length() - 1
                coming[kind, i] = links.send(tok(ref, i - (1 << step)), tok(ref, i), "tensor", tbits - step)
        else:
            buf = pbuf if kind == "P" else idb
            axis, bit = ("dp", bits[i - 1]) if kind == "P" or i == 1 else ("tensor", tbits + 1 - i)
            size = 1 << (i - 1)
            coming[kind, i] = links.send(buf.at[pl.ds(0, size)], buf.at[pl.ds(size, size)], axis, bit)

    def wait(kind, i):
        if kind in gathers:
            gathers[kind].wait(i)
            complete = gathers[kind].left == 0
        else:
            coming[kind, i].wait_recv()
            complete = False
            if kind in token_bufs:
                token_left[kind] -= 1
                complete = token_left[kind] == 0
        if complete:
            stores.append(links.local(*outs[kind]))

    def arrived(name):
        for copy in loads[name]:
            copy.wait()

    def cast_q():
        arrived("q")
        sq[...] = std[:, 0 : 3 * width].astype(bf16)
        wq[0:blk, :] = stc[:, 0 : 3 * width].astype(bf16)
        loads["1"].append(links.local(w1_ref.at[:, other_h], std))
        loads["1"].append(links.local(w1_ref.at[:, own_h], stc))

    def cast_1():
        arrived("1")
        s1[...] = std[...].astype(bf16)
        w1[0:blk, :] = stc[...].astype(bf16)

    def cast_2():
        arrived("2")
        s2[...] = stb[...].astype(bf16)
        w2_own[...] = sta[...].astype(bf16)
        loads["o"].append(links.local(wo_ref.at[other_q, :], stb.at[pl.ds(0, width), :]))
        loads["o"].append(links.local(wo_ref.at[own_q, :], sta.at[pl.ds(0, width), :]))

    def cast_o():
        arrived("o")
        so[...] = stb[0:width, :].astype(bf16)
        wo_own[...] = sta[0:width, :].astype(bf16)

    def statistics():
        x = x_ref[...].astype(f32)
        x = x - jnp.mean(x, axis=-1, keepdims=True)
        inv = lax.rsqrt(jnp.mean(x * x, axis=-1, keepdims=True) + norm_eps)
        tmp[...] = x * inv

    def store_to(ref):
        def store(lanes, value):
            ref[0:rows, lanes] = value.astype(bf16)

        return store

    load_tmp = lambda lanes: tmp[:, lanes]
    load_dy = lambda lanes: dy_ref[:, lanes].astype(f32)

    def norm():
        per = max(1, 128 // blk)
        for a in range(0, count, per):
            part = [pbuf[place_of((a + k) ^ me, count)].astype(f32) for k in range(per)]
            lanes = pl.ds(a * blk, per * blk)
            params_out[:, lanes] = part[0] if per == 1 else jnp.concatenate(part, axis=1)
        tmp[...] = tmp[...] * params_out[0:1, :] + params_out[1:2, :]
        move_blocks(count, lambda j: me ^ order[j ^ 1], load_tmp, store_to(nsw))
        move_blocks(count, lambda j: me ^ order[j], load_tmp, store_to(n))

    def back_own():
        move_blocks(count, lambda j: me ^ order[j], load_dy, store_to(dyb))
        dysum_out[...] = jnp.sum(dy_ref[...].astype(f32), axis=0, keepdims=True)

    def back_swapped():
        links.sent_done(coming["n", 1])
        move_blocks(count, lambda j: me ^ order[j ^ 1], load_dy, store_to(nsw))

    def tables():
        for seq in range(seqs):
            row = jnp.concatenate(
                [idb[rel_index(me_t ^ b, seq, tbits)][0:1, :] for b in range(blocks)], axis=1
            ).astype(f32)
            first = jnp.sum(jnp.where(row < 1.0, 1.0, 0.0), axis=1, keepdims=True)
            second = jnp.sum(jnp.where(row < 2.0, 1.0, 0.0), axis=1, keepdims=True)
            begin = jnp.where(row < 1.0, 0.0, jnp.where(row < 2.0, first, second))
            place = lax.broadcasted_iota(jnp.int32, (1, length), 1).astype(f32)
            startb[seq, 0:1, :] = begin.astype(jnp.int32)
            angle = freq_ref[:, 0:1] * (place - begin)
            cosine, sine = jnp.cos(angle), jnp.sin(angle)
            rest = (HD - ROT, length)
            cosine = jnp.concatenate([cosine, cosine, jnp.ones(rest, f32)], axis=0)
            sine = jnp.concatenate([-sine, sine, jnp.zeros(rest, f32)], axis=0)
            cosb[seq] = jnp.concatenate([cosine, cosine], axis=0).T
            sinb[seq] = jnp.concatenate([sine, sine], axis=0).T

    head_start = me_t * (2 * width) + sub * width
    hidden_start = me_t * (2 * hidden) + sub * hidden
    pairs = width // 128

    def two_blocks(c):
        return pl.ds(2 * c * rows, 2 * rows)

    def project(c):
        lanes = pl.ds(pl.multiple_of(head_start, width), width)
        qkv_bias = [params_out[2 + j : 3 + j, lanes] for j in range(3)]
        rel = sum(((c >> (tbits - 1 - b)) & 1) << b for b in range(tbits))
        block = me_t ^ rel
        place = pl.ds(pl.multiple_of(block * rows, rows), rows)
        part = dot_nn(n[two_blocks(c), :], wq[...])
        for seq in range(seqs):
            seq_rows = slice(seq * rows, (seq + 1) * rows)
            cosine, sine = cosb[seq, place, :], sinb[seq, place, :]
            for j in range(3 * pairs):
                kind, pair = j // pairs, j % pairs
                value = part[seq_rows, j * 128 : (j + 1) * 128] + qkv_bias[kind][:, pair * 128 : (pair + 1) * 128]
                if kind < 2:
                    value = value * cosine + swap_rotary(value) * sine
                qkvb[seq, place, j * 128 : (j + 1) * 128] = value.astype(bf16)

    def seq_rows_of(seq, b):
        return pl.ds(pl.multiple_of(rel_index(me_t ^ b, seq, tbits) * rows, rows), rows)

    def attend(seq, qb):
        mask_bias(bias, startb[seq, 0:1, qb * rows : (qb + 1) * rows], qb, rows)
        attend_rows(qkvb, lse, bias, o, seq, qb, width, seq_rows_of(seq, qb))
        attended.add((seq, qb))
        if len(attended) == seqs * blocks:
            stores.append(links.local(o, o_out))

    def attend_back(seq, qb):
        if seq not in begun:
            begun.add(seq)
            dk[...] = jnp.zeros_like(dk)
            dv[...] = jnp.zeros_like(dv)
        mask_bias(bias, startb[seq, 0:1, qb * rows : (qb + 1) * rows], qb, rows)
        attend_back_rows(
            qkvb, lse, bias, do, cosb, sinb, dk, dv, dp, sums_out, seq, qb, width, seq_rows_of(seq, qb)
        )

    def attend_keys(seq):
        for b in range(blocks):
            attend_back_keys(cosb, sinb, dk, dv, dp, sums_out, seq, b, width, seq_rows_of(seq, b))

    tile = hst.shape[2]

    def hide(c):
        row = 7 + hidden_start // D
        hidden_bias = params_out[pl.ds(row, 1), pl.ds(pl.multiple_of(hidden_start % D, hidden), hidden)]
        for t in range(hidden // tile):
            lanes = pl.ds(t * tile, tile)
            slot = t % 2
            for copy in kept.pop(slot, ()):
                copy.wait()
            v = dot_nn(n[two_blocks(c), :], w1[:, lanes]) + hidden_bias[:, t * tile : (t + 1) * tile]
            root = 0.7978845608028654
            square = v * v
            th = jnp.tanh(root * (v + 0.044715 * v * square))
            hst[slot] = (0.5 * v * (1.0 + th)).astype(bf16)
            gst[slot] = (
                0.5 * (1.0 + th) + 0.5 * v * (1.0 - th * th) * (root * (1.0 + (3 * 0.044715) * square))
            ).astype(bf16)
            kept[slot] = (
                links.local(hst.at[slot], h_out.at[two_blocks(c), lanes]),
                links.local(gst.at[slot], gp_out.at[two_blocks(c), lanes]),
            )

    def output_back(c):
        do[two_blocks(c), :] = dot_nt(dyb[two_blocks(c), :], wo[...]).astype(bf16)

    def end():
        stores.append(links.local(dp, dp_out))
        for copies in kept.values():
            stores.extend(copies)
        for copy in stores:
            copy.wait()
        links.finish()

    pbuf[0] = small_ref[...]
    idb[0] = ids_ref[...]
    sums_out[...] = jnp.zeros_like(sums_out)
    greet(dbits, tbits)
    steps = {
        "castq": cast_q, "cast1": cast_1, "cast2": cast_2, "casto": cast_o, "stat": statistics, "ln": norm,
        "dyr": back_own, "dys": back_swapped, "table": tables, "end": end,
    }
    indexed = {"Q": project, "A": attend, "B": attend_back, "K": attend_keys, "H": hide, "D": output_back}
    for name in gather_schedule(count, blocks):
        if name in steps:
            steps[name]()
        elif name[0] == "S":
            send(name[1], int(name[2:]))
        elif name[0] == "W":
            wait(name[1], int(name[2:]))
        else:
            indexed[name[0]](*[int(i) for i in name[1:]])


GATHER_ORDER = [
    6, 0, 14, 29, 1, 2, 30, 7, 8, 9, 3, 75, 4, 78, 12, 31, 44, 49, 5, 13, 92, 15, 47, 32, 34, 16, 33, 17, 18,
    35, 40, 36, 48, 37, 38, 39, 46, 45, 61, 10, 19, 20, 50, 57, 41, 25, 42, 51, 11, 52, 91, 21, 26, 104, 43,
    105, 23, 62, 24, 119, 53, 22, 120, 86, 106, 121, 27, 54, 28, 122, 125, 129, 77, 90, 128, 55, 56, 130,
    126, 127, 63, 64, 67, 100, 58, 68, 59, 65, 123, 107, 111, 124, 108, 96, 110, 60, 109, 134, 112, 97, 66,
    131, 71, 76, 133, 113, 72, 114, 82, 93, 73, 83, 94, 95, 132, 115, 69, 116, 70, 79, 80, 118, 117, 81, 135,
    137, 136, 74, 138, 141, 139, 142, 98, 99, 140, 143, 147, 88, 84, 85, 146, 144, 145, 87, 148, 89, 102,
    103, 101, 149,
]


def gather_schedule(count, blocks):
    names = []

    def take(kind, places, first):
        def push(p):
            size = first
            while size < places:
                if p < size:
                    names.append("S%s%d" % (kind, p + size))
                size *= 2

        names.append("S%s1" % kind)
        push(0)
        for p in range(1, places):
            names.append("W%s%d" % (kind, p))
            push(p)

    for i in range(1, count.bit_length()):
        names.extend(["SP%d" % i, "WP%d" % i])
    for i in range(1, blocks.bit_length() + 1):
        names.extend(["SI%d" % i, "WI%d" % i])
    names.extend(["stat", "ln", "castq"])
    take("n", 2 * blocks, 2)
    take("q", count, 2)
    names.extend(["table", "cast1", "dyr", "dys"])
    take("1", count, 2)
    take("d", 2 * blocks, 2)
    names.append("cast2")
    take("2", count, 2)
    take("3", count, 2)
    names.append("casto")
    take("o", count, 2)
    names.extend("Q%d" % c for c in range(blocks))
    names.extend("A%d%d" % (s, b) for s in range(2) for b in range(blocks))
    names.extend("H%d" % c for c in range(blocks))
    names.extend("D%d" % c for c in range(blocks))
    for s in range(2):
        names.extend("B%d%d" % (s, b) for b in range(blocks))
        names.append("K%d" % s)
    names.append("end")
    if (count, blocks) == (8, 4):
        return [names[i] for i in GATHER_ORDER]
    return names


def gather_call(dbits, tbits, x, dy, ids, small, qkv_weight, expand_weight, dense_weight, shrink_weight):
    count = 1 << dbits
    blk = D // count
    rows = x.shape[0]
    width = qkv_weight.shape[2] // 2
    hidden = expand_weight.shape[1] // 2
    tokens = rows * (2 << tbits)
    length = rows << tbits
    heads = width // HD
    half = ROT // 2
    powers = (10000.0 ** (-np.arange(half) / half)).astype(np.float32)
    freqs = jnp.asarray(np.repeat(powers[:, None], 128, axis=1))
    any_spec = pl.BlockSpec(memory_space=pl.ANY)
    vm = pl.BlockSpec(memory_space=pltpu.VMEM)
    shape = lambda s, t=bf16: jax.ShapeDtypeStruct(s, t)
    vmem = lambda s, t=bf16: pltpu.VMEM(s, t)
    weights = 5 * (count - 1) + 4 * (2 << tbits) + 2 * (dbits + tbits) + 8
    scratch = [
        vmem((tokens, D)),
        vmem((tokens, D)),
        vmem((D, 3 * width)),
        vmem((D, hidden)),
        vmem((width, D)),
        vmem((hidden, D)),
        vmem((blk, 3 * width)),
        vmem((blk, hidden)),
        vmem((width, blk)),
        vmem((hidden, blk)),
        vmem((hidden, blk), f32),
        vmem((hidden, blk), f32),
        vmem((blk, hidden), f32),
        vmem((blk, hidden), f32),
        vmem((rows, D), f32),
        vmem((rows, D)),
        vmem((count, small.shape[0], blk)),
        vmem((2 << tbits, 8, rows), jnp.int32),
        vmem((2, length, 128), f32),
        vmem((2, length, 128), f32),
        vmem((2, 8, length), jnp.int32),
        vmem((2, length, 3 * width)),
        vmem((2, heads, length), f32),
        vmem((length, rows), f32),
        vmem((tokens, width)),
        vmem((tokens, width)),
        vmem((length, width), f32),
        vmem((length, width), f32),
        vmem((tokens, 3 * width)),
        vmem((2, 2 * rows, min(hidden, 512))),
        vmem((2, 2 * rows, min(hidden, 512))),
        pltpu.SemaphoreType.DMA((weights,)),
        pltpu.SemaphoreType.DMA((weights,)),
        pltpu.SemaphoreType.DMA((48,)),
    ]
    pieces = (vmem((width, blk)), vmem((hidden, blk)))
    scratch += [pieces[0]] * 2 + [pieces[1]] * 2 if blk % 128 else [vmem((16, 128))] * 4
    return pl.pallas_call(
        functools.partial(gather_kernel, (dbits, tbits)),
        out_shape=[
            shape((tokens, D)),
            shape((tokens, D)),
            shape((D, 3 * width)),
            shape((D, hidden)),
            shape((width, D)),
            shape((hidden, D)),
            shape((tokens, hidden)),
            shape((tokens, hidden)),
            shape((tokens, width)),
            shape((tokens, 3 * width)),
            shape((small.shape[0], D), f32),
            shape((1, D), f32),
            shape((8, 3 * width), f32),
        ],
        in_specs=[vm] * 5 + [any_spec] * 4,
        out_specs=[any_spec] * 10 + [vm] * 3,
        scratch_shapes=scratch,
        compiler_params=pltpu.CompilerParams(
            vmem_limit_bytes=62 * 2**20, collective_id=0, has_side_effects=True
        ),
        cost_estimate=pl.CostEstimate(flops=2 * 10**10, bytes_accessed=10**8, transcendentals=10**7),
        name="gather",
    )(x, dy, ids, small, freqs, qkv_weight, expand_weight, dense_weight, shrink_weight)


class Unit:
    def __init__(self, start, rows, lhs, first, rhs, send_start, frees):
        self.here, self.rows = pl.ds(start, rows), rows
        self.lhs, self.first, self.rhs = lhs, first, rhs
        self.out = pl.ds(send_start, rows)
        self.frees, self.hop, self.load, self.slot = frees, None, None, None


class TokenSum:
    def __init__(self, partial, far, near, keep, rc, rx, rs):
        self.partial, self.far, self.near, self.keep = partial, far, near, keep
        self.rc, self.rx, self.rs = rc, rx, rs
        self.hops = {}


def reduce_kernel(
    cfg,
    x_ref, dy_own_ref, params_ref, back_sum_ref, sums_ref,
    n_hbm, dy_hbm, wq_hbm, w1_hbm, wo_hbm, w2_hbm, h_hbm, gp_hbm, o_hbm, dp_hbm,
    y_out, dx_out, own_out, rl, pg_out, ry, rc1, rx1, rs1, rc2, rx2, rs2, *rest
):
    dbits, tbits = cfg
    highs = dbits - 2
    rz, rest = rest[:highs], rest[highs:]
    (
        big, hw1, gp, w2, wo, wq, o, dp, outgoing, keep, own, came, sx, kx, sz, sc, stage, tmp, pg, hsum,
        send_sems, recv_sems, local_sems, *rest
    ) = rest
    prb, last = rest[: dbits + tbits], rest[dbits + tbits :]
    order = place_order(1 << dbits)
    count = len(order)
    me = lax.axis_index("dp")
    me_t = lax.axis_index("tensor")
    sub = (me >> SUB_BIT) & 1
    rows = x_ref.shape[0]
    blk = D // count
    width, hidden = wo.shape[0], w2.shape[0]
    tokens = n_hbm.shape[0]
    links = Links(send_sems, recv_sems, local_sems)
    high_bits = list(range(2, dbits))
    side = D // 2
    half, quarter = tokens // 2, tokens // 4
    step_lanes = 512

    pending = {}

    def fetch(name, src, dst):
        pending.setdefault(name, []).append(links.local(src, dst))

    def need(*names):
        for name in names:
            for copy in pending.pop(name, ()):
                copy.wait()

    fetch("o", o_hbm, o)
    fetch("dy", dy_hbm, big)
    fetch("h", h_hbm, hw1)

    def load_more():
        fetch("w2", w2_hbm, w2)
        fetch("gp", gp_hbm, gp)
        fetch("dp", dp_hbm, dp)
        fetch("wq", wq_hbm, wq)
        fetch("wo", wo_hbm, wo)

    def load_n():
        for i in range(2):
            links.sent_done(sums["dn"].hops["c", i])
        for i in range(2):
            part = pl.ds(i * half, half)
            fetch("n", n_hbm.at[part, :], big.at[part, :])

    units = {"o": Unit(2 * hidden + 3 * width, width, o, 0, "dy", hidden + 3 * width, None)}
    per = hidden // width
    for i in range(per):
        at = i * width
        units["a%d" % i] = Unit(at, width, hw1, at, "dy", at, None)
        units["c%d" % i] = Unit(at + hidden, width, gp, at, "n", at, "a%d" % i)
    for j in range(3):
        at = hidden + j * width
        units["q%d" % j] = Unit(at + hidden, width, dp, j * width, "n", at, None)

    def product(unit, part):
        need(unit.rhs, *(["dp"] if unit.lhs is dp else ["h"] if unit.lhs is hw1 else ["o"]))
        lhs = unit.lhs[:, pl.ds(unit.first, unit.rows)]
        return dot_tn(lhs, big[:, pl.ds(part * side, side)]).astype(bf16)

    def away(unit):
        if unit.frees:
            links.sent_done(units[unit.frees].first_hop)
        outgoing[unit.out, :] = product(unit, 1)

    def home(unit):
        keep[unit.here, :] = product(unit, 0)

    def send_y(unit):
        unit.hop = links.send(outgoing.at[unit.out, :], ry.at[unit.here, :], "dp", ROW_BIT)
        unit.first_hop = unit.hop

    free = list(range(came.shape[0]))

    def load_received(unit, src):
        if free:
            unit.slot = free.pop()
            part = came.at[unit.slot, :, pl.ds(0, src.shape[1])]
            unit.load = links.local(src.at[unit.here, :], part)

    def add_received(unit, src):
        lanes = src.shape[1]
        value = keep[unit.here, 0:lanes].astype(f32)
        if unit.load is None:
            part = stage.at[pl.ds(0, unit.rows), pl.ds(0, lanes)]
            links.local_wait(src.at[unit.here, :], part)
            return value + part[...].astype(f32)
        unit.load.wait()
        unit.load = None
        free.append(unit.slot)
        return value + came[unit.slot, :, 0:lanes].astype(f32)

    def fold_first(unit):
        keep[unit.here, :] = add_received(unit, ry).astype(bf16)

    def send_high(unit, k=0):
        lanes = side >> (k + 1)
        part = keep.at[unit.here, pl.ds(lanes, lanes)]
        unit.hop = links.send(part, rz[k].at[unit.here, :], "dp", high_bits[highs - 1 - k])

    slots = []

    def fold_last(unit):
        for k in range(highs - 1):
            keep[unit.here, 0 : side >> (k + 1)] = add_received(unit, rz[k]).astype(bf16)
            send_high(unit, k + 1)
            unit.hop.wait_recv()
        value = add_received(unit, rz[highs - 1])
        slot = len(slots) % own.shape[0]
        if len(slots) >= own.shape[0]:
            slots[-own.shape[0]].wait()
        own[slot] = value[:, 0:blk]
        slots.append(links.local(own.at[slot], own_out.at[unit.here, :]))
        if last:
            last[0][unit.here, :] = value[:, blk : 2 * blk].astype(bf16)
        else:
            keep[unit.here, blk : 2 * blk] = value[:, blk : 2 * blk].astype(bf16)

    def send_sub(unit):
        part = last[0].at[unit.here, :] if last else keep.at[unit.here, pl.ds(blk, blk)]
        unit.hop = links.send(part, rl.at[unit.here, :], "dp", SUB_BIT)

    hsum[...] = jnp.zeros_like(hsum)

    def hidden_back(c):
        need("dy", "w2", "gp")
        place = pl.ds(c * quarter, quarter)
        for t in range(0, hidden, 512):
            lanes = slice(t, t + 512)
            value = (dot_nt(big[place, :], w2[lanes, :]) * gp[place, lanes].astype(f32)).astype(bf16)
            gp[place, lanes] = value
            hsum[0:1, lanes] += jnp.sum(value.astype(f32), axis=0, keepdims=True)

    def branch(place, lanes):
        return dot_nn(o[place, :], wo[:, lanes]) + dot_nn(hw1[place, :], w2[:, lanes])

    def normed_back(place, lanes):
        return dot_nt(dp[place, :], wq[lanes, :]) + dot_nt(gp[place, :], hw1[lanes, :])

    def part_rows(partial, first, dst, added):
        place = pl.ds(first, quarter)

        def body(t, carry):
            lanes = pl.ds(pl.multiple_of(t * step_lanes, step_lanes), step_lanes)
            value = partial(place, lanes)
            if added is not None:
                value = value + added[:, lanes].astype(f32)
            dst[:, lanes] = value.astype(bf16)
            return carry

        lax.fori_loop(0, D // step_lanes, body, 0)

    big_rows = lambda first: big.at[pl.ds(first, quarter), :]
    sums = {
        "dn": TokenSum(normed_back, (big_rows(half), big_rows(half + quarter)), sx, kx, rc1, rx1, rs1),
        "br": TokenSum(branch, (sc, sc), sc, sx, rc2, rx2, rs2),
    }

    def far_rows(t, i):
        need("wo", "w2", "o", "h") if t is sums["br"] else need("dp", "wq", "w1")
        if t is sums["br"] and i == 0:
            links.sent_done(t.hops["c", 1])
        part_rows(t.partial, half + i * quarter, t.far[i], None)

    def send_core(t, i):
        there = pl.ds(i * quarter, quarter)
        t.hops["c", i] = links.send(t.far[i], t.rc.at[there, :], "tensor", 0)

    def near_rows(t):
        if t is sums["br"]:
            links.sent_done(t.hops["c", 0])
        links.local_wait(t.rc.at[pl.ds(quarter, quarter), :], stage)
        part_rows(t.partial, quarter, t.near, stage)

    def send_x(t, i):
        part = pl.ds(i * rows, rows)
        t.hops["x", i] = links.send(t.near.at[part, :], t.rx.at[part, :], "tensor", 1)

    def keep_rows(t):
        if t is sums["br"]:
            for i in range(2):
                links.sent_done(sums["dn"].hops["x", i])
        links.local_wait(t.rc.at[pl.ds(0, quarter), :], stage)
        part_rows(t.partial, 0, t.keep, stage)

    def partner_rows(t):
        if t is sums["br"]:
            links.sent_done(sums["dn"].hops["s"])
        links.local_wait(t.rx.at[pl.ds(rows, rows), :], stage.at[pl.ds(0, rows), :])
        sz[...] = (t.keep[rows : 2 * rows, :].astype(f32) + stage[0:rows, :].astype(f32)).astype(bf16)

    def send_last(t):
        t.hops["s"] = links.send(sz, t.rs, "dp", SUB_BIT)

    def own_rows(t):
        links.local_wait(t.rx.at[pl.ds(0, rows), :], stage.at[pl.ds(0, rows), :])
        t.keep[0:rows, :] = (t.keep[0:rows, :].astype(f32) + stage[0:rows, :].astype(f32)).astype(bf16)
        received = stage.at[pl.ds(rows, rows), :]
        links.local_wait(t.rs, received)
        assemble(order, me, t.keep.at[pl.ds(0, rows), :], received, tmp)

    def norm_back():
        own_rows(sums["dn"])
        pg[...] = jnp.zeros_like(pg)
        strip = 64

        def body(i, carry):
            place = pl.ds(pl.multiple_of(i * strip, strip), strip)
            x = x_ref[place, :].astype(f32)
            x = x - jnp.mean(x, axis=-1, keepdims=True)
            inv = lax.rsqrt(jnp.mean(x * x, axis=-1, keepdims=True) + norm_eps)
            x = x * inv
            back = tmp[place, :]
            pg[0:1, :] += jnp.sum(back * x, axis=0, keepdims=True)
            pg[1:2, :] += jnp.sum(back, axis=0, keepdims=True)
            e = back * params_ref[0:1, :]
            tmp[place, :] = dy_own_ref[place, :].astype(f32) + inv * (
                e - jnp.mean(e, axis=-1, keepdims=True) - x * jnp.mean(e * x, axis=-1, keepdims=True)
            )
            return carry

        lax.fori_loop(0, rows // strip, body, 0)
        fetch("dx", tmp, dx_out)
        head_start = me_t * (2 * width) + sub * width
        hidden_start = me_t * (2 * hidden) + sub * hidden
        lanes = pl.ds(pl.multiple_of(head_start, width), width)
        for j in range(3):
            pg[2 + j : 3 + j, lanes] = sums_ref[0:1, j * width : (j + 1) * width]
        pg[5:6, :] = back_sum_ref[...]
        pg[6:7, :] = back_sum_ref[...]
        pg[pl.ds(7 + hidden_start // D, 1), pl.ds(pl.multiple_of(hidden_start % D, hidden), hidden)] = hsum[0:1, :]

    hops, base, size = [], 0, D
    for bit in reversed(range(dbits)):
        mine = (me >> bit) & 1
        if size >= 256:
            size //= 2
            there = (base + (1 - mine) * size, size)
            base = base + mine * size
        else:
            there = (base, size)
        hops.append(("dp", bit, there, (base, size)))
    for bit in range(tbits):
        hops.append(("tensor", bit, (base, size), (base, size)))
    lanes_of = lambda at: pl.ds(pl.multiple_of(at[0], at[1]), at[1])
    small_hops = {}

    def send_small(i):
        axis, bit, there, _ = hops[i]
        small_hops[i] = links.send(pg.at[:, lanes_of(there)], prb[i], axis, bit)

    def add_small(i):
        links.sent_done(small_hops[i])
        pg[:, lanes_of(hops[i][3])] += prb[i][...]

    def block_output():
        need("dx")
        own_rows(sums["br"])
        kx[0:rows, :] = (x_ref[...].astype(f32) + tmp[...] + params_ref[5:6, :] + params_ref[6:7, :]).astype(bf16)
        fetch("y", kx.at[pl.ds(0, rows), :], y_out)

    def end():
        pg_out[...] = pg[:, lanes_of((base, size))]
        need("y")
        for copy in slots[-own.shape[0] :]:
            copy.wait()
        links.finish()

    greet(dbits, tbits)
    plain = {
        "load0": lambda: need("o", "dy", "h"),
        "load1": load_more,
        "w1load": lambda: fetch("w1", w1_hbm, hw1),
        "hload": lambda: fetch("h", h_hbm, hw1),
        "nload": load_n,
        "dnout": norm_back,
        "brout": block_output,
        "end": end,
    }
    of_unit = {"away": away, "home": home, "f1": fold_first, "f2": fold_last}
    send_unit = {"y": send_y, "h": send_high, "z": send_sub}
    of_sum = {
        "31": lambda t: far_rows(t, 1), "30": lambda t: far_rows(t, 0), "01": near_rows, "00": keep_rows,
        "own": partner_rows,
    }
    send_sum = {
        "c1": lambda t: send_core(t, 1), "c0": lambda t: send_core(t, 0), "b": lambda t: send_x(t, 1),
        "a": lambda t: send_x(t, 0), "s": send_last,
    }
    wait_sum = {"c1": ("c", 1), "c0": ("c", 0), "b": ("x", 1), "a": ("x", 0), "s": "s"}
    for name in reduce_schedule(count, units, len(hops)):
        kind, _, rest = name.partition("_")
        if name in plain:
            plain[name]()
        elif kind in of_unit:
            of_unit[kind](units[rest])
        elif name[:2] == "dh":
            hidden_back(int(name[2:]))
        elif name[0] == "g":
            add_small(int(name[1:]))
        elif name[:2] == "SG":
            send_small(int(name[2:]))
        elif name[:2] == "WG":
            small_hops[int(name[2:])].wait_recv()
        elif name[0] == "S" and name[1:3] in sums:
            send_sum[name[3:]](sums[name[1:3]])
        elif name[0] == "W" and name[1:3] in sums:
            sums[name[1:3]].hops[wait_sum[name[3:]]].wait_recv()
        elif name[0] == "S":
            send_unit[name[1]](units[name[2:]])
        elif name[0] == "W":
            unit = units[name[2:]]
            unit.hop.wait_recv()
            if name[1] in "yh":
                load_received(unit, ry if name[1] == "y" else rz[0])
        else:
            of_sum[name[2:]](sums[name[:2]])


REDUCE_ORDER = [
    0, 5, 6, 8, 11, 1, 4, 2, 17, 9, 19, 7, 43, 13, 44, 45, 16, 20, 3, 18, 14, 46, 10, 21, 47, 48, 12, 22, 23,
    15, 58, 24, 40, 59, 60, 26, 41, 42, 25, 28, 29, 27, 49, 39, 61, 73, 50, 51, 74, 62, 63, 31, 55, 52, 30,
    79, 53, 54, 75, 56, 57, 38, 80, 91, 70, 92, 32, 33, 34, 64, 71, 110, 81, 111, 112, 76, 95, 93, 116, 82,
    94, 117, 65, 118, 96, 83, 107, 77, 97, 98, 66, 67, 72, 108, 36, 85, 164, 131, 86, 109, 84, 68, 165, 69,
    87, 88, 100, 119, 120, 99, 121, 132, 78, 35, 101, 137, 102, 103, 37, 128, 122, 149, 123, 89, 124, 150,
    151, 138, 152, 113, 114, 129, 90, 115, 171, 125, 133, 105, 126, 143, 167, 127, 153, 154, 155, 144, 145,
    134, 156, 139, 157, 158, 159, 104, 160, 140, 161, 141, 142, 130, 172, 135, 136, 162, 163, 173, 174, 146,
    169, 147, 148, 106, 166, 170, 175, 168, 176,
]


def reduce_schedule(count, units, hops):
    names = ["load0", "load1"]
    early = [u for u in units if u[0] in "oa"]
    late = [u for u in units if u[0] in "cq"]

    def start(group):
        for u in group:
            names.extend(["away_" + u, "Sy" + u, "home_" + u])

    def fold(group):
        for u in group:
            names.extend(["Wy" + u, "f1_" + u, "Sh" + u])
        for u in group:
            names.extend(["Wh" + u, "f2_" + u, "Sz" + u])

    def total(k):
        for part in ("31", "Sc1", "30", "Sc0", "Wc1", "Wc0", "01", "Sb", "Sa", "00", "Wb", "own", "Ss", "Ws", "Wa", "out"):
            names.append(part[0] + k + part[1:] if part[0] in "SW" else k + part)

    start(early)
    names.extend("dh%d" % c for c in range(4))
    names.append("w1load")
    total("dn")
    names.extend(["hload", "nload"])
    fold(early)
    start(late)
    total("br")
    fold(late)
    for i in range(hops):
        names.extend(["SG%d" % i, "WG%d" % i, "g%d" % i])
    names.extend("Wz" + u for u in units)
    names.append("end")
    if count == 8 and len(units) == 12 and hops == 5:
        return [names[i] for i in REDUCE_ORDER]
    return names


def reduce_call(dbits, tbits, x, dy, params, back_sum, sums, gathered):
    normed, back_rows, wq, w1, wo, w2, hidden_act, slope, attended, proj_back = gathered
    count = 1 << dbits
    blk = D // count
    rows = x.shape[0]
    tokens = normed.shape[0]
    width, hidden = wo.shape[0], w2.shape[0]
    total = 4 * width + 2 * hidden
    half, quarter = tokens // 2, tokens // 4
    any_spec = pl.BlockSpec(memory_space=pl.ANY)
    vm = pl.BlockSpec(memory_space=pltpu.VMEM)
    shape = lambda s, t=bf16: jax.ShapeDtypeStruct(s, t)
    vmem = lambda s, t=bf16: pltpu.VMEM(s, t)
    prb, size = [], D
    for _ in range(dbits):
        size = size // 2 if size >= 256 else size
        prb.append(vmem((16, size), f32))
    prb += [vmem((16, size), f32)] * tbits
    outs = [
        shape((rows, D)),
        shape((rows, D), f32),
        shape((total, blk), f32),
        shape((total, blk)),
        shape((16, size), f32),
        shape((total, D // 2)),
    ]
    outs += [shape((half, D)), shape((quarter, D)), shape((rows, D))] * 2
    outs += [shape((total, D >> (2 + k))) for k in range(dbits - 2)]
    scratch = [
        vmem((tokens, D)),
        vmem((tokens, hidden)),
        vmem((tokens, hidden)),
        vmem((hidden, D)),
        vmem((width, D)),
        vmem((D, 3 * width)),
        vmem((tokens, width)),
        vmem((tokens, 3 * width)),
        vmem((total - hidden, D // 2)),
        vmem((total, D // 2)),
        vmem((2, width, blk), f32),
        vmem((3, width, D // 2)),
        vmem((quarter, D)),
        vmem((quarter, D)),
        vmem((rows, D)),
        vmem((quarter, D)),
        vmem((quarter, D)),
        vmem((rows, D), f32),
        vmem((16, D), f32),
        vmem((8, hidden), f32),
        pltpu.SemaphoreType.DMA((80,)),
        pltpu.SemaphoreType.DMA((80,)),
        pltpu.SemaphoreType.DMA((160,)),
    ] + prb
    if blk % 128:
        scratch.append(vmem((total, blk)))
    return pl.pallas_call(
        functools.partial(reduce_kernel, (dbits, tbits)),
        out_shape=outs,
        in_specs=[vm] * 5 + [any_spec] * 10,
        out_specs=[any_spec] * 4 + [vm] + [any_spec] * (len(outs) - 5),
        scratch_shapes=scratch,
        compiler_params=pltpu.CompilerParams(
            vmem_limit_bytes=62 * 2**20, collective_id=1, has_side_effects=True
        ),
        cost_estimate=pl.CostEstimate(flops=5 * 10**10, bytes_accessed=10**8, transcendentals=10**6),
        name="reduce",
    )(x, dy, params, back_sum, sums, *gathered)


def adam_matrix(weight, first, second, grad):
    first_new = beta_first * first + (1.0 - beta_first) * grad
    second_new = beta_second * second + (1.0 - beta_second) * grad * grad
    root = jnp.sqrt(second_new * (1.0 / (1.0 - beta_second**STEP))) + adam_eps
    change = (first_new * (matrix_rate / (1.0 - beta_first**STEP))) / root
    return (weight * (1.0 - matrix_rate * weight_decay) - change, first_new, second_new)


def adam_kernel(plans, me_ref, *refs):
    sub = (me_ref[0] >> SUB_BIT) & 1
    step = pl.program_id(0)
    count = len(plans)
    ins, outs = refs[: 5 * count], refs[5 * count :]
    for k, (begin, half, turned) in enumerate(plans):
        w_ref, m_ref, v_ref, own_ref, recv_ref = ins[5 * k : 5 * k + 5]
        wo_ref, mo_ref, vo_ref = outs[3 * k : 3 * k + 3]

        @pl.when((step >= begin) & (step < begin + 2 * half))
        def _():
            mine = ((step - begin) // half) == sub
            grad = jnp.where(mine, own_ref[...], recv_ref[...].astype(f32))
            grad = (grad.T if turned else grad).reshape(w_ref.shape)
            wo_ref[...], mo_ref[...], vo_ref[...] = adam_matrix(w_ref[...], m_ref[...], v_ref[...], grad)


def adam_call(me, matrices, own, recv):
    blk = own.shape[1]
    plans, operands, in_specs, out_specs, out_shape = [], [], [], [], []
    begin = 0
    for weight, first, second, start, rows, turned in matrices:
        shape = weight.shape
        half = shape[0] if len(shape) == 3 else shape[1 if turned else 0] // (2 * rows)

        def at(i, begin=begin, half=half):
            return jnp.clip(i - begin, 0, 2 * half - 1)

        def grad_at(own, base=start // rows, at=at, half=half):
            def index(i, me_ref):
                sub = (me_ref[0] >> SUB_BIT) & 1
                skip = sub * half if own else (1 - sub) * half
                return (base + jnp.clip(at(i) - skip, 0, half - 1), 0)

            return pl.BlockSpec((rows, blk), index)

        if len(shape) == 3:
            full = pl.BlockSpec((1, blk, rows), lambda i, _, at=at, half=half: (at(i) % half, 0, at(i) // half))
        elif turned:
            full = pl.BlockSpec((blk, rows), lambda i, _, at=at: (0, at(i)))
        else:
            full = pl.BlockSpec((rows, blk), lambda i, _, at=at: (at(i), 0))
        plans.append((begin, half, turned))
        operands += [weight, first, second, own, recv]
        in_specs += [full] * 3 + [grad_at(True), grad_at(False)]
        out_specs += [full] * 3
        out_shape += [jax.ShapeDtypeStruct(shape, f32)] * 3
        begin += 2 * half
    return tuple(
        pl.pallas_call(
            functools.partial(adam_kernel, plans),
            grid_spec=pltpu.PrefetchScalarGridSpec(
                num_scalar_prefetch=1, grid=(begin,), in_specs=in_specs, out_specs=out_specs
            ),
            out_shape=out_shape,
            compiler_params=vmem_params(60),
            name="adam",
        )(me, *operands)
    )


def per_device(
    inputs,
    segments,
    cotangent,
    qkv_weight,
    qkv_first,
    qkv_second,
    dense_weight,
    dense_first,
    dense_second,
    expand_weight,
    expand_first,
    expand_second,
    shrink_weight,
    shrink_first,
    shrink_second,
    small_params,
    small_first,
    small_second,
):
    dp = lax.axis_size("dp")
    tensor_count = lax.axis_size("tensor")
    dbits = dp.bit_length() - 1
    tbits = tensor_count.bit_length() - 1
    d_me = lax.axis_index("dp")
    t_me = lax.axis_index("tensor")
    sub = (d_me >> SUB_BIT) & 1
    order = place_order(dp)
    high_bits = list(range(2, dbits))
    gather_bits = high_bits + [ROW_BIT]
    rows = inputs.shape[0]
    me = jnp.stack([d_me, t_me]).astype(jnp.int32)

    small_low = jnp.pad(small_params.astype(bf16), ((0, 16 - small_params.shape[0]), (0, 0)))
    ids = jnp.broadcast_to(segments, (8, rows))
    (
        normed, back_rows, qkv_wide, expand_full, dense_full, shrink_full, hidden_act, gelu_slope, attended, proj_back,
        params, back_sum, sums,
    ) = gather_call(
        dbits, tbits, inputs, cotangent, ids, small_low, qkv_weight, expand_weight, dense_weight, shrink_weight
    )
    width, hidden = dense_full.shape[0], shrink_full.shape[0]
    gathered = (
        normed, back_rows, qkv_wide, expand_full, dense_full, shrink_full, hidden_act, gelu_slope, attended, proj_back,
    )
    output, input_grad, own, recv, small_sum, *_ = reduce_call(
        dbits, tbits, inputs, cotangent, params, back_sum, sums, gathered
    )
    blk = D // dp
    if small_sum.shape[1] > blk:
        small_sum = lax.dynamic_slice_in_dim(small_sum, (d_me % (small_sum.shape[1] // blk)) * blk, blk, 1)
    small_sum = small_sum[: small_params.shape[0]]
    block = hidden
    new = adam_call(
        me,
        [
            (shrink_weight, shrink_first, shrink_second, 0, block, False),
            (expand_weight, expand_first, expand_second, hidden, block, True),
            (qkv_weight, qkv_first, qkv_second, 2 * hidden, width, True),
            (dense_weight, dense_first, dense_second, 2 * hidden + 3 * width, width, False),
        ],
        own,
        recv,
    )
    shrink_new, expand_new, qkv_new, dense_new = new[0:3], new[3:6], new[6:9], new[9:12]
    small_new = adam_update(small_params, small_first, small_second, small_sum, vector_rate, 0.0)
    return (output, input_grad) + qkv_new + dense_new + expand_new + shrink_new + small_new


def solution(mesh):
    token_spec = P(("dp", "tensor"), None)
    qkv_spec = P(None, "dp", "tensor")
    row_spec = P("tensor", "dp")
    column_spec = P("dp", "tensor")
    small_spec = P(None, "dp")
    weight_specs = (qkv_spec,) * 3 + (row_spec,) * 3 + (column_spec,) * 3 + (row_spec,) * 3 + (small_spec,) * 3
    return jax.shard_map(
        per_device,
        mesh=mesh,
        in_specs=(token_spec, P("dp", "tensor"), token_spec) + weight_specs,
        out_specs=(token_spec, token_spec) + weight_specs,
        check_vma=False,
    )
```
